128 devices in a mesh: gz: 8 (over y, z_hi), gy: 4 (over z_lo, core), gx: 4 (over x).
Axes of the slice: x: 4, y: 4, z: 4 (z_hi: 2, z_lo: 2; z = z_hi * 2 + z_lo), core: 2. Of those that a mesh axis runs over, the one named last changes fastest.
Arguments:
- e_start: float32 [3, 64, 128, 512], P(None, 'gz', 'gy', 'gx'), may hold values from -6 to 6
- h_start: float32 [3, 64, 128, 512], P(None, 'gz', 'gy', 'gx'), may hold values from -6 to 6
- adjoint_e: float32 [3, 64, 128, 512], P(None, 'gz', 'gy', 'gx'), may hold values from -6 to 6
- adjoint_h: float32 [3, 64, 128, 512], P(None, 'gz', 'gy', 'gx'), may hold values from -6 to 6
- permittivity: float32 [64, 128, 512], P('gz', 'gy', 'gx'), may hold values from 1 to 4
- current: float32 [64, 128, 512], P('gz', 'gy', 'gx'), may hold values from -6 to 6
- layer_of_cell: int32 [64], P('gz'), may hold values from 0 to 15, as said below
- pml_cells: int32 [3], replicated, may hold values from 4 to 8
- start_step: int32 [1], replicated, may hold values from 0 to 99999
Outputs:
- gradient: float32 [16, 128, 512], P('gz', 'gy', 'gx')
- adjoint_e_out: float32 [3, 64, 128, 512], P(None, 'gz', 'gy', 'gx')
- adjoint_h_out: float32 [3, 64, 128, 512], P(None, 'gz', 'gy', 'gx')
The draws below stay inside these ranges and needn't reach their ends.
Inputs may be any that keep to these rules, and one draw needn't show every extreme that they name: `layer_of_cell`: every aligned block of 16 consecutive z planes holds each layer exactly once.
All inputs are finite; a program needn't handle non-finite values.
Results may differ from the reference program's by a relative error of at most 0.00011.
Values sent between devices are 32-bit elements; how exact they have to be, the bound alone decides.
No kernel may reach another device: no remote copies, remote signals or barrier semaphores. Data moves between devices by JAX's collectives and lax.ppermute only.
A program may use at most 128 MiB of HBM per device.

```python
import math
import jax
import jax.numpy as jnp
from jax import lax

NZ = 64
NY = 128
NX = 512
NL = 16


def draw_layer_of_cell(key, part):
    key = jax.random.fold_in(key, 7)
    blocks = NZ // NL
    block_keys = jax.random.split(key, blocks)
    orders = jax.vmap(lambda block_key: jax.random.permutation(block_key, NL))(block_keys)
    return orders.reshape(NZ).astype(jnp.int32)


def shard_levels(own_key, dims, cuts, low, high):
    def one(position, blocks):
        draws = jax.random.uniform(jax.random.fold_in(jax.random.fold_in(own_key, 6), position), (blocks,), jnp.float32, low / len(cuts), high / len(cuts))
        return jnp.repeat(jnp.exp(draws), dims[position] // blocks).reshape((-1,) + (1,) * (len(dims) - position - 1))

    gain = one(*cuts[0])
    for cut in cuts[1:]:
        gain = gain * one(*cut)
    return gain


def centred(stream_key, shape, scale, bound, shards=(), kind=jnp.bfloat16):
    entries = jax.random.normal(stream_key, shape, jnp.float32) * scale
    if len(shards) > 0:
        entries = shard_levels(stream_key, shape, shards, -0.22, 0.18) * entries
    return jnp.clip(entries, min=-bound, max=bound).astype(kind)


def setup_inputs(seed: int = 0) -> dict:
    streams_of = jax.random.split(jax.random.key(seed), 10)
    return {
        "e_start": centred(streams_of[0], (3, NZ, NY, NX), 1.0, 6.0, ((1, 8), (2, 4), (3, 4)), jnp.float32),
        "h_start": centred(streams_of[1], (3, NZ, NY, NX), 1.0, 6.0, ((1, 8), (2, 4), (3, 4)), jnp.float32),
        "adjoint_e": centred(streams_of[2], (3, NZ, NY, NX), 1.0, 6.0, ((1, 8), (2, 4), (3, 4)), jnp.float32),
        "adjoint_h": centred(streams_of[3], (3, NZ, NY, NX), 1.0, 6.0, ((1, 8), (2, 4), (3, 4)), jnp.float32),
        "permittivity": jnp.clip(1.0 + 3.0 * jax.random.uniform(streams_of[4], (NZ, NY, NX), jnp.float32) ** shard_levels(streams_of[4], (NZ, NY, NX), ((0, 8), (1, 4), (2, 4)), -0.2, 0.2), 1.0, 4.0),
        "current": centred(streams_of[5], (NZ, NY, NX), 1.0, 6.0, ((0, 8), (1, 4), (2, 4)), jnp.float32),
        "layer_of_cell": draw_layer_of_cell(jax.random.fold_in(streams_of[9], 71), 0),
        "pml_cells": jax.random.randint(streams_of[7], (3,), 4, 9).astype(jnp.int32),
        "start_step": jax.random.randint(streams_of[8], (1,), 0, 100000).astype(jnp.int32),
    }


time_step = 0.5
sigma_peak = 0.8
period_steps = 64


def profile(positions, extent, thickness):
    distance = jnp.minimum(positions, extent - 1 - positions)
    depth = jnp.maximum(thickness - distance, 0).astype(jnp.float32) / thickness.astype(jnp.float32)
    return sigma_peak * depth * depth


def magnetic_coeffs(sigma):
    half_loss = sigma * (time_step * 0.5)
    return (1.0 - half_loss) / (1.0 + half_loss), time_step / (1.0 + half_loss)


def electric_coeffs(sigma, permittivity):
    half_loss = sigma * time_step / (2.0 * permittivity)
    return (1.0 - half_loss) / (1.0 + half_loss), time_step / (permittivity * (1.0 + half_loss))


def diff_next(values, along):
    widths = [(0, 0), (0, 0), (0, 0)]
    widths[along] = (0, 1)
    padded = jnp.pad(values, widths)
    return lax.slice_in_dim(padded, 1, values.shape[along] + 1, axis=along) - values


def diff_prev(values, along):
    widths = [(0, 0), (0, 0), (0, 0)]
    widths[along] = (1, 0)
    padded = jnp.pad(values, widths)
    return values - lax.slice_in_dim(padded, 0, values.shape[along], axis=along)


def curl_forward(field):
    return jnp.stack([diff_next(field[2], 1) - diff_next(field[1], 0),
                      diff_next(field[0], 0) - diff_next(field[2], 2),
                      diff_next(field[1], 2) - diff_next(field[0], 1)])


def curl_backward(field):
    return jnp.stack([diff_prev(field[2], 1) - diff_prev(field[1], 0),
                      diff_prev(field[0], 0) - diff_prev(field[2], 2),
                      diff_prev(field[1], 2) - diff_prev(field[0], 1)])


def advance(e_field, h_field, coeffs, drive):
    mag_keep, mag_scale, ele_keep, ele_scale = coeffs
    h_next = mag_keep * h_field - mag_scale * curl_forward(e_field)
    curl_h = curl_backward(h_next)
    if drive is not None:
        curl_h = jnp.stack([curl_h[0], curl_h[1], curl_h[2] - drive])
    e_next = ele_keep * e_field + ele_scale * curl_h
    return e_next, h_next


def inner(first_field, second_field):
    return first_field[0] * second_field[0] + first_field[1] * second_field[1] + first_field[2] * second_field[2]


def reference(e_start, h_start, adjoint_e, adjoint_h, permittivity, current, layer_of_cell, pml_cells, start_step):
    sigma = (profile(jnp.arange(NZ, dtype=jnp.int32), NZ, pml_cells[0])[:, None, None]
             + profile(jnp.arange(NY, dtype=jnp.int32), NY, pml_cells[1])[None, :, None]
             + profile(jnp.arange(NX, dtype=jnp.int32), NX, pml_cells[2])[None, None, :])
    mag_keep, mag_scale = magnetic_coeffs(sigma)
    ele_keep, ele_scale = electric_coeffs(sigma, permittivity)
    coeffs = (mag_keep, mag_scale, ele_keep, ele_scale)
    drives = []
    for offset in (1, 2):
        phase = ((start_step[0] + offset) % period_steps).astype(jnp.float32) * (2.0 * math.pi / period_steps)
        drives.append(current * jnp.sin(phase))
    e_one, h_one = advance(e_start, h_start, coeffs, drives[0])
    e_two, h_two = advance(e_one, h_one, coeffs, drives[1])
    lam_e_one, lam_h_one = advance(adjoint_e, adjoint_h, coeffs, None)
    lam_e_zero, lam_h_zero = advance(lam_e_one, lam_h_one, coeffs, None)
    density = inner(e_start, lam_e_zero) + inner(e_one, lam_e_one) + inner(e_two, adjoint_e)
    onehot = (jnp.arange(NL, dtype=jnp.int32)[:, None] == layer_of_cell[None, :]).astype(jnp.float32)
    gradient = jnp.dot(onehot, density.reshape(NZ, NY * NX), precision=lax.Precision.HIGHEST).reshape(NL, NY, NX)
    return gradient, lam_e_zero, lam_h_zero
```

```python
import functools
import math

import jax
import jax.numpy as jnp
from jax import lax
from jax.experimental import pallas as pl
from jax.experimental.pallas import tpu as pltpu
from jax.sharding import PartitionSpec as P

F32 = jnp.float32
PLANES, ROWS, COLS = 8, 32, 128
DEEP, TALL = PLANES + 4, ROWS + 8
LAYERS = 16
PERIOD = 64
COMPS = 14
BELOW = [(k, 1) for k in range(14)] + [(k, 2) for k in (0, 1, 2, 3, 4, 6, 7, 8, 9, 10)]
ABOVE = [(k, 0) for k in range(13)] + [(k, 1) for k in (0, 1, 6, 7)]
BELOW_TILES, ABOVE_TILES = (len(BELOW) + 1) // 2, (len(ABOVE) + 1) // 2


def lanes(rows=8):
    return lax.broadcasted_iota(jnp.int32, (rows, COLS), 1)


def subs(rows=8):
    return lax.broadcasted_iota(jnp.int32, (rows, COLS), 0)


def turn(value, shift, axis):
    shift = shift % value.shape[axis]
    return value if shift == 0 else pltpu.roll(value, shift, axis)


def slot(k):
    return k // 8, (k % 8) // 4, k % 4


def slot_mask(k, rows):
    _, half, pair = slot(k)
    lane = lanes(rows)
    inside = ((lane - 16 - 64 * half) & 127) < 64
    return inside & (((lane & 7) >> 1) == pair)


def window(p, rows):
    lane = lanes(rows)
    return (lane >= 8 * (p + 2)) & (lane < 8 * (p + 2) + 4)


def parity(axis):
    return lax.rem(lax.axis_index(axis), 2) == 0


def strip(planes, rows):
    out = jnp.zeros((rows, COLS), F32)
    for p, plane in enumerate(planes):
        out = jnp.where(window(p, rows), turn(plane, 8 * (p + 2) + 2, 1), out)
    return out


def face_pack(strips, rows):
    right = [jnp.zeros((rows, COLS), F32) for _ in range(2)]
    left = [jnp.zeros((rows, COLS), F32) for _ in range(2)]
    for k, value in enumerate(strips):
        array, half, pair = slot(k)
        mask = slot_mask(k, rows)
        right[array] = jnp.where(mask, turn(value, 2 * pair + 64 * half, 1), right[array])
        left[array] = jnp.where(mask, turn(value, 2 * pair - 2 + 64 * half, 1), left[array])
    return right, left


def first_kernel(e, h, ae, ah, eps, cur, zu, zd, ya, yb, strips, right_out, left_out):
    def plane(k, p):
        if k < 12:
            return (e, h, ae, ah)[k // 3][k % 3, p]
        return (eps, cur)[k - 12][p]

    even = parity("gy")
    sub = subs()
    for k in range(COMPS):
        for half in range(2):
            up = jnp.zeros((8, COLS), F32)
            down = jnp.zeros((8, COLS), F32)
            for j in range(4):
                block = plane(k, 4 * half + j)
                mask = (sub >> 1) == j
                up = jnp.where(mask, turn(block[24:32], 2 * j - 6, 0), up)
                down = jnp.where(mask, turn(block[0:8], 2 * j, 0), down)
            at = 8 * (2 * k + half)
            ya[at : at + 8] = jnp.where(even, up, down)
            yb[at : at + 8] = jnp.where(even, down, up)
    for i, (k, below) in enumerate(BELOW):
        zu[i] = plane(k, PLANES - below)
    for i, (k, above) in enumerate(ABOVE):
        zd[i] = plane(k, above)
    values = []
    for k in range(COMPS):
        value = strip([plane(k, p) for p in range(PLANES)], ROWS)
        strips[k] = value
        values.append(value)
    right, left = face_pack(values, ROWS)
    for a in range(2):
        right_out[a] = right[a]
        left_out[a] = left[a]


def second_kernel(ya, yb, right_in, left_in, tiles, strips, xa, xb):
    index = lax.axis_index("gy")
    even = parity("gy")
    has_after = (index < lax.axis_size("gy") - 1).astype(F32)
    has_before = (index > 0).astype(F32)
    sub = subs()
    values = []
    for k in range(COMPS):
        planes = []
        for half in range(2):
            at = 8 * (2 * k + half)
            got_a, got_b = ya[at : at + 8], yb[at : at + 8]
            after = jnp.where(even, got_a, got_b) * has_after
            before = jnp.where(even, got_b, got_a) * has_before
            for j in range(4):
                tile = jnp.where(sub < 2, turn(after, -2 * j, 0), jnp.where(sub >= 6, turn(before, 6 - 2 * j, 0), 0.0))
                tiles[k, 4 * half + j] = tile
                planes.append(tile)
        value = strip(planes, 8)
        strips[k] = value
        values.append(value)
    right, left = face_pack(values, 8)
    even = parity("gx")
    for a in range(2):
        xa[a, 0:ROWS] = jnp.where(even, right_in[a], left_in[a])
        xb[a, 0:ROWS] = jnp.where(even, left_in[a], right_in[a])
        xa[a, ROWS:TALL] = jnp.where(even, right[a], left[a])
        xb[a, ROWS:TALL] = jnp.where(even, left[a], right[a])


def rim_pack(out, items, plane_of, tiles, side, first_lane):
    sub = subs()
    kept = (sub < 2) | (sub >= 6)
    count = (len(items) + 1) // 2
    for i in range(count):
        k, at = items[2 * i]
        tile = tiles[k, plane_of(at)]
        if 2 * i + 1 < len(items):
            k, at = items[2 * i + 1]
            tile = jnp.where(kept, tile, turn(tiles[k, plane_of(at)], 4, 0))
        out[8 * i : 8 * i + 8] = tile
    lane = lanes(TALL)
    for a in range(2):
        packed = jnp.zeros((TALL, COLS), F32)
        for k in range(8 * a, min(8 * a + 8, COMPS)):
            packed = jnp.where((lane >> 4) == k % 8, turn(side[k], 16 * (k % 8) - first_lane, 1), packed)
        at = 8 * count + TALL * a
        out[at : at + TALL] = packed


def third_kernel(xa, xb, strips, strips_rim, tiles, sides, rim_up, rim_down):
    index = lax.axis_index("gx")
    even = parity("gx")
    has_after = (index < lax.axis_size("gx") - 1).astype(F32)
    has_before = (index > 0).astype(F32)
    lane = lanes(TALL)
    pair_of = (lane & 7) >> 1
    own = (lane >= 16) & (lane < 80)
    after = [jnp.where(even, xa[a], xb[a]) * has_after for a in range(2)]
    before = [jnp.where(even, xb[a], xa[a]) * has_before for a in range(2)]
    side = []
    for k in range(COMPS):
        array, half, pair = slot(k)
        mine = jnp.concatenate([strips[k], strips_rim[k]], axis=0)
        value = jnp.where(pair_of == 0, mine, turn(mine, 4, 1))
        value = jnp.where(pair_of == 1, turn(after[array], 2 - 2 * pair - 64 * half, 1), value)
        value = jnp.where(pair_of == 2, turn(before[array], 4 - 2 * pair - 64 * half, 1), value)
        value = jnp.where(own, value, 0.0)
        sides[k] = value
        side.append(value)
    rim_pack(rim_up, BELOW, lambda below: PLANES - below, tiles, side, 64)
    rim_pack(rim_down, ABOVE, lambda above: above, tiles, side, 16)


def profile(position, extent, thickness):
    distance = jnp.minimum(position, extent - 1 - position)
    depth = jnp.maximum(thickness - distance, 0).astype(F32) / thickness.astype(F32)
    return 0.8 * depth * depth


def magnetic(ex, ey, ez, ex_up, ey_up, hx, hy, hz, r, next_x, next_y, at=(0, 1, 2)):
    cx = (next_y(ez, 2) - ez) - (ey_up - ey)
    cy = (ex_up - ex) - (next_x(ez, 2) - ez)
    cz = (next_x(ey, 1) - ey) - (next_y(ex, 0) - ex)
    return [r * (h + h - 0.5 * c) - h for h, c in ((hx, cx), (hy, cy), (hz, cz))]


def electric(hx, hy, hz, hx_down, hy_down, ex, ey, ez, q, g, drive, prev_x, prev_y):
    cx = (hz - prev_y(hz, 2)) - (hy - hy_down)
    cy = (hx - hx_down) - (hz - prev_x(hz, 2))
    cz = (hy - prev_x(hy, 1)) - (hx - prev_y(hx, 0))
    if drive is not None:
        cz = cz - drive
    return [q * (g * e + c) for e, c in ((ex, cx), (ey, cy), (ez, cz))]


def main_kernel(
    layer, pml, start, e, h, ae, ah, eps, cur, zu, zd, tiles, sides, rim_up, rim_down,
    sums, e_out, h_out,
    f, one, rr, qq, gg, xf, xone, xr, xq, xg,
):
    iz, iy, ix = (lax.axis_index(a) for a in ("gz", "gy", "gx"))
    nz, ny, nx = (PLANES * lax.axis_size("gz"), ROWS * lax.axis_size("gy"), COLS * lax.axis_size("gx"))
    has_above = (iz < lax.axis_size("gz") - 1).astype(F32)
    has_below = (iz > 0).astype(F32)
    for k in range(COMPS):
        for p in range(PLANES):
            if k < 12:
                f[k, p + 2, 0:ROWS] = (e, h, ae, ah)[k // 3][k % 3, p]
            else:
                f[k, p + 2, 0:ROWS] = (eps, cur)[k - 12][p]
            f[k, p + 2, ROWS:TALL] = tiles[k, p]
    sent = set()
    for items, faces, rim, place, keep in (
        (BELOW, zu, rim_up, lambda below: 2 - below, has_below),
        (ABOVE, zd, rim_down, lambda above: PLANES + 2 + above, has_above),
    ):
        for i, (k, at) in enumerate(items):
            idx = place(at)
            sent.add((k, idx))
            tile = rim[8 * (i // 2) : 8 * (i // 2) + 8]
            f[k, idx, 0:ROWS] = faces[i] * keep
            f[k, idx, ROWS:TALL] = turn(tile, 4 * (i % 2), 0) * keep
    for k in range(COMPS):
        for idx in (0, 1, PLANES + 2, PLANES + 3):
            if (k, idx) not in sent:
                f[k, idx] = jnp.zeros((TALL, COLS), F32)
    lane = lanes(TALL)
    row = subs(TALL)
    for k in range(COMPS):
        at = 8 * BELOW_TILES + TALL * (k // 8)
        low = turn(rim_up[at : at + TALL], -16 * (k % 8), 1) * has_below
        at = 8 * ABOVE_TILES + TALL * (k // 8)
        high = turn(rim_down[at : at + TALL], 80 - 16 * (k % 8), 1) * has_above
        value = jnp.where(lane < 16, low, sides[k])
        xf[k] = jnp.where((lane >= 80) & (lane < 96), high, value)
    y_at = ROWS * iy + jnp.where(row >= 36, row - TALL, row)
    x_at = COLS * ix + lane
    y_in = (y_at >= 0) & (y_at < ny)
    profile_y = profile(y_at, ny, pml[1])
    profile_yx = profile_y + profile(x_at, nx, pml[2])

    def coefficients(sigma, inside, permittivity):
        permittivity = jnp.maximum(permittivity, 1.0)
        r = jnp.where(inside, 1.0 / (1.0 + 0.25 * sigma), 0.0)
        q = jnp.where(inside, 1.0 / (2.0 * permittivity + 0.5 * sigma), 0.0)
        return r, q, 2.0 * permittivity - 0.5 * sigma

    def plane_coefficients(idx, carry):
        z_at = jnp.full((TALL, COLS), PLANES * iz + idx - 2, jnp.int32)
        inside = y_in & (z_at >= 0) & (z_at < nz)
        sigma = profile(z_at[0:8], nz, pml[0])
        sigma = jnp.concatenate([sigma] * (TALL // 8), axis=0) + profile_yx
        rr[idx], qq[idx], gg[idx] = coefficients(sigma, inside, f[12, idx])
        return carry

    lax.fori_loop(0, DEEP, plane_coefficients, 0)
    column = lane & 7
    x_at = COLS * ix + jnp.where(column < 4, COLS - 2 + column, column - 6)
    z_at = PLANES * iz + (lane >> 3) - 2
    inside = y_in & (z_at >= 0) & (z_at < nz) & (x_at >= 0) & (x_at < nx)
    sigma = profile(z_at, nz, pml[0]) + profile_y + profile(x_at, nx, pml[2])
    xr[...], xq[...], xg[...] = coefficients(sigma, inside, xf[12])
    factors = []
    for k in (1, 2):
        phase = jnp.full((8, COLS), lax.rem(start[0] + k, PERIOD), jnp.int32).astype(F32)
        factor = jnp.sin(phase * (2.0 * math.pi / PERIOD))
        factors.append(jnp.concatenate([factor] * (TALL // 8), axis=0))
    first_lane, last_lane = lane == 0, lane == COLS - 1

    def up_row(value, _):
        return pltpu.roll(value, TALL - 1, 0)

    def down_row(value, _):
        return pltpu.roll(value, 1, 0)

    def side_magnetic(e_ref, e_base, h_base):
        got = [e_ref[e_base + c] for c in range(3)]
        new = magnetic(
            *got, pltpu.roll(got[0], 120, 1), pltpu.roll(got[1], 120, 1), *[xf[h_base + c] for c in range(3)], xr[...],
            lambda v, _: pltpu.roll(v, 127, 1), up_row,
        )
        for c in range(3):
            xf[h_base + c] = new[c]

    def side_electric(e_base, h_base, out_base, factor):
        got = [xf[h_base + c] for c in range(3)]
        drive = None if factor is None else xf[13] * factor
        new = electric(
            *got, pltpu.roll(got[0], 8, 1), pltpu.roll(got[1], 8, 1), *[xf[e_base + c] for c in range(3)], xq[...], xg[...], drive,
            lambda v, _: pltpu.roll(v, 1, 1), down_row,
        )
        for c in range(3):
            xone[out_base + c] = new[c]

    def plane_magnetic(idx, e_ref, x_ref, e_base, h_base):
        def next_x(value, c):
            halo = pltpu.roll(x_ref[e_base + c], 125 - 8 * idx, 1)
            return jnp.where(last_lane, halo, pltpu.roll(value, COLS - 1, 1))

        new = magnetic(
            *[e_ref[e_base + c, idx] for c in range(3)], e_ref[e_base, idx + 1], e_ref[e_base + 1, idx + 1],
            *[f[h_base + c, idx] for c in range(3)], rr[idx], next_x, up_row,
        )
        for c in range(3):
            f[h_base + c, idx] = new[c]

    def plane_electric(idx, e_ref, e_base, h_base, factor):
        def prev_x(value, c):
            halo = pltpu.roll(xf[h_base + c], 123 - 8 * idx, 1)
            return jnp.where(first_lane, halo, pltpu.roll(value, 1, 1))

        drive = None if factor is None else f[13, idx] * factor
        return electric(
            *[f[h_base + c, idx] for c in range(3)], f[h_base, idx - 1], f[h_base + 1, idx - 1],
            *[e_ref[e_base + c, idx] for c in range(3)], qq[idx], gg[idx], drive, prev_x, down_row,
        )

    def body(idx, carry):
        plane_magnetic(idx, f, xf, 0, 3)
        plane_magnetic(idx, f, xf, 6, 9)
        return carry

    lax.fori_loop(0, PLANES + 3, body, 0)
    side_magnetic(xf, 0, 3)
    side_magnetic(xf, 6, 9)

    def body(idx, carry):
        for base, out, factor in ((0, 0, factors[0]), (6, 3, None)):
            new = plane_electric(idx, f, base, base + 3, factor)
            for c in range(3):
                one[out + c, idx] = new[c]
        return carry

    lax.fori_loop(1, PLANES + 3, body, 0)
    side_electric(0, 3, 0, factors[0])
    side_electric(6, 9, 3, None)

    def body(idx, carry):
        plane_magnetic(idx, one, xone, 0, 3)
        plane_magnetic(idx, one, xone, 3, 9)
        return carry

    lax.fori_loop(1, PLANES + 2, body, 0)
    side_magnetic(xone, 0, 3)
    side_magnetic(xone, 3, 9)
    sums[...] = jnp.zeros((LAYERS, ROWS, COLS), F32)

    def body(p, carry):
        idx = p + 2
        two = plane_electric(idx, one, 0, 3, factors[1])
        zero = plane_electric(idx, one, 3, 9, None)
        density = jnp.zeros((ROWS, COLS), F32)
        for c in range(3):
            last = zero[c][0:ROWS]
            e_out[c, p] = last
            h_out[c, p] = f[9 + c, idx, 0:ROWS]
            density = density + f[c, idx, 0:ROWS] * last + one[c, idx, 0:ROWS] * one[3 + c, idx, 0:ROWS]
            density = density + two[c][0:ROWS] * f[6 + c, idx, 0:ROWS]
        sums[layer[p]] = density
        return carry

    lax.fori_loop(0, PLANES, body, 0)


def sum_kernel(got, out):
    total = got[0]
    for i in range(1, got.shape[0]):
        total = total + got[i]
    out[...] = total


def call(kernel, outs, scratch=(), scalars=0, flops=1000000):
    def run(*args):
        specs = [pl.BlockSpec(memory_space=pltpu.SMEM)] * scalars
        specs += [pl.BlockSpec(memory_space=pltpu.VMEM)] * (len(args) - scalars)
        size = sum(4 * math.prod(s) for s in outs) + sum(4 * math.prod(a.shape) for a in args)
        return pl.pallas_call(
            kernel,
            out_shape=[jax.ShapeDtypeStruct(s, F32) for s in outs],
            in_specs=specs,
            out_specs=[pl.BlockSpec(memory_space=pltpu.VMEM)] * len(outs),
            scratch_shapes=[pltpu.VMEM(s, F32) for s in scratch],
            compiler_params=pltpu.CompilerParams(vmem_limit_bytes=24 * 2**20),
            cost_estimate=pl.CostEstimate(flops=flops, bytes_accessed=size, transcendentals=0),
        )(*args)

    return run


def ring(axis, step):
    count = lax.axis_size(axis)
    return [(i, (i + step) % count) for i in range(count)]


def swaps(axis, first):
    count = lax.axis_size(axis)
    pairs = [(i % count, (i + 1) % count) for i in range(first, count, 2)]
    return pairs + [(b, a) for a, b in pairs]


def local(e_start, h_start, adjoint_e, adjoint_h, permittivity, current, layer_of_cell, pml_cells, start_step):
    raw = (e_start, h_start, adjoint_e, adjoint_h, permittivity, current)
    block = (ROWS, COLS)
    zu, zd, ya, yb, strips, right, left = call(
        first_kernel,
        [(len(BELOW),) + block, (len(ABOVE),) + block, (16 * COMPS, COLS), (16 * COMPS, COLS), (COMPS,) + block, (2,) + block, (2,) + block],
    )(*raw)
    ya = lax.ppermute(ya, "gy", swaps("gy", 0))
    yb = lax.ppermute(yb, "gy", swaps("gy", 1))
    zu = lax.ppermute(zu, "gz", ring("gz", 1))
    zd = lax.ppermute(zd, "gz", ring("gz", -1))
    tiles, strips_rim, xa, xb = call(
        second_kernel, [(COMPS, PLANES, 8, COLS), (COMPS, 8, COLS), (2, TALL, COLS), (2, TALL, COLS)]
    )(ya, yb, right, left)
    xa = lax.ppermute(xa, "gx", swaps("gx", 0))
    xb = lax.ppermute(xb, "gx", swaps("gx", 1))
    sides, rim_up, rim_down = call(
        third_kernel,
        [(COMPS, TALL, COLS), (8 * BELOW_TILES + 2 * TALL, COLS), (8 * ABOVE_TILES + 2 * TALL, COLS)],
    )(xa, xb, strips, strips_rim, tiles)
    rim_up = lax.ppermute(rim_up, "gz", ring("gz", 1))
    rim_down = lax.ppermute(rim_down, "gz", ring("gz", -1))
    deep, tall = (DEEP, TALL, COLS), (TALL, COLS)
    sums, e_out, h_out = call(
        main_kernel,
        [(LAYERS,) + block, (3, PLANES) + block, (3, PLANES) + block],
        [(COMPS,) + deep, (6,) + deep, deep, deep, deep, (COMPS,) + tall, (6,) + tall, tall, tall, tall],
        scalars=3,
    )(layer_of_cell, pml_cells, start_step, *raw, zu, zd, tiles, sides, rim_up, rim_down)
    count = lax.axis_size("gz")
    got = lax.all_to_all(sums, "gz", 0, 0, tiled=True)
    (gradient,) = call(sum_kernel, [(LAYERS // count,) + block])(got.reshape((count, LAYERS // count) + block))
    return gradient, e_out, h_out


def solution(mesh):
    fields = P(None, "gz", "gy", "gx")
    cells = P("gz", "gy", "gx")
    return jax.shard_map(
        local,
        mesh=mesh,
        in_specs=(fields, fields, fields, fields, cells, cells, P("gz"), P(), P()),
        out_specs=(cells, fields, fields),
        check_vma=False,
    )
```

```python
import functools
import math

import jax
import jax.numpy as jnp
from jax import lax
from jax.experimental import pallas as pl
from jax.experimental.pallas import tpu as pltpu
from jax.sharding import PartitionSpec as P

F32 = jnp.float32
PLANES, ROWS, COLS = 8, 32, 128
DEEP, TALL = PLANES + 4, ROWS + 8
LAYERS = 16
PERIOD = 64
COMPS = 14
BELOW = [(k, 1) for k in range(14)] + [(k, 2) for k in (0, 1, 2, 3, 4, 6, 7, 8, 9, 10)]
ABOVE = [(k, 0) for k in range(13)] + [(k, 1) for k in (0, 1, 6, 7)]
BELOW_ROWS = [(k, 1) for k in range(14)] + [(2, 2), (8, 2)]
BELOW_LAST = [(2, 1), (8, 1)]
ABOVE_ROWS = [(k, 0) for k in range(13)] + [(1, 1), (7, 1)]
ABOVE_LAST = [(1, 0), (7, 0)]
BELOW_SIDE = [(k, 1) for k in range(14)] + [(2, 2), (8, 2)]
ABOVE_SIDE = [(k, 0) for k in range(13)] + [(0, 1), (6, 1)]


def tiles_of(rows, last):
    return (len(rows) + 3) // 4 + (len(last) + 3) // 4


BELOW_TILES, ABOVE_TILES = tiles_of(BELOW_ROWS, BELOW_LAST), tiles_of(ABOVE_ROWS, ABOVE_LAST)


def lanes(rows=8):
    return lax.broadcasted_iota(jnp.int32, (rows, COLS), 1)


def subs(rows=8):
    return lax.broadcasted_iota(jnp.int32, (rows, COLS), 0)


def turn(value, shift, axis):
    shift = shift % value.shape[axis]
    return value if shift == 0 else pltpu.roll(value, shift, axis)


def slot(k):
    return k // 8, (k % 8) // 4, k % 4


def slot_mask(k, rows):
    _, half, pair = slot(k)
    lane = lanes(rows)
    inside = ((lane - 16 - 64 * half) & 127) < 64
    return inside & (((lane & 7) >> 1) == pair)


def window(p, rows):
    lane = lanes(rows)
    return (lane >= 8 * (p + 2)) & (lane < 8 * (p + 2) + 4)


def parity(axis):
    return lax.rem(lax.axis_index(axis), 2) == 0


def strip(planes, rows):
    out = jnp.zeros((rows, COLS), F32)
    for p, plane in enumerate(planes):
        out = jnp.where(window(p, rows), turn(plane, 8 * (p + 2) + 2, 1), out)
    return out


def face_pack(strips, rows):
    right = [jnp.zeros((rows, COLS), F32) for _ in range(2)]
    left = [jnp.zeros((rows, COLS), F32) for _ in range(2)]
    for k, value in enumerate(strips):
        array, half, pair = slot(k)
        mask = slot_mask(k, rows)
        right[array] = jnp.where(mask, turn(value, 2 * pair + 64 * half, 1), right[array])
        left[array] = jnp.where(mask, turn(value, 2 * pair - 2 + 64 * half, 1), left[array])
    return right, left


def first_kernel(e, h, ae, ah, eps, cur, f, ya, yb, sems):
    copies = []
    for k in range(COMPS):
        source = (e, h, ae, ah)[k // 3].at[k % 3] if k < 12 else (eps, cur)[k - 12]
        copies.append(pltpu.make_async_copy(source, f.at[k, 2 : PLANES + 2, 0:ROWS], sems.at[k]))
    for copy in copies:
        copy.start()
    even = parity("gy")
    sub = subs()
    for k in range(COMPS):
        copies[k].wait()
        for half in range(2):
            up = jnp.zeros((8, COLS), F32)
            down = jnp.zeros((8, COLS), F32)
            for j in range(4):
                idx = 4 * half + j + 2
                mask = (sub >> 1) == j
                up = jnp.where(mask, turn(f[k, idx, 24:32], 2 * j - 6, 0), up)
                down = jnp.where(mask, turn(f[k, idx, 0:8], 2 * j, 0), down)
            at = 8 * (2 * k + half)
            ya[at : at + 8] = jnp.where(even, up, down)
            yb[at : at + 8] = jnp.where(even, down, up)


def face_kernel(f, after_a, after_b, zu, zd):
    del after_a, after_b
    for i, (k, below) in enumerate(BELOW):
        zu[i] = f[k, PLANES + 2 - below, 0:ROWS]
    for i, (k, above) in enumerate(ABOVE):
        zd[i] = f[k, above + 2, 0:ROWS]


def strip_kernel(f, strips, right_out, left_out):
    values = []
    for k in range(COMPS):
        value = strip([f[k, p + 2, 0:ROWS] for p in range(PLANES)], ROWS)
        strips[k] = value
        values.append(value)
    right, left = face_pack(values, ROWS)
    for a in range(2):
        right_out[a] = right[a]
        left_out[a] = left[a]


def second_kernel(ya, yb, right_in, left_in, tiles, strips, xa, xb):
    index = lax.axis_index("gy")
    even = parity("gy")
    has_after = (index < lax.axis_size("gy") - 1).astype(F32)
    has_before = (index > 0).astype(F32)
    sub = subs()
    values = []
    for k in range(COMPS):
        planes = []
        for half in range(2):
            at = 8 * (2 * k + half)
            got_a, got_b = ya[at : at + 8], yb[at : at + 8]
            after = jnp.where(even, got_a, got_b) * has_after
            before = jnp.where(even, got_b, got_a) * has_before
            for j in range(4):
                tile = jnp.where(sub < 2, turn(after, -2 * j, 0), jnp.where(sub >= 6, turn(before, 6 - 2 * j, 0), 0.0))
                tiles[k, 4 * half + j] = tile
                planes.append(tile)
        value = strip(planes, 8)
        strips[k] = value
        values.append(value)
    right, left = face_pack(values, 8)
    even = parity("gx")
    for a in range(2):
        xa[a, 0:ROWS] = jnp.where(even, right_in[a], left_in[a])
        xb[a, 0:ROWS] = jnp.where(even, left_in[a], right_in[a])
        xa[a, ROWS:TALL] = jnp.where(even, right[a], left[a])
        xb[a, ROWS:TALL] = jnp.where(even, left[a], right[a])


def rim_pack(out, rows, last, sides, plane_of, extra, tiles, side):
    sub = subs()
    count = 0
    for items, first in ((rows, 1), (last, extra)):
        for i in range(0, len(items), 4):
            tile = jnp.zeros((8, COLS), F32)
            for j, (k, at) in enumerate(items[i : i + 4]):
                tile = jnp.where((sub >> 1) == j, turn(tiles[k, plane_of(at)], 2 * j + first, 0), tile)
            out[8 * count : 8 * count + 8] = tile
            count += 1
    lane = lanes(TALL)
    packed = jnp.zeros((TALL, COLS), F32)
    for i, (k, at) in enumerate(sides):
        packed = jnp.where((lane >> 3) == i, turn(side[k], 8 * i - 8 * (plane_of(at) + 2), 1), packed)
    out[8 * count : 8 * count + TALL] = packed


def rim_rows(rim, rows, last, extra):
    got = {}
    for i, item in enumerate(rows):
        at = 8 * (i // 4)
        got[item] = turn(rim[at : at + 8], -(2 * (i % 4) + 1), 0)
    for i, item in enumerate(last):
        at = 8 * ((len(rows) + 3) // 4 + i // 4)
        tile = turn(rim[at : at + 8], -(2 * (i % 4) + extra), 0)
        got[item] = jnp.where(subs() == (1 if extra == 0 else 6), tile, got[item])
    return got


def third_kernel(xa, xb, strips, strips_rim, tiles, sides, rim_up, rim_down):
    index = lax.axis_index("gx")
    even = parity("gx")
    has_after = (index < lax.axis_size("gx") - 1).astype(F32)
    has_before = (index > 0).astype(F32)
    lane = lanes(TALL)
    pair_of = (lane & 7) >> 1
    own = (lane >= 16) & (lane < 80)
    after = [jnp.where(even, xa[a], xb[a]) * has_after for a in range(2)]
    before = [jnp.where(even, xb[a], xa[a]) * has_before for a in range(2)]
    side = []
    for k in range(COMPS):
        array, half, pair = slot(k)
        mine = jnp.concatenate([strips[k], strips_rim[k]], axis=0)
        value = jnp.where(pair_of == 0, mine, turn(mine, 4, 1))
        value = jnp.where(pair_of == 1, turn(after[array], 2 - 2 * pair - 64 * half, 1), value)
        value = jnp.where(pair_of == 2, turn(before[array], 4 - 2 * pair - 64 * half, 1), value)
        value = jnp.where(own, value, 0.0)
        sides[k] = value
        side.append(value)
    rim_pack(rim_up, BELOW_ROWS, BELOW_LAST, BELOW_SIDE, lambda below: PLANES - below, 0, tiles, side)
    rim_pack(rim_down, ABOVE_ROWS, ABOVE_LAST, ABOVE_SIDE, lambda above: above, 2, tiles, side)


def profile(position, extent, thickness):
    distance = jnp.minimum(position, extent - 1 - position)
    depth = jnp.maximum(thickness - distance, 0).astype(F32) / thickness.astype(F32)
    return 0.8 * depth * depth


def magnetic(ex, ey, ez, ex_up, ey_up, hx, hy, hz, r, next_x, next_y, at=(0, 1, 2)):
    cx = (next_y(ez, 2) - ez) - (ey_up - ey)
    cy = (ex_up - ex) - (next_x(ez, 2) - ez)
    cz = (next_x(ey, 1) - ey) - (next_y(ex, 0) - ex)
    return [r * (h + h - 0.5 * c) - h for h, c in ((hx, cx), (hy, cy), (hz, cz))]


def electric(hx, hy, hz, hx_down, hy_down, ex, ey, ez, q, g, drive, prev_x, prev_y):
    cx = (hz - prev_y(hz, 2)) - (hy - hy_down)
    cy = (hx - hx_down) - (hz - prev_x(hz, 2))
    cz = (hy - prev_x(hy, 1)) - (hx - prev_y(hx, 0))
    if drive is not None:
        cz = cz - drive
    return [q * (g * e + c) for e, c in ((ex, cx), (ey, cy), (ez, cz))]


def main_kernel(
    layer, pml, start, own, zu, zd, tiles, sides, rim_up, rim_down,
    f, sums, e_out, h_out,
    one, rr, qq, gg, xf, xone, xr, xq, xg,
):
    iz, iy, ix = (lax.axis_index(a) for a in ("gz", "gy", "gx"))
    nz, ny, nx = (PLANES * lax.axis_size("gz"), ROWS * lax.axis_size("gy"), COLS * lax.axis_size("gx"))
    has_above = (iz < lax.axis_size("gz") - 1).astype(F32)
    has_below = (iz > 0).astype(F32)
    del own
    for k in range(COMPS):
        for p in range(PLANES):
            f[k, p + 2, ROWS:TALL] = tiles[k, p]
    sent = set()
    lane = lanes(TALL)
    row = subs(TALL)
    for k in range(COMPS):
        xf[k] = sides[k]
    for items, faces, rim, lists, place, extra, keep in (
        (BELOW, zu, rim_up, (BELOW_ROWS, BELOW_LAST, BELOW_SIDE), lambda below: 2 - below, 0, has_below),
        (ABOVE, zd, rim_down, (ABOVE_ROWS, ABOVE_LAST, ABOVE_SIDE), lambda above: PLANES + 2 + above, 2, has_above),
    ):
        rows, last, side = lists
        edge = rim_rows(rim, rows, last, extra)
        for i, (k, at) in enumerate(items):
            idx = place(at)
            sent.add((k, idx))
            f[k, idx, 0:ROWS] = faces[i] * keep
            f[k, idx, ROWS:TALL] = edge[k, at] * keep if (k, at) in edge else jnp.zeros((8, COLS), F32)
        at = 8 * tiles_of(rows, last)
        packed = rim[at : at + TALL] * keep
        for i, (k, at) in enumerate(side):
            idx = place(at)
            xf[k] = jnp.where((lane >> 3) == idx, turn(packed, 8 * idx - 8 * i, 1), xf[k])
    for k in range(COMPS):
        for idx in (0, 1, PLANES + 2, PLANES + 3):
            if (k, idx) not in sent:
                f[k, idx] = jnp.zeros((TALL, COLS), F32)
    y_at = ROWS * iy + jnp.where(row >= 36, row - TALL, row)
    x_at = COLS * ix + lane
    y_in = (y_at >= 0) & (y_at < ny)
    profile_y = profile(y_at, ny, pml[1])
    profile_yx = profile_y + profile(x_at, nx, pml[2])

    def coefficients(sigma, inside, permittivity):
        permittivity = jnp.maximum(permittivity, 1.0)
        r = jnp.where(inside, 1.0 / (1.0 + 0.25 * sigma), 0.0)
        q = jnp.where(inside, 1.0 / (2.0 * permittivity + 0.5 * sigma), 0.0)
        return r, q, 2.0 * permittivity - 0.5 * sigma

    def plane_coefficients(idx, carry):
        z_at = jnp.full((TALL, COLS), PLANES * iz + idx - 2, jnp.int32)
        inside = y_in & (z_at >= 0) & (z_at < nz)
        sigma = profile(z_at[0:8], nz, pml[0])
        sigma = jnp.concatenate([sigma] * (TALL // 8), axis=0) + profile_yx
        rr[idx], qq[idx], gg[idx] = coefficients(sigma, inside, f[12, idx])
        return carry

    lax.fori_loop(0, DEEP, plane_coefficients, 0)
    column = lane & 7
    x_at = COLS * ix + jnp.where(column < 4, COLS - 2 + column, column - 6)
    z_at = PLANES * iz + (lane >> 3) - 2
    inside = y_in & (z_at >= 0) & (z_at < nz) & (x_at >= 0) & (x_at < nx)
    sigma = profile(z_at, nz, pml[0]) + profile_y + profile(x_at, nx, pml[2])
    xr[...], xq[...], xg[...] = coefficients(sigma, inside, xf[12])
    factors = []
    for k in (1, 2):
        phase = jnp.full((8, COLS), lax.rem(start[0] + k, PERIOD), jnp.int32).astype(F32)
        factor = jnp.sin(phase * (2.0 * math.pi / PERIOD))
        factors.append(jnp.concatenate([factor] * (TALL // 8), axis=0))
    first_lane, last_lane = lane == 0, lane == COLS - 1

    def up_row(value, _):
        return pltpu.roll(value, TALL - 1, 0)

    def down_row(value, _):
        return pltpu.roll(value, 1, 0)

    def side_magnetic(e_ref, e_base, h_base):
        got = [e_ref[e_base + c] for c in range(3)]
        new = magnetic(
            *got, pltpu.roll(got[0], 120, 1), pltpu.roll(got[1], 120, 1), *[xf[h_base + c] for c in range(3)], xr[...],
            lambda v, _: pltpu.roll(v, 127, 1), up_row,
        )
        for c in range(3):
            xf[h_base + c] = new[c]

    def side_electric(e_base, h_base, out_base, factor):
        got = [xf[h_base + c] for c in range(3)]
        drive = None if factor is None else xf[13] * factor
        new = electric(
            *got, pltpu.roll(got[0], 8, 1), pltpu.roll(got[1], 8, 1), *[xf[e_base + c] for c in range(3)], xq[...], xg[...], drive,
            lambda v, _: pltpu.roll(v, 1, 1), down_row,
        )
        for c in range(3):
            xone[out_base + c] = new[c]

    def plane_magnetic(idx, e_ref, x_ref, e_base, h_base):
        def next_x(value, c):
            halo = pltpu.roll(x_ref[e_base + c], 125 - 8 * idx, 1)
            return jnp.where(last_lane, halo, pltpu.roll(value, COLS - 1, 1))

        new = magnetic(
            *[e_ref[e_base + c, idx] for c in range(3)], e_ref[e_base, idx + 1], e_ref[e_base + 1, idx + 1],
            *[f[h_base + c, idx] for c in range(3)], rr[idx], next_x, up_row,
        )
        for c in range(3):
            f[h_base + c, idx] = new[c]

    def plane_electric(idx, e_ref, e_base, h_base, factor):
        def prev_x(value, c):
            halo = pltpu.roll(xf[h_base + c], 123 - 8 * idx, 1)
            return jnp.where(first_lane, halo, pltpu.roll(value, 1, 1))

        drive = None if factor is None else f[13, idx] * factor
        return electric(
            *[f[h_base + c, idx] for c in range(3)], f[h_base, idx - 1], f[h_base + 1, idx - 1],
            *[e_ref[e_base + c, idx] for c in range(3)], qq[idx], gg[idx], drive, prev_x, down_row,
        )

    def body(idx, carry):
        plane_magnetic(idx, f, xf, 0, 3)
        plane_magnetic(idx, f, xf, 6, 9)
        return carry

    lax.fori_loop(0, PLANES + 3, body, 0)
    side_magnetic(xf, 0, 3)
    side_magnetic(xf, 6, 9)

    def body(idx, carry):
        for base, out, factor in ((0, 0, factors[0]), (6, 3, None)):
            new = plane_electric(idx, f, base, base + 3, factor)
            for c in range(3):
                one[out + c, idx] = new[c]
        return carry

    lax.fori_loop(1, PLANES + 3, body, 0)
    side_electric(0, 3, 0, factors[0])
    side_electric(6, 9, 3, None)

    def body(idx, carry):
        plane_magnetic(idx, one, xone, 0, 3)
        plane_magnetic(idx, one, xone, 3, 9)
        return carry

    lax.fori_loop(1, PLANES + 2, body, 0)
    side_magnetic(xone, 0, 3)
    side_magnetic(xone, 3, 9)
    sums[...] = jnp.zeros((LAYERS, ROWS, COLS), F32)

    def body(p, carry):
        idx = p + 2
        two = plane_electric(idx, one, 0, 3, factors[1])
        zero = plane_electric(idx, one, 3, 9, None)
        density = jnp.zeros((ROWS, COLS), F32)
        for c in range(3):
            last = zero[c][0:ROWS]
            e_out[c, p] = last
            h_out[c, p] = f[9 + c, idx, 0:ROWS]
            density = density + f[c, idx, 0:ROWS] * last + one[c, idx, 0:ROWS] * one[3 + c, idx, 0:ROWS]
            density = density + two[c][0:ROWS] * f[6 + c, idx, 0:ROWS]
        sums[layer[p]] = density
        return carry

    lax.fori_loop(0, PLANES, body, 0)


def sum_kernel(got, out):
    total = got[0]
    for i in range(1, got.shape[0]):
        total = total + got[i]
    out[...] = total


def call(kernel, outs, scratch=(), scalars=0, far=0, aliases=None):
    def run(*args):
        near = len(args) - scalars - far
        specs = [pl.BlockSpec(memory_space=pltpu.SMEM)] * scalars
        specs += [pl.BlockSpec(memory_space=pltpu.VMEM)] * near + [pl.BlockSpec(memory_space=pl.ANY)] * far
        size = sum(4 * math.prod(s) for s in outs) + sum(4 * math.prod(a.shape) for a in args)
        return pl.pallas_call(
            kernel,
            out_shape=[jax.ShapeDtypeStruct(s, F32) for s in outs],
            in_specs=specs,
            out_specs=[pl.BlockSpec(memory_space=pltpu.VMEM)] * len(outs),
            scratch_shapes=[pltpu.VMEM(s, F32) if isinstance(s, tuple) else s for s in scratch],
            input_output_aliases=aliases or {},
            compiler_params=pltpu.CompilerParams(vmem_limit_bytes=24 * 2**20),
            cost_estimate=pl.CostEstimate(flops=1000000, bytes_accessed=size, transcendentals=0),
        )(*args)

    return run


def ring(axis, step):
    count = lax.axis_size(axis)
    return [(i, (i + step) % count) for i in range(count)]


def swaps(axis, first, wrap=True):
    count = lax.axis_size(axis)
    pairs = [(i, (i + 1) % count) for i in range(first, count, 2) if wrap or i + 1 < count]
    return pairs + [(b, a) for a, b in pairs]


def local(e_start, h_start, adjoint_e, adjoint_h, permittivity, current, layer_of_cell, pml_cells, start_step):
    raw = (e_start, h_start, adjoint_e, adjoint_h, permittivity, current)
    raw = [pltpu.with_memory_space_constraint(a, pltpu.HBM) for a in raw]
    block, deep, tall = (ROWS, COLS), (DEEP, TALL, COLS), (TALL, COLS)
    f, ya, yb = call(
        first_kernel, [(COMPS,) + deep, (16 * COMPS, COLS), (16 * COMPS, COLS)], [pltpu.SemaphoreType.DMA((COMPS,))], far=6
    )(*raw)
    yb = lax.ppermute(yb, "gy", swaps("gy", 1))
    ya = lax.ppermute(ya, "gy", swaps("gy", 0))
    strips, right, left = call(strip_kernel, [(COMPS,) + block, (2,) + block, (2,) + block])(f)
    zu, zd = call(face_kernel, [(len(BELOW),) + block, (len(ABOVE),) + block], far=2)(f, ya, yb)
    zu = lax.ppermute(zu, "gz", ring("gz", 1))
    zd = lax.ppermute(zd, "gz", ring("gz", -1))
    tiles, strips_rim, xa, xb = call(
        second_kernel, [(COMPS, PLANES, 8, COLS), (COMPS, 8, COLS), (2, TALL, COLS), (2, TALL, COLS)]
    )(ya, yb, right, left)
    xa = lax.ppermute(xa, "gx", swaps("gx", 0))
    xb = lax.ppermute(xb, "gx", swaps("gx", 1))
    sides, rim_up, rim_down = call(
        third_kernel,
        [(COMPS,) + tall, (8 * BELOW_TILES + TALL, COLS), (8 * ABOVE_TILES + TALL, COLS)],
    )(xa, xb, strips, strips_rim, tiles)
    rim_up = lax.ppermute(rim_up, "gz", ring("gz", 1))
    rim_down = lax.ppermute(rim_down, "gz", ring("gz", -1))
    _, sums, e_out, h_out = call(
        main_kernel,
        [(COMPS,) + deep, (LAYERS,) + block, (3, PLANES) + block, (3, PLANES) + block],
        [(6,) + deep, deep, deep, deep, (COMPS,) + tall, (6,) + tall, tall, tall, tall],
        scalars=3,
        aliases={3: 0},
    )(layer_of_cell, pml_cells, start_step, f, zu, zd, tiles, sides, rim_up, rim_down)
    count = lax.axis_size("gz")
    got = lax.all_to_all(sums, "gz", 0, 0, tiled=True)
    (gradient,) = call(sum_kernel, [(LAYERS // count,) + block])(got.reshape((count, LAYERS // count) + block))
    return gradient, e_out, h_out


def solution(mesh):
    fields = P(None, "gz", "gy", "gx")
    cells = P("gz", "gy", "gx")
    return jax.shard_map(
        local,
        mesh=mesh,
        in_specs=(fields, fields, fields, fields, cells, cells, P("gz"), P(), P()),
        out_specs=(cells, fields, fields),
        check_vma=False,
    )
```

```python
import functools
import math

import jax
import jax.numpy as jnp
from jax import lax
from jax.experimental import pallas as pl
from jax.experimental.pallas import tpu as pltpu
from jax.sharding import PartitionSpec as P

F32 = jnp.float32
PLANES, ROWS, COLS = 8, 32, 128
DEEP, TALL = PLANES + 4, ROWS + 8
LAYERS = 16
PERIOD = 64
COMPS = 14
HALF = (3, 4, 5, 9, 10, 11)
UP_FACES = [(k, 7) for k in range(14)] + [(k, 6) for k in (3, 4, 9, 10)]
DOWN_FACES = [(k, 0) for k in (0, 1, 6, 7, 12) + HALF]
UP_ROWS = [(k, 7, 7) for k in range(14)] + [(k, 7, 0) for k in (2, 8)]
DOWN_ROWS = [(k, 0, 7) for k in (0, 1, 6, 7, 12, 3, 5, 9, 11)] + [(k, 0, 6) for k in (1, 7)]
UP_SIDES = [(k, 7) for k in range(14)] + [(k, 6) for k in (4, 10)]
DOWN_SIDES = DOWN_FACES


def face_rows(faces, rows):
    return ROWS * len(faces) + 8 * ((len(rows) + 3) // 4)


def lanes(rows=8):
    return lax.broadcasted_iota(jnp.int32, (rows, COLS), 1)


def subs(rows=8):
    return lax.broadcasted_iota(jnp.int32, (rows, COLS), 0)


def turn(value, shift, axis):
    shift = shift % value.shape[axis]
    return value if shift == 0 else pltpu.roll(value, shift, axis)


def slot(k):
    return k // 8, (k % 8) // 4, k % 4


def slot_mask(k, rows):
    _, half, pair = slot(k)
    lane = lanes(rows)
    inside = ((lane - 16 - 64 * half) & 127) < 64
    return inside & (((lane & 7) >> 1) == pair)


def window(p, rows):
    lane = lanes(rows)
    return (lane >= 8 * (p + 2)) & (lane < 8 * (p + 2) + 4)


def parity(axis):
    return lax.rem(lax.axis_index(axis), 2) == 0


def strip(planes, rows):
    out = jnp.zeros((rows, COLS), F32)
    for p, plane in enumerate(planes):
        out = jnp.where(window(p, rows), turn(plane, 8 * (p + 2) + 2, 1), out)
    return out


def face_pack(strips, rows):
    right = [jnp.zeros((rows, COLS), F32) for _ in range(2)]
    left = [jnp.zeros((rows, COLS), F32) for _ in range(2)]
    for k, value in enumerate(strips):
        array, half, pair = slot(k)
        mask = slot_mask(k, rows)
        right[array] = jnp.where(mask, turn(value, 2 * pair + 64 * half, 1), right[array])
        left[array] = jnp.where(mask, turn(value, 2 * pair - 2 + 64 * half, 1), left[array])
    return right, left


def first_kernel(e, h, ae, ah, eps, cur, f, ya, yb, sems):
    copies = []
    for k in range(COMPS):
        source = (e, h, ae, ah)[k // 3].at[k % 3] if k < 12 else (eps, cur)[k - 12]
        copies.append(pltpu.make_async_copy(source, f.at[k, 2 : PLANES + 2, 0:ROWS], sems.at[k]))
    for copy in copies:
        copy.start()
    even = parity("gy")
    sub = subs()
    for k in range(COMPS):
        copies[k].wait()
        for half in range(2):
            up = jnp.zeros((8, COLS), F32)
            down = jnp.zeros((8, COLS), F32)
            for j in range(4):
                idx = 4 * half + j + 2
                mask = (sub >> 1) == j
                up = jnp.where(mask, turn(f[k, idx, 24:32], 2 * j - 6, 0), up)
                down = jnp.where(mask, turn(f[k, idx, 0:8], 2 * j, 0), down)
            at = 8 * (2 * k + half)
            ya[at : at + 8] = jnp.where(even, up, down)
            yb[at : at + 8] = jnp.where(even, down, up)


def strip_kernel(f, strips, right_out, left_out):
    values = []
    for k in range(COMPS):
        value = strip([f[k, p + 2, 0:ROWS] for p in range(PLANES)], ROWS)
        strips[k] = value
        values.append(value)
    right, left = face_pack(values, ROWS)
    for a in range(2):
        right_out[a] = right[a]
        left_out[a] = left[a]


def profile(position, extent, thickness):
    distance = jnp.minimum(position, extent - 1 - position)
    depth = jnp.maximum(thickness - distance, 0).astype(F32) / thickness.astype(F32)
    return 0.8 * depth * depth


def magnetic(ex, ey, ez, ex_up, ey_up, hx, hy, hz, r, next_x, next_y, at=(0, 1, 2)):
    cx = (next_y(ez, 2) - ez) - (ey_up - ey)
    cy = (ex_up - ex) - (next_x(ez, 2) - ez)
    cz = (next_x(ey, 1) - ey) - (next_y(ex, 0) - ex)
    return [r * (h + h - 0.5 * c) - h for h, c in ((hx, cx), (hy, cy), (hz, cz))]


def electric(hx, hy, hz, hx_down, hy_down, ex, ey, ez, q, g, drive, prev_x, prev_y):
    cx = (hz - prev_y(hz, 2)) - (hy - hy_down)
    cy = (hx - hx_down) - (hz - prev_x(hz, 2))
    cz = (hy - prev_x(hy, 1)) - (hx - prev_y(hx, 0))
    if drive is not None:
        cz = cz - drive
    return [q * (g * e + c) for e, c in ((ex, cx), (ey, cy), (ez, cz))]


def grid_sizes():
    return PLANES * lax.axis_size("gz"), ROWS * lax.axis_size("gy"), COLS * lax.axis_size("gx")


def row_grid():
    row = subs(TALL)
    at = ROWS * lax.axis_index("gy") + jnp.where(row >= 36, row - TALL, row)
    return at, (at >= 0) & (at < grid_sizes()[1])


def damping(sigma, inside):
    return jnp.where(inside, 1.0 / (1.0 + 0.25 * sigma), 0.0)


def electric_coefficients(sigma, inside, permittivity):
    permittivity = jnp.maximum(permittivity, 1.0)
    return jnp.where(inside, 1.0 / (2.0 * permittivity + 0.5 * sigma), 0.0), 2.0 * permittivity - 0.5 * sigma


def block_sigma(pml):
    nz, ny, nx = grid_sizes()
    at, row_in = row_grid()
    flat = profile(at, ny, pml[1]) + profile(COLS * lax.axis_index("gx") + lanes(TALL), nx, pml[2])

    def of_plane(p):
        z_at = jnp.full((TALL, COLS), PLANES * lax.axis_index("gz") + p, jnp.int32)
        sigma = profile(z_at[0:8], nz, pml[0])
        sigma = jnp.concatenate([sigma] * (TALL // 8), axis=0) + flat
        return sigma, row_in & (z_at >= 0) & (z_at < nz)

    return of_plane


def side_sigma(pml):
    nz, ny, nx = grid_sizes()
    at, row_in = row_grid()
    lane = lanes(TALL)
    column = lane & 7
    x_at = COLS * lax.axis_index("gx") + jnp.where(column < 4, COLS - 2 + column, column - 6)
    z_at = PLANES * lax.axis_index("gz") + (lane >> 3) - 2
    inside = row_in & (z_at >= 0) & (z_at < nz) & (x_at >= 0) & (x_at < nx)
    return profile(z_at, nz, pml[0]) + profile(at, ny, pml[1]) + profile(x_at, nx, pml[2]), inside


def up_row(value, _):
    return pltpu.roll(value, TALL - 1, 0)


def down_row(value, _):
    return pltpu.roll(value, 1, 0)


def side_magnetic(e, h, r):
    return magnetic(
        *e, pltpu.roll(e[0], 120, 1), pltpu.roll(e[1], 120, 1), *h, r, lambda v, _: pltpu.roll(v, 127, 1), up_row
    )


def side_electric(h, e, q, g, drive):
    return electric(
        *h, pltpu.roll(h[0], 8, 1), pltpu.roll(h[1], 8, 1), *e, q, g, drive, lambda v, _: pltpu.roll(v, 1, 1), down_row
    )


def face_out(out, faces, rows, value_of):
    for i, (k, p) in enumerate(faces):
        out[ROWS * i : ROWS * i + ROWS] = value_of(k, p)[0:ROWS]
    sub = subs()
    for i in range(0, len(rows), 4):
        tile = jnp.zeros((8, COLS), F32)
        for j, (k, p, first) in enumerate(rows[i : i + 4]):
            tile = jnp.where((sub >> 1) == j, turn(value_of(k, p)[ROWS:TALL], 2 * j - first, 0), tile)
        at = ROWS * len(faces) + 2 * i
        out[at : at + 8] = tile


def face_in(ref, faces, rows, keep):
    got = {}
    for i, (k, p) in enumerate(faces):
        got[k, p] = [ref[ROWS * i : ROWS * i + ROWS] * keep, jnp.zeros((8, COLS), F32)]
    sub = subs()
    for i, (k, p, first) in enumerate(rows):
        at = ROWS * len(faces) + 8 * (i // 4)
        tile = turn(ref[at : at + 8], first - 2 * (i % 4), 0) * keep
        mask = (sub == first) | (sub == (first + 1) % 8)
        got[k, p][1] = jnp.where(mask, tile, got[k, p][1])
    return got


def second_kernel(pml, f, ya, yb, right_in, left_in, tiles, strips, xa, xb, zu, zd):
    index = lax.axis_index("gy")
    even = parity("gy")
    has_after = (index < lax.axis_size("gy") - 1).astype(F32)
    has_before = (index > 0).astype(F32)
    sub = subs()
    values = []
    for k in range(COMPS):
        planes = []
        for half in range(2):
            at = 8 * (2 * k + half)
            got_a, got_b = ya[at : at + 8], yb[at : at + 8]
            after = jnp.where(even, got_a, got_b) * has_after
            before = jnp.where(even, got_b, got_a) * has_before
            for j in range(4):
                tile = jnp.where(sub < 2, turn(after, -2 * j, 0), jnp.where(sub >= 6, turn(before, 6 - 2 * j, 0), 0.0))
                tiles[k, 4 * half + j] = tile
                planes.append(tile)
        value = strip(planes, 8)
        strips[k] = value
        values.append(value)
    right, left = face_pack(values, 8)
    even = parity("gx")
    for a in range(2):
        xa[a, 0:ROWS] = jnp.where(even, right_in[a], left_in[a])
        xb[a, 0:ROWS] = jnp.where(even, left_in[a], right_in[a])
        xa[a, ROWS:TALL] = jnp.where(even, right[a], left[a])
        xb[a, ROWS:TALL] = jnp.where(even, left[a], right[a])

    def field(k, p):
        return jnp.concatenate([f[k, p + 2, 0:ROWS], tiles[k, p]], axis=0)

    of_plane = block_sigma(pml)
    half = {}
    for p in (0, 6):
        r = damping(*of_plane(p))
        for base in (0, 6):
            new = magnetic(
                *[field(base + c, p) for c in range(3)], field(base, p + 1), field(base + 1, p + 1),
                *[field(base + 3 + c, p) for c in range(3)], r, lambda v, _: pltpu.roll(v, COLS - 1, 1), up_row,
            )
            for c in range(3):
                half[base + 3 + c, p] = new[c]

    def value_of(k, p):
        return half[k, p] if (k, p) in half else field(k, p)

    face_out(zu, UP_FACES, UP_ROWS, value_of)
    face_out(zd, DOWN_FACES, DOWN_ROWS, value_of)


def third_kernel(pml, xa, xb, strips, strips_rim, sides, rim_up, rim_down):
    index = lax.axis_index("gx")
    even = parity("gx")
    has_after = (index < lax.axis_size("gx") - 1).astype(F32)
    has_before = (index > 0).astype(F32)
    lane = lanes(TALL)
    pair_of = (lane & 7) >> 1
    own = (lane >= 16) & (lane < 80)
    after = [jnp.where(even, xa[a], xb[a]) * has_after for a in range(2)]
    before = [jnp.where(even, xb[a], xa[a]) * has_before for a in range(2)]
    side = []
    for k in range(COMPS):
        array, half, pair = slot(k)
        mine = jnp.concatenate([strips[k], strips_rim[k]], axis=0)
        value = jnp.where(pair_of == 0, mine, turn(mine, 4, 1))
        value = jnp.where(pair_of == 1, turn(after[array], 2 - 2 * pair - 64 * half, 1), value)
        value = jnp.where(pair_of == 2, turn(before[array], 4 - 2 * pair - 64 * half, 1), value)
        value = jnp.where(own, value, 0.0)
        sides[k] = value
        side.append(value)
    r = damping(*side_sigma(pml))
    stepped = list(side)
    for base in (0, 6):
        stepped[base + 3 : base + 6] = side_magnetic(side[base : base + 3], side[base + 3 : base + 6], r)
    for out, items in ((rim_up, UP_SIDES), (rim_down, DOWN_SIDES)):
        packed = jnp.zeros((TALL, COLS), F32)
        for i, (k, p) in enumerate(items):
            value = side[k] if p == 7 else stepped[k]
            packed = jnp.where((lane >> 3) == i, turn(value, 8 * i - 8 * (p + 2), 1), packed)
        out[...] = packed


def drive_factors(start):
    factors = []
    for k in (1, 2):
        phase = jnp.full((8, COLS), lax.rem(start[0] + k, PERIOD), jnp.int32).astype(F32)
        factor = jnp.sin(phase * (2.0 * math.pi / PERIOD))
        factors.append(jnp.concatenate([factor] * (TALL // 8), axis=0))
    return factors


def spread(first, split, gap):
    return lambda i: i + first + (gap if i >= split else 0)


def home(layer):
    mine = lax.axis_index("gz") >> 1
    return (((layer >> 2) ^ mine) << 2) + (layer & 3)


def run_steps(pml, start, layer, f, one, rr, qq, gg, xf, xone, frozen, planes, sums, put):
    sigma, inside = side_sigma(pml)
    xr = damping(sigma, inside)
    xq, xg = electric_coefficients(sigma, inside, xf[12])
    factors = drive_factors(start)
    lane = lanes(TALL)
    first_lane, last_lane = lane == 0, lane == COLS - 1
    held = (lane >> 3) == -1
    for idx in frozen:
        held = held | ((lane >> 3) == idx)

    def side_half(e_ref, e_base, h_base, hold):
        old = [xf[h_base + c] for c in range(3)]
        new = side_magnetic([e_ref[e_base + c] for c in range(3)], old, xr)
        for c in range(3):
            xf[h_base + c] = jnp.where(held, old[c], new[c]) if hold else new[c]

    def side_full(e_base, h_base, out_base, factor):
        drive = None if factor is None else xf[13] * factor
        new = side_electric(
            [xf[h_base + c] for c in range(3)], [xf[e_base + c] for c in range(3)], xq, xg, drive
        )
        for c in range(3):
            xone[out_base + c] = new[c]

    def plane_magnetic(idx, e_ref, x_ref, e_base, h_base):
        def next_x(value, c):
            halo = pltpu.roll(x_ref[e_base + c], 125 - 8 * idx, 1)
            return jnp.where(last_lane, halo, pltpu.roll(value, COLS - 1, 1))

        new = magnetic(
            *[e_ref[e_base + c, idx] for c in range(3)], e_ref[e_base, idx + 1], e_ref[e_base + 1, idx + 1],
            *[f[h_base + c, idx] for c in range(3)], rr[idx], next_x, up_row,
        )
        for c in range(3):
            f[h_base + c, idx] = new[c]

    def plane_electric(idx, e_ref, e_base, h_base, factor):
        def prev_x(value, c):
            halo = pltpu.roll(xf[h_base + c], 123 - 8 * idx, 1)
            return jnp.where(first_lane, halo, pltpu.roll(value, 1, 1))

        drive = None if factor is None else f[13, idx] * factor
        return electric(
            *[f[h_base + c, idx] for c in range(3)], f[h_base, idx - 1], f[h_base + 1, idx - 1],
            *[e_ref[e_base + c, idx] for c in range(3)], qq[idx], gg[idx], drive, prev_x, down_row,
        )

    def over(which, body):
        count, index = planes[which]

        for i in range(count):
            body(index(i))

    def body(idx):
        plane_magnetic(idx, f, xf, 0, 3)
        plane_magnetic(idx, f, xf, 6, 9)

    over(0, body)
    side_half(xf, 0, 3, True)
    side_half(xf, 6, 9, True)

    def body(idx):
        for base, out, factor in ((0, 0, factors[0]), (6, 3, None)):
            new = plane_electric(idx, f, base, base + 3, factor)
            for c in range(3):
                one[out + c, idx] = new[c]

    over(1, body)
    side_full(0, 3, 0, factors[0])
    side_full(6, 9, 3, None)

    def body(idx):
        plane_magnetic(idx, one, xone, 0, 3)
        plane_magnetic(idx, one, xone, 3, 9)

    over(2, body)
    side_half(xone, 0, 3, False)
    side_half(xone, 3, 9, False)

    def body(idx):
        two = plane_electric(idx, one, 0, 3, factors[1])
        zero = plane_electric(idx, one, 3, 9, None)
        density = jnp.zeros((ROWS, COLS), F32)
        for c in range(3):
            last = zero[c][0:ROWS]
            put(c, idx, last, f[9 + c, idx, 0:ROWS])
            density = density + f[c, idx, 0:ROWS] * last + one[c, idx, 0:ROWS] * one[3 + c, idx, 0:ROWS]
            density = density + two[c][0:ROWS] * f[6 + c, idx, 0:ROWS]
        sums[home(layer[idx - 2])] = density

    over(3, body)


def inner_kernel(layer, pml, start, own, tiles, sides, f, one, rr, qq, gg, sums, e_mid, h_mid, xf, xone):
    del own
    for k in range(COMPS):
        for p in range(PLANES):
            f[k, p + 2, ROWS:TALL] = tiles[k, p]
        xf[k] = sides[k]
    of_plane = block_sigma(pml)

    def coefficients(i, carry):
        sigma, inside = of_plane(i)
        rr[i + 2] = damping(sigma, inside)
        qq[i + 2], gg[i + 2] = electric_coefficients(sigma, inside, f[12, i + 2])
        return carry

    lax.fori_loop(0, PLANES, coefficients, 0)
    sums[...] = jnp.zeros((LAYERS, ROWS, COLS), F32)

    def put(c, idx, e_new, h_new):
        e_mid[c, idx - 4] = e_new
        h_mid[c, idx - 4] = h_new

    planes = [(7, lambda i: i + 2), (6, lambda i: i + 3), (5, lambda i: i + 3), (4, lambda i: i + 4)]
    run_steps(pml, start, layer, f, one, rr, qq, gg, xf, xone, (), planes, sums, put)


def outer_kernel(
    layer, pml, start, f_in, one_in, rr_in, qq_in, gg_in, sums_in, zu, zd, sides, rim_up, rim_down,
    f, one, rr, qq, gg, sums, e_rest, h_rest, first, second, third, xf, xone,
):
    del f_in, one_in, rr_in, qq_in, gg_in, sums_in
    index = lax.axis_index("gz")
    has_above = (index < lax.axis_size("gz") - 1).astype(F32)
    has_below = (index > 0).astype(F32)
    lane = lanes(TALL)
    for k in range(COMPS):
        xf[k] = sides[k]
    for ref, faces, rows, rim, items, shift, keep in (
        (zu, UP_FACES, UP_ROWS, rim_up, UP_SIDES, -6, has_below),
        (zd, DOWN_FACES, DOWN_ROWS, rim_down, DOWN_SIDES, PLANES + 2, has_above),
    ):
        for (k, p), (plane, tile) in face_in(ref, faces, rows, keep).items():
            f[k, p + shift, 0:ROWS] = plane
            f[k, p + shift, ROWS:TALL] = tile
        packed = rim[...] * keep
        for i, (k, p) in enumerate(items):
            xf[k] = jnp.where((lane >> 3) == p + shift, turn(packed, 8 * (p + shift) - 8 * i, 1), xf[k])
    last_lane = lane == COLS - 1
    top = PLANES + 2
    for k, idx in ((4, 0), (10, 0), (4, top), (5, top), (10, top), (11, top)):
        f[k, idx] = jnp.where(last_lane, turn(xf[k], 126 - 8 * idx, 1), f[k, idx])
    of_plane = block_sigma(pml)
    for idx in (1, top):
        sigma, inside = of_plane(idx - 2)
        rr[idx] = damping(sigma, inside)
        qq[idx], gg[idx] = electric_coefficients(sigma, inside, f[12, idx])

    def put(c, idx, e_new, h_new):
        at = idx - 2 if idx < 4 else idx - 6
        e_rest[c, at] = e_new
        h_rest[c, at] = h_new

    planes = [(2, lambda i: 8 * i + 1), (4, spread(1, 2, 6)), (4, spread(1, 2, 5)), (4, spread(2, 2, 4))]
    run_steps(pml, start, layer, f, one, rr, qq, gg, xf, xone, (0, top), planes, sums, put)
    for i, out in enumerate((first, second, third)):
        out[...] = sums[4 * i + 4 : 4 * i + 8]


def store_kernel(e_mid, h_mid, e_rest, h_rest, e_out, h_out, sems):
    copies = []
    for mid, rest, out in ((e_mid, e_rest, e_out), (h_mid, h_rest, h_out)):
        for source, at, first, count in ((mid, 0, 2, 4), (rest, 0, 0, 2), (rest, 2, 6, 2)):
            copies.append((source.at[:, at : at + count], out.at[:, first : first + count]))
    copies = [pltpu.make_async_copy(a, b, sems.at[i]) for i, (a, b) in enumerate(copies)]
    for copy in copies:
        copy.start()
    for copy in copies:
        copy.wait()


def fold_kernel(sums, first, second, third, kept, sent):
    upper = lax.rem(lax.axis_index("gz"), 2) == 1
    for i in range(2):
        low, high = (sums[j] + first[j] + second[j] + third[j] for j in (i, i + 2))
        kept[i] = jnp.where(upper, high, low)
        sent[i] = jnp.where(upper, low, high)


def sum_kernel(kept, got, out):
    out[...] = kept[...] + got[...]


def call(kernel, outs, scratch=(), scalars=0, far=0, aliases=None, out_space=pltpu.VMEM):
    def run(*args):
        near = len(args) - scalars - far
        specs = [pl.BlockSpec(memory_space=pltpu.SMEM)] * scalars
        specs += [pl.BlockSpec(memory_space=pltpu.VMEM)] * near + [pl.BlockSpec(memory_space=pl.ANY)] * far
        size = sum(4 * math.prod(s) for s in outs) + sum(4 * math.prod(a.shape) for a in args)
        return pl.pallas_call(
            kernel,
            out_shape=[jax.ShapeDtypeStruct(s, F32) for s in outs],
            in_specs=specs,
            out_specs=[pl.BlockSpec(memory_space=out_space)] * len(outs),
            scratch_shapes=[pltpu.VMEM(s, F32) if isinstance(s, tuple) else s for s in scratch],
            input_output_aliases=aliases or {},
            compiler_params=pltpu.CompilerParams(vmem_limit_bytes=24 * 2**20),
            cost_estimate=pl.CostEstimate(flops=1000000, bytes_accessed=size, transcendentals=0),
        )(*args)

    return run


def ring(axis, step):
    count = lax.axis_size(axis)
    return [(i, (i + step) % count) for i in range(count)]


def swaps(axis, first):
    count = lax.axis_size(axis)
    pairs = [(i, (i + 1) % count) for i in range(first, count, 2)]
    return pairs + [(b, a) for a, b in pairs]


def across(axis, bits):
    return [(i, i ^ bits) for i in range(lax.axis_size(axis))]


def inner_swaps():
    count, width = lax.axis_size("gy"), lax.axis_size("gx")
    pairs = []
    for j in range(width):
        pairs += [(i * width + j, (i + 1) * width + j) for i in range(1, count - 1, 2)]
        if j % 2 == 0:
            pairs += [(i * width + j, i * width + j + 1) for i in (0, count - 1)]
    return pairs + [(b, a) for a, b in pairs]


def local(e_start, h_start, adjoint_e, adjoint_h, permittivity, current, layer_of_cell, pml_cells, start_step):
    raw = (e_start, h_start, adjoint_e, adjoint_h, permittivity, current)
    raw = [pltpu.with_memory_space_constraint(a, pltpu.HBM) for a in raw]
    block, deep, tall = (ROWS, COLS), (DEEP, TALL, COLS), (TALL, COLS)
    f, ya, yb = call(
        first_kernel, [(COMPS,) + deep, (16 * COMPS, COLS), (16 * COMPS, COLS)], [pltpu.SemaphoreType.DMA((COMPS,))], far=6
    )(*raw)
    yb = lax.ppermute(yb, ("gy", "gx"), inner_swaps())
    ya = lax.ppermute(ya, "gy", swaps("gy", 0))
    strips, right, left = call(strip_kernel, [(COMPS,) + block, (2,) + block, (2,) + block])(f)
    side = (2,) + tall
    tiles, strips_rim, xa, xb, zu, zd = call(
        second_kernel,
        [(COMPS, PLANES, 8, COLS), (COMPS, 8, COLS), side, side, (face_rows(UP_FACES, UP_ROWS), COLS), (face_rows(DOWN_FACES, DOWN_ROWS), COLS)],
        scalars=1,
    )(pml_cells, f, ya, yb, right, left)
    zu = lax.ppermute(zu, "gz", ring("gz", 1))
    zd = lax.ppermute(zd, "gz", ring("gz", -1))
    xa = lax.ppermute(xa, "gx", swaps("gx", 0))
    xb = lax.ppermute(xb, "gx", swaps("gx", 1))
    sides, rim_up, rim_down = call(third_kernel, [(COMPS,) + tall, tall, tall], scalars=1)(pml_cells, xa, xb, strips, strips_rim)
    rim_up = lax.ppermute(rim_up, "gz", ring("gz", 1))
    rim_down = lax.ppermute(rim_down, "gz", ring("gz", -1))
    state = [(COMPS,) + deep, (6,) + deep, deep, deep, deep, (LAYERS,) + block]
    mid, out = (3, PLANES // 2) + block, (3, PLANES) + block
    side = [(COMPS,) + tall, (6,) + tall]
    *held, e_mid, h_mid = call(inner_kernel, state + [mid, mid], side, scalars=3, aliases={3: 0})(
        layer_of_cell, pml_cells, start_step, f, tiles, sides
    )
    quarter, pair = (LAYERS // 4,) + block, (2,) + block
    *_, sums, e_rest, h_rest, first, second, third = call(
        outer_kernel, state + [mid, mid, quarter, quarter, quarter], side, scalars=3, aliases={3 + i: i for i in range(len(state))}
    )(layer_of_cell, pml_cells, start_step, *held, zu, zd, sides, rim_up, rim_down)
    e_out, h_out = call(store_kernel, [out, out], [pltpu.SemaphoreType.DMA((6,))], out_space=pltpu.HBM)(e_mid, h_mid, e_rest, h_rest)
    first, second, third = (lax.ppermute(v, "gz", across("gz", m)) for v, m in ((first, 2), (second, 4), (third, 6)))
    kept, sent = call(fold_kernel, [pair, pair])(sums, first, second, third)
    (gradient,) = call(sum_kernel, [pair])(kept, lax.ppermute(sent, "gz", across("gz", 1)))
    return gradient, e_out, h_out


def solution(mesh):
    fields = P(None, "gz", "gy", "gx")
    cells = P("gz", "gy", "gx")
    return jax.shard_map(
        local,
        mesh=mesh,
        in_specs=(fields, fields, fields, fields, cells, cells, P("gz"), P(), P()),
        out_specs=(cells, fields, fields),
        check_vma=False,
    )
```

```python
import functools
import math

import jax
import jax.numpy as jnp
from jax import lax
from jax.experimental import pallas as pl
from jax.experimental.pallas import tpu as pltpu
from jax.sharding import PartitionSpec as P

F32 = jnp.float32
PLANES, ROWS, COLS = 8, 32, 128
DEEP, TALL = PLANES + 4, ROWS + 8
LAYERS = 16
PERIOD = 64
COMPS = 14
UP_FACES = [("h", k) for k in (3, 4, 9, 10)] + [("e", k) for k in (0, 1, 2, 6, 7, 8)] + [("f", 12)]
DOWN_FACES = [("f", k) for k in (0, 1, 6, 7, 12)] + [("e", k) for k in (0, 1, 6, 7)]
UP_ROWS = [("h", k, 7) for k in (3, 4, 9, 10)] + [("e", 2, 7), ("e", 8, 7), ("f", 12, 7)]
DOWN_ROWS = [("f", k, 7) for k in (0, 1, 6, 7, 12)] + [("e", 1, 7), ("e", 7, 7), ("f", 1, 6), ("f", 7, 6)]
UP_SIDES, DOWN_SIDES = UP_FACES, DOWN_FACES


def face_rows(faces, rows):
    return ROWS * len(faces) + 8 * ((len(rows) + 3) // 4)


def lanes(rows=8):
    return lax.broadcasted_iota(jnp.int32, (rows, COLS), 1)


def subs(rows=8):
    return lax.broadcasted_iota(jnp.int32, (rows, COLS), 0)


def turn(value, shift, axis):
    shift = shift % value.shape[axis]
    return value if shift == 0 else pltpu.roll(value, shift, axis)


def slot(k):
    return k // 8, (k % 8) // 4, k % 4


def slot_mask(k, rows):
    _, half, pair = slot(k)
    lane = lanes(rows)
    inside = ((lane - 16 - 64 * half) & 127) < 64
    return inside & (((lane & 7) >> 1) == pair)


def window(p, rows):
    lane = lanes(rows)
    return (lane >= 8 * (p + 2)) & (lane < 8 * (p + 2) + 4)


def parity(axis):
    return lax.rem(lax.axis_index(axis), 2) == 0


def strip(planes, rows):
    out = jnp.zeros((rows, COLS), F32)
    for p, plane in enumerate(planes):
        out = jnp.where(window(p, rows), turn(plane, 8 * (p + 2) + 2, 1), out)
    return out


def face_pack(strips, rows):
    right = [jnp.zeros((rows, COLS), F32) for _ in range(2)]
    left = [jnp.zeros((rows, COLS), F32) for _ in range(2)]
    for k, value in enumerate(strips):
        array, half, pair = slot(k)
        mask = slot_mask(k, rows)
        right[array] = jnp.where(mask, turn(value, 2 * pair + 64 * half, 1), right[array])
        left[array] = jnp.where(mask, turn(value, 2 * pair - 2 + 64 * half, 1), left[array])
    return right, left


def first_kernel(e, h, ae, ah, eps, cur, f, ya, yb, sems):
    copies = []
    for k in range(COMPS):
        source = (e, h, ae, ah)[k // 3].at[k % 3] if k < 12 else (eps, cur)[k - 12]
        copies.append(pltpu.make_async_copy(source, f.at[k, 2 : PLANES + 2, 0:ROWS], sems.at[k]))
    for copy in copies:
        copy.start()
    even = parity("gy")
    sub = subs()
    for k in range(COMPS):
        copies[k].wait()
        for half in range(2):
            up = jnp.zeros((8, COLS), F32)
            down = jnp.zeros((8, COLS), F32)
            for j in range(4):
                idx = 4 * half + j + 2
                mask = (sub >> 1) == j
                up = jnp.where(mask, turn(f[k, idx, 24:32], 2 * j - 6, 0), up)
                down = jnp.where(mask, turn(f[k, idx, 0:8], 2 * j, 0), down)
            at = 8 * (2 * k + half)
            ya[at : at + 8] = jnp.where(even, up, down)
            yb[at : at + 8] = jnp.where(even, down, up)


def strip_kernel(start, f, strips, right_out, left_out, factors):
    for k in range(2):
        phase = jnp.full((8, COLS), lax.rem(start[0] + k + 1, PERIOD), jnp.int32).astype(F32)
        factors[k] = jnp.sin(phase * (2.0 * math.pi / PERIOD))
    values = []
    for k in range(COMPS):
        value = strip([f[k, p + 2, 0:ROWS] for p in range(PLANES)], ROWS)
        strips[k] = value
        values.append(value)
    right, left = face_pack(values, ROWS)
    for a in range(2):
        right_out[a] = right[a]
        left_out[a] = left[a]


def profile(position, extent, thickness):
    distance = jnp.minimum(position, extent - 1 - position)
    depth = jnp.maximum(thickness - distance, 0).astype(F32) / thickness.astype(F32)
    return 0.8 * depth * depth


def magnetic(ex, ey, ez, ex_up, ey_up, hx, hy, hz, r, next_x, next_y, at=(0, 1, 2)):
    cx = (next_y(ez, 2) - ez) - (ey_up - ey)
    cy = (ex_up - ex) - (next_x(ez, 2) - ez)
    cz = (next_x(ey, 1) - ey) - (next_y(ex, 0) - ex)
    return [r * (h + h - 0.5 * c) - h for h, c in ((hx, cx), (hy, cy), (hz, cz))]


def electric(hx, hy, hz, hx_down, hy_down, ex, ey, ez, q, g, drive, prev_x, prev_y):
    cx = (hz - prev_y(hz, 2)) - (hy - hy_down)
    cy = (hx - hx_down) - (hz - prev_x(hz, 2))
    cz = (hy - prev_x(hy, 1)) - (hx - prev_y(hx, 0))
    if drive is not None:
        cz = cz - drive
    return [q * (g * e + c) for e, c in ((ex, cx), (ey, cy), (ez, cz))]


def grid_sizes():
    return PLANES * lax.axis_size("gz"), ROWS * lax.axis_size("gy"), COLS * lax.axis_size("gx")


def row_grid():
    row = subs(TALL)
    at = ROWS * lax.axis_index("gy") + jnp.where(row >= 36, row - TALL, row)
    return at, (at >= 0) & (at < grid_sizes()[1])


def damping(sigma, inside):
    return jnp.where(inside, 1.0 / (1.0 + 0.25 * sigma), 0.0)


def electric_coefficients(sigma, inside, permittivity):
    permittivity = jnp.maximum(permittivity, 1.0)
    return jnp.where(inside, 1.0 / (2.0 * permittivity + 0.5 * sigma), 0.0), 2.0 * permittivity - 0.5 * sigma


def block_sigma(pml):
    nz, ny, nx = grid_sizes()
    at, row_in = row_grid()
    flat = profile(at, ny, pml[1]) + profile(COLS * lax.axis_index("gx") + lanes(TALL), nx, pml[2])

    def of_plane(p):
        z_at = jnp.full((TALL, COLS), PLANES * lax.axis_index("gz") + p, jnp.int32)
        sigma = profile(z_at[0:8], nz, pml[0])
        sigma = jnp.concatenate([sigma] * (TALL // 8), axis=0) + flat
        return sigma, row_in & (z_at >= 0) & (z_at < nz)

    return of_plane


def side_sigma(pml):
    nz, ny, nx = grid_sizes()
    at, row_in = row_grid()
    lane = lanes(TALL)
    column = lane & 7
    x_at = COLS * lax.axis_index("gx") + jnp.where(column < 4, COLS - 2 + column, column - 6)
    z_at = PLANES * lax.axis_index("gz") + (lane >> 3) - 2
    inside = row_in & (z_at >= 0) & (z_at < nz) & (x_at >= 0) & (x_at < nx)
    return profile(z_at, nz, pml[0]) + profile(at, ny, pml[1]) + profile(x_at, nx, pml[2]), inside


def up_row(value, _):
    return pltpu.roll(value, TALL - 1, 0)


def down_row(value, _):
    return pltpu.roll(value, 1, 0)


def side_magnetic(e, h, r):
    return magnetic(
        *e, pltpu.roll(e[0], 120, 1), pltpu.roll(e[1], 120, 1), *h, r, lambda v, _: pltpu.roll(v, 127, 1), up_row
    )


def side_electric(h, e, q, g, drive):
    return electric(
        *h, pltpu.roll(h[0], 8, 1), pltpu.roll(h[1], 8, 1), *e, q, g, drive, lambda v, _: pltpu.roll(v, 1, 1), down_row
    )


def face_out(out, faces, rows, values):
    for i, item in enumerate(faces):
        out[ROWS * i : ROWS * i + ROWS] = values[item][0:ROWS]
    sub = subs()
    for i in range(0, len(rows), 4):
        tile = jnp.zeros((8, COLS), F32)
        for j, (kind, k, first) in enumerate(rows[i : i + 4]):
            tile = jnp.where((sub >> 1) == j, turn(values[kind, k][ROWS:TALL], 2 * j - first, 0), tile)
        at = ROWS * len(faces) + 2 * i
        out[at : at + 8] = tile


def face_in(ref, faces, rows, keep):
    got = {}
    for i, item in enumerate(faces):
        got[item] = [ref[ROWS * i : ROWS * i + ROWS] * keep, jnp.zeros((8, COLS), F32)]
    sub = subs()
    for i, (kind, k, first) in enumerate(rows):
        at = ROWS * len(faces) + 8 * (i // 4)
        tile = turn(ref[at : at + 8], first - 2 * (i % 4), 0) * keep
        mask = (sub == first) | (sub == (first + 1) % 8)
        got[kind, k][1] = jnp.where(mask, tile, got[kind, k][1])
    return {item: jnp.concatenate(parts, axis=0) for item, parts in got.items()}


def second_kernel(ya, yb, right_in, left_in, tiles, strips, xa, xb):
    index = lax.axis_index("gy")
    even = parity("gy")
    has_after = (index < lax.axis_size("gy") - 1).astype(F32)
    has_before = (index > 0).astype(F32)
    sub = subs()
    values = []
    for k in range(COMPS):
        planes = []
        for half in range(2):
            at = 8 * (2 * k + half)
            got_a, got_b = ya[at : at + 8], yb[at : at + 8]
            after = jnp.where(even, got_a, got_b) * has_after
            before = jnp.where(even, got_b, got_a) * has_before
            for j in range(4):
                tile = jnp.where(sub < 2, turn(after, -2 * j, 0), jnp.where(sub >= 6, turn(before, 6 - 2 * j, 0), 0.0))
                tiles[k, 4 * half + j] = tile
                planes.append(tile)
        value = strip(planes, 8)
        strips[k] = value
        values.append(value)
    right, left = face_pack(values, 8)
    even = parity("gx")
    for a in range(2):
        xa[a, 0:ROWS] = jnp.where(even, right_in[a], left_in[a])
        xb[a, 0:ROWS] = jnp.where(even, left_in[a], right_in[a])
        xa[a, ROWS:TALL] = jnp.where(even, right[a], left[a])
        xb[a, ROWS:TALL] = jnp.where(even, left[a], right[a])


def face_kernel(pml, f, tiles, factors, zu, zd):
    def field(k, p):
        return jnp.concatenate([f[k, p + 2, 0:ROWS], tiles[k, p]], axis=0)

    of_plane = block_sigma(pml)
    zero = jnp.zeros((TALL, COLS), F32)
    drive = jnp.concatenate([factors[0]] * (TALL // 8), axis=0) * field(13, 7)

    def next_x(value, _):
        return pltpu.roll(value, COLS - 1, 1)

    def prev_x(value, _):
        return pltpu.roll(value, 1, 1)

    def half_step(base, p):
        up = [field(base + c, p + 1) for c in range(2)] if p < 7 else [zero, zero]
        return magnetic(
            *[field(base + c, p) for c in range(3)], *up, *[field(base + 3 + c, p) for c in range(3)],
            damping(*of_plane(p)), next_x, up_row,
        )

    for out, p, faces, rows in ((zu, 7, UP_FACES, UP_ROWS), (zd, 0, DOWN_FACES, DOWN_ROWS)):
        values = {("f", k): field(k, p) for k in (0, 1, 6, 7, 12)}
        q, g = electric_coefficients(*of_plane(p), values["f", 12])
        for base in (0, 6):
            h = half_step(base, p)
            down = half_step(base, 6)[0:2] if p == 7 else [zero, zero]
            e = electric(
                *h, *down, *[field(base + c, p) for c in range(3)], q, g, drive if p == 7 and base == 0 else None, prev_x, down_row
            )
            for c in range(3):
                values["h", base + 3 + c] = h[c]
                values["e", base + c] = e[c]
        face_out(out, faces, rows, values)


def third_kernel(pml, xa, xb, strips, strips_rim, factors, sides, rim_up, rim_down):
    index = lax.axis_index("gx")
    even = parity("gx")
    has_after = (index < lax.axis_size("gx") - 1).astype(F32)
    has_before = (index > 0).astype(F32)
    lane = lanes(TALL)
    pair_of = (lane & 7) >> 1
    own = (lane >= 16) & (lane < 80)
    after = [jnp.where(even, xa[a], xb[a]) * has_after for a in range(2)]
    before = [jnp.where(even, xb[a], xa[a]) * has_before for a in range(2)]
    side = []
    for k in range(COMPS):
        array, half, pair = slot(k)
        mine = jnp.concatenate([strips[k], strips_rim[k]], axis=0)
        value = jnp.where(pair_of == 0, mine, turn(mine, 4, 1))
        value = jnp.where(pair_of == 1, turn(after[array], 2 - 2 * pair - 64 * half, 1), value)
        value = jnp.where(pair_of == 2, turn(before[array], 4 - 2 * pair - 64 * half, 1), value)
        value = jnp.where(own, value, 0.0)
        sides[k] = value
        side.append(value)
    sigma, inside = side_sigma(pml)
    r = damping(sigma, inside)
    q, g = electric_coefficients(sigma, inside, side[12])
    drive = jnp.concatenate([factors[0]] * (TALL // 8), axis=0) * side[13]
    values = {("f", k): side[k] for k in range(COMPS)}
    for base in (0, 6):
        e = side[base : base + 3]
        h = [jnp.where(own, v, 0.0) for v in side_magnetic(e, side[base + 3 : base + 6], r)]
        e = side_electric(h, e, q, g, drive if base == 0 else None)
        for c in range(3):
            values["h", base + 3 + c] = h[c]
            values["e", base + c] = e[c]
    for out, items, p in ((rim_up, UP_SIDES, 7), (rim_down, DOWN_SIDES, 0)):
        packed = jnp.zeros((TALL, COLS), F32)
        for i, item in enumerate(items):
            packed = jnp.where((lane >> 3) == i, turn(values[item], 8 * i - 8 * (p + 2), 1), packed)
        out[...] = packed


def home(layer):
    mine = lax.axis_index("gz") >> 1
    return (((layer >> 2) ^ mine) << 2) + (layer & 3)


def run_steps(pml, factors, layer, f, one, rr, qq, gg, xf, xone, planes, sums, put, halo=None):
    sigma, inside = side_sigma(pml)
    xr = damping(sigma, inside)
    xq, xg = electric_coefficients(sigma, inside, xf[12])
    factors = [jnp.concatenate([factors[k]] * (TALL // 8), axis=0) for k in range(2)]
    lane = lanes(TALL)
    first_lane, last_lane = lane == 0, lane == COLS - 1

    def side_half(e_ref, e_base, h_base):
        new = side_magnetic([e_ref[e_base + c] for c in range(3)], [xf[h_base + c] for c in range(3)], xr)
        for c in range(3):
            xf[h_base + c] = new[c]

    def side_full(e_base, h_base, out_base, factor):
        drive = None if factor is None else xf[13] * factor
        new = side_electric(
            [xf[h_base + c] for c in range(3)], [xf[e_base + c] for c in range(3)], xq, xg, drive
        )
        for c in range(3):
            xone[out_base + c] = new[c]

    def plane_magnetic(idx, e_ref, x_ref, e_base, h_base):
        def next_x(value, c):
            halo = pltpu.roll(x_ref[e_base + c], 125 - 8 * idx, 1)
            return jnp.where(last_lane, halo, pltpu.roll(value, COLS - 1, 1))

        new = magnetic(
            *[e_ref[e_base + c, idx] for c in range(3)], e_ref[e_base, idx + 1], e_ref[e_base + 1, idx + 1],
            *[f[h_base + c, idx] for c in range(3)], rr[idx], next_x, up_row,
        )
        for c in range(3):
            f[h_base + c, idx] = new[c]

    def plane_electric(idx, e_ref, e_base, h_base, factor):
        def prev_x(value, c):
            halo = pltpu.roll(xf[h_base + c], 123 - 8 * idx, 1)
            return jnp.where(first_lane, halo, pltpu.roll(value, 1, 1))

        drive = None if factor is None else f[13, idx] * factor
        return electric(
            *[f[h_base + c, idx] for c in range(3)], f[h_base, idx - 1], f[h_base + 1, idx - 1],
            *[e_ref[e_base + c, idx] for c in range(3)], qq[idx], gg[idx], drive, prev_x, down_row,
        )

    def over(which, body):
        for idx in planes[which]:
            body(idx)

    def body(idx):
        plane_magnetic(idx, f, xf, 0, 3)
        plane_magnetic(idx, f, xf, 6, 9)

    over(0, body)
    side_half(xf, 0, 3)
    side_half(xf, 6, 9)
    if halo is not None:
        halo(xr, xq, sides=False)

    def body(idx):
        for base, out, factor in ((0, 0, factors[0]), (6, 3, None)):
            new = plane_electric(idx, f, base, base + 3, factor)
            for c in range(3):
                one[out + c, idx] = new[c]

    over(1, body)
    side_full(0, 3, 0, factors[0])
    side_full(6, 9, 3, None)
    if halo is not None:
        halo(xr, xq, sides=True)

    def body(idx):
        plane_magnetic(idx, one, xone, 0, 3)
        plane_magnetic(idx, one, xone, 3, 9)

    over(2, body)
    side_half(xone, 0, 3)
    side_half(xone, 3, 9)

    def body(idx):
        two = plane_electric(idx, one, 0, 3, factors[1])
        zero = plane_electric(idx, one, 3, 9, None)
        density = jnp.zeros((ROWS, COLS), F32)
        for c in range(3):
            last = zero[c][0:ROWS]
            put(c, idx, last, f[9 + c, idx, 0:ROWS])
            density = density + f[c, idx, 0:ROWS] * last + one[c, idx, 0:ROWS] * one[3 + c, idx, 0:ROWS]
            density = density + two[c][0:ROWS] * f[6 + c, idx, 0:ROWS]
        sums[home(layer[idx - 2])] = density

    over(3, body)


def inner_kernel(layer, pml, factors, own, tiles, sides, f, one, rr, qq, gg, sums, e_mid, h_mid, xf, xone):
    del own
    for k in range(COMPS):
        for p in range(PLANES):
            f[k, p + 2, ROWS:TALL] = tiles[k, p]
        xf[k] = sides[k]
    of_plane = block_sigma(pml)

    def coefficients(i, carry):
        sigma, inside = of_plane(i)
        rr[i + 2] = damping(sigma, inside)
        qq[i + 2], gg[i + 2] = electric_coefficients(sigma, inside, f[12, i + 2])
        return carry

    lax.fori_loop(0, PLANES, coefficients, 0)
    sums[...] = jnp.zeros((LAYERS, ROWS, COLS), F32)

    def put(c, idx, e_new, h_new):
        e_mid[c, idx - 4] = e_new
        h_mid[c, idx - 4] = h_new

    planes = [range(2, 9), range(3, 9), range(3, 8), range(4, 8)]
    run_steps(pml, factors, layer, f, one, rr, qq, gg, xf, xone, planes, sums, put)


def outer_kernel(
    layer, pml, factors, f_in, one_in, rr_in, qq_in, gg_in, sums_in, zu, zd, sides, rim_up, rim_down,
    f, one, rr, qq, gg, sums, e_rest, h_rest, first, second, third, xf, xone,
):
    del f_in, one_in, rr_in, qq_in, gg_in, sums_in
    index = lax.axis_index("gz")
    has_above = (index < lax.axis_size("gz") - 1).astype(F32)
    has_below = (index > 0).astype(F32)
    lane = lanes(TALL)
    low, top = 1, PLANES + 2
    for k in range(COMPS):
        xf[k] = sides[k]
    got = {}
    for ref, faces, rows, rim, items, idx, keep in (
        (zu, UP_FACES, UP_ROWS, rim_up, UP_SIDES, low, has_below),
        (zd, DOWN_FACES, DOWN_ROWS, rim_down, DOWN_SIDES, top, has_above),
    ):
        packed = rim[...] * keep
        planes = face_in(ref, faces, rows, keep)
        for i, (kind, k) in enumerate(items):
            if kind != "f":
                at_last, at_first = turn(packed, 126 - 8 * i, 1), turn(packed, -6 - 8 * i, 1)
                fixed = jnp.where(lane == COLS - 1, at_last, planes[kind, k])
                planes[kind, k] = jnp.where(lane == 0, at_first, fixed) if kind == "e" else fixed
            got[kind, k, idx] = (planes[kind, k], turn(packed, 8 * idx - 8 * i, 1))
        for k in (0, 1, 6, 7, 12):
            if ("f", k) in planes:
                f[k, idx] = planes["f", k]
                xf[k] = jnp.where((lane >> 3) == idx, got["f", k, idx][1], xf[k])
    of_plane = block_sigma(pml)
    for idx in (low, top):
        sigma, inside = of_plane(idx - 2)
        rr[idx] = damping(sigma, inside)
        qq[idx], gg[idx] = electric_coefficients(sigma, inside, f[12, idx])

    def add_z(q, x, y, prev_x):
        return q * ((y - prev_x(y)) - (x - down_row(x, 0)))

    def halo(xr, xq, sides):
        q, q_top, r_half = qq[low], qq[top], 0.5 * rr[low]
        for base, out in ((0, 0), (6, 3)):
            x_side = 0.5 * xr * pltpu.roll(xf[base + 1], 120, 1)
            y_side = -0.5 * xr * pltpu.roll(xf[base], 120, 1)
            if sides:
                added = got["e", base + 2, low][1] + add_z(xq, x_side, y_side, lambda v: pltpu.roll(v, 1, 1))
                xone[out + 2] = jnp.where((lane >> 3) == low, added, xone[out + 2])
                added = got["e", base, top][1] + xq * pltpu.roll(xf[base + 4], 8, 1)
                xone[out] = jnp.where((lane >> 3) == top, added, xone[out])
                added = got["e", base + 1, top][1] - xq * pltpu.roll(xf[base + 3], 8, 1)
                xone[out + 1] = jnp.where((lane >> 3) == top, added, xone[out + 1])
                continue
            x, y = r_half * f[base + 1, 2], -r_half * f[base, 2]

            def prev_x(value):
                return jnp.where(lane == 0, pltpu.roll(y_side, 123 - 8 * low, 1), pltpu.roll(value, 1, 1))

            for k, term, side_term in ((base + 3, x, x_side), (base + 4, y, y_side)):
                plane, side = got["h", k, low]
                f[k, low] = plane + term
                xf[k] = jnp.where((lane >> 3) == low, side + side_term, xf[k])
            f[base + 5, low] = jnp.zeros((TALL, COLS), F32)
            one[out, low] = got["e", base, low][0] - q * y
            one[out + 1, low] = got["e", base + 1, low][0] + q * x
            one[out + 2, low] = got["e", base + 2, low][0] + add_z(q, x, y, prev_x)
            one[out, top] = got["e", base, top][0] + q_top * f[base + 4, top - 1]
            one[out + 1, top] = got["e", base + 1, top][0] - q_top * f[base + 3, top - 1]

    def put(c, idx, e_new, h_new):
        at = idx - 2 if idx < 4 else idx - 6
        e_rest[c, at] = e_new
        h_rest[c, at] = h_new

    planes = [(9,), (2, 9), (1, 2, 8, 9), (2, 3, 8, 9)]
    run_steps(pml, factors, layer, f, one, rr, qq, gg, xf, xone, planes, sums, put, halo)
    for i, out in enumerate((first, second, third)):
        out[...] = sums[4 * i + 4 : 4 * i + 8]


def store_kernel(e_mid, h_mid, e_rest, h_rest, e_out, h_out, sems):
    copies = []
    for mid, rest, out in ((e_mid, e_rest, e_out), (h_mid, h_rest, h_out)):
        for source, at, first, count in ((mid, 0, 2, 4), (rest, 0, 0, 2), (rest, 2, 6, 2)):
            copies.append((source.at[:, at : at + count], out.at[:, first : first + count]))
    copies = [pltpu.make_async_copy(a, b, sems.at[i]) for i, (a, b) in enumerate(copies)]
    for copy in copies:
        copy.start()
    for copy in copies:
        copy.wait()


def fold_kernel(sums, first, second, third, kept, sent):
    upper = lax.rem(lax.axis_index("gz"), 2) == 1
    for i in range(2):
        low, high = (sums[j] + first[j] + second[j] + third[j] for j in (i, i + 2))
        kept[i] = jnp.where(upper, high, low)
        sent[i] = jnp.where(upper, low, high)


def sum_kernel(kept, got, out):
    out[...] = kept[...] + got[...]


def call(kernel, outs, scratch=(), scalars=0, far=0, aliases=None, out_space=pltpu.VMEM, flops=1000000):
    def run(*args):
        near = len(args) - scalars - far
        specs = [pl.BlockSpec(memory_space=pltpu.SMEM)] * scalars
        specs += [pl.BlockSpec(memory_space=pltpu.VMEM)] * near + [pl.BlockSpec(memory_space=pl.ANY)] * far
        size = sum(4 * math.prod(s) for s in outs) + sum(4 * math.prod(a.shape) for a in args)
        return pl.pallas_call(
            kernel,
            out_shape=[jax.ShapeDtypeStruct(s, F32) for s in outs],
            in_specs=specs,
            out_specs=[pl.BlockSpec(memory_space=out_space)] * len(outs),
            scratch_shapes=[pltpu.VMEM(s, F32) if isinstance(s, tuple) else s for s in scratch],
            input_output_aliases=aliases or {},
            compiler_params=pltpu.CompilerParams(vmem_limit_bytes=24 * 2**20),
            cost_estimate=pl.CostEstimate(flops=flops, bytes_accessed=size, transcendentals=0),
        )(*args)

    return run


def ring(axis, step):
    count = lax.axis_size(axis)
    return [(i, (i + step) % count) for i in range(count)]


def swaps(axis, first):
    count = lax.axis_size(axis)
    pairs = [(i, (i + 1) % count) for i in range(first, count, 2)]
    return pairs + [(b, a) for a, b in pairs]


def across(axis, bits):
    return [(i, i ^ bits) for i in range(lax.axis_size(axis))]


def inner_swaps():
    count, width = lax.axis_size("gy"), lax.axis_size("gx")
    pairs = []
    for j in range(width):
        pairs += [(i * width + j, (i + 1) * width + j) for i in range(1, count - 1, 2)]
        if j % 2 == 0:
            pairs += [(i * width + j, i * width + j + 1) for i in (0, count - 1)]
    return pairs + [(b, a) for a, b in pairs]


def local(e_start, h_start, adjoint_e, adjoint_h, permittivity, current, layer_of_cell, pml_cells, start_step):
    raw = (e_start, h_start, adjoint_e, adjoint_h, permittivity, current)
    raw = [pltpu.with_memory_space_constraint(a, pltpu.HBM) for a in raw]
    block, deep, tall = (ROWS, COLS), (DEEP, TALL, COLS), (TALL, COLS)
    f, ya, yb = call(
        first_kernel, [(COMPS,) + deep, (16 * COMPS, COLS), (16 * COMPS, COLS)], [pltpu.SemaphoreType.DMA((COMPS,))], far=6
    )(*raw)
    yb = lax.ppermute(yb, ("gy", "gx"), inner_swaps())
    ya = lax.ppermute(ya, "gy", swaps("gy", 0))
    strips, right, left, factors = call(
        strip_kernel, [(COMPS,) + block, (2,) + block, (2,) + block, (2, 8, COLS)], scalars=1
    )(start_step, f)
    side = (2,) + tall
    tiles, strips_rim, xa, xb = call(second_kernel, [(COMPS, PLANES, 8, COLS), (COMPS, 8, COLS), side, side])(ya, yb, right, left)
    sizes = [(face_rows(*lists), COLS) for lists in ((UP_FACES, UP_ROWS), (DOWN_FACES, DOWN_ROWS))]
    zu, zd = call(face_kernel, sizes, scalars=1)(pml_cells, f, tiles, factors)
    zu = lax.ppermute(zu, "gz", ring("gz", 1))
    zd = lax.ppermute(zd, "gz", ring("gz", -1))
    xa = lax.ppermute(xa, "gx", swaps("gx", 0))
    xb = lax.ppermute(xb, "gx", swaps("gx", 1))
    sides, rim_up, rim_down = call(third_kernel, [(COMPS,) + tall, tall, tall], scalars=1)(pml_cells, xa, xb, strips, strips_rim, factors)
    rim_up = lax.ppermute(rim_up, "gz", ring("gz", 1))
    rim_down = lax.ppermute(rim_down, "gz", ring("gz", -1))
    state = [(COMPS,) + deep, (6,) + deep, deep, deep, deep, (LAYERS,) + block]
    mid, out = (3, PLANES // 2) + block, (3, PLANES) + block
    side = [(COMPS,) + tall, (6,) + tall]
    *held, e_mid, h_mid = call(inner_kernel, state + [mid, mid], side, scalars=2, aliases={3: 0}, flops=10**11)(
        layer_of_cell, pml_cells, factors, f, tiles, sides
    )
    quarter, pair = (LAYERS // 4,) + block, (2,) + block
    *_, sums, e_rest, h_rest, first, second, third = call(
        outer_kernel, state + [mid, mid, quarter, quarter, quarter], side, scalars=2, aliases={3 + i: i for i in range(len(state))}
    )(layer_of_cell, pml_cells, factors, *held, zu, zd, sides, rim_up, rim_down)
    e_out, h_out = call(store_kernel, [out, out], [pltpu.SemaphoreType.DMA((6,))], out_space=pltpu.HBM)(e_mid, h_mid, e_rest, h_rest)
    first, second, third = (lax.ppermute(v, "gz", across("gz", m)) for v, m in ((first, 2), (second, 4), (third, 6)))
    kept, sent = call(fold_kernel, [pair, pair])(sums, first, second, third)
    (gradient,) = call(sum_kernel, [pair])(kept, lax.ppermute(sent, "gz", across("gz", 1)))
    return gradient, e_out, h_out


def solution(mesh):
    fields = P(None, "gz", "gy", "gx")
    cells = P("gz", "gy", "gx")
    return jax.shard_map(
        local,
        mesh=mesh,
        in_specs=(fields, fields, fields, fields, cells, cells, P("gz"), P(), P()),
        out_specs=(cells, fields, fields),
        check_vma=False,
    )
```

```python
import functools
import math

import jax
import jax.numpy as jnp
from jax import lax
from jax.experimental import pallas as pl
from jax.experimental.pallas import tpu as pltpu
from jax.sharding import PartitionSpec as P

F32 = jnp.float32
PLANES, ROWS, COLS = 8, 32, 128
DEEP, TALL = PLANES + 4, ROWS + 8
LAYERS = 16
PERIOD = 64
COMPS = 14
UP_FACES = [("h", k) for k in (3, 4, 9, 10)] + [("e", k) for k in (0, 1, 2, 6, 7, 8)] + [("f", 12)]
DOWN_FACES = [("f", k) for k in (0, 1, 6, 7, 12)] + [("e", k) for k in (0, 1, 6, 7)]
UP_ROWS = [("h", k, 7) for k in (3, 4, 9, 10)] + [("e", 2, 7), ("e", 8, 7), ("f", 12, 7)]
DOWN_ROWS = [("f", k, 7) for k in (0, 1, 6, 7, 12)] + [("e", 1, 7), ("e", 7, 7), ("f", 1, 6), ("f", 7, 6)]
UP_SIDES, DOWN_SIDES = UP_FACES, DOWN_FACES


def face_rows(faces, rows):
    return ROWS * len(faces) + 8 * ((len(rows) + 3) // 4)


FACE_ROWS = max(face_rows(UP_FACES, UP_ROWS), face_rows(DOWN_FACES, DOWN_ROWS))


def lanes(rows=8):
    return lax.broadcasted_iota(jnp.int32, (rows, COLS), 1)


def subs(rows=8):
    return lax.broadcasted_iota(jnp.int32, (rows, COLS), 0)


def turn(value, shift, axis):
    shift = shift % value.shape[axis]
    return value if shift == 0 else pltpu.roll(value, shift, axis)


def slot(k):
    return k // 8, (k % 8) // 4, k % 4


def slot_mask(k, rows):
    _, half, pair = slot(k)
    lane = lanes(rows)
    inside = ((lane - 16 - 64 * half) & 127) < 64
    return inside & (((lane & 7) >> 1) == pair)


def window(p, rows):
    lane = lanes(rows)
    return (lane >= 8 * (p + 2)) & (lane < 8 * (p + 2) + 4)


def parity(axis):
    return lax.rem(lax.axis_index(axis), 2) == 0


def strip(planes, rows):
    out = jnp.zeros((rows, COLS), F32)
    for p, plane in enumerate(planes):
        out = jnp.where(window(p, rows), turn(plane, 8 * (p + 2) + 2, 1), out)
    return out


def face_pack(strips, rows):
    right = [jnp.zeros((rows, COLS), F32) for _ in range(2)]
    left = [jnp.zeros((rows, COLS), F32) for _ in range(2)]
    for k, value in enumerate(strips):
        array, half, pair = slot(k)
        mask = slot_mask(k, rows)
        right[array] = jnp.where(mask, turn(value, 2 * pair + 64 * half, 1), right[array])
        left[array] = jnp.where(mask, turn(value, 2 * pair - 2 + 64 * half, 1), left[array])
    return right, left


def first_kernel(e, h, ae, ah, eps, cur, f, ya, yb, sems):
    copies = []
    for k in range(COMPS):
        source = (e, h, ae, ah)[k // 3].at[k % 3] if k < 12 else (eps, cur)[k - 12]
        copies.append(pltpu.make_async_copy(source, f.at[k, 2 : PLANES + 2, 0:ROWS], sems.at[k]))
    for copy in copies:
        copy.start()
    even = parity("gy")
    sub = subs()
    for k in range(COMPS):
        copies[k].wait()
        for half in range(2):
            up = jnp.zeros((8, COLS), F32)
            down = jnp.zeros((8, COLS), F32)
            for j in range(4):
                idx = 4 * half + j + 2
                mask = (sub >> 1) == j
                up = jnp.where(mask, turn(f[k, idx, 24:32], 2 * j - 6, 0), up)
                down = jnp.where(mask, turn(f[k, idx, 0:8], 2 * j, 0), down)
            at = 8 * (2 * k + half)
            ya[at : at + 8] = jnp.where(even, up, down)
            yb[at : at + 8] = jnp.where(even, down, up)


def strip_kernel(start, pml, f, strips, right_out, left_out, factors, rr, ss, xr, xs):
    of_plane = block_sigma(pml)
    for idx in range(1, PLANES + 3):
        sigma, inside = of_plane(idx - 2)
        rr[idx], ss[idx] = damping(sigma, inside), 0.5 * sigma
    sigma, inside = side_sigma(pml)
    xr[...], xs[...] = damping(sigma, inside), 0.5 * sigma
    for k in range(2):
        phase = jnp.full((8, COLS), lax.rem(start[0] + k + 1, PERIOD), jnp.int32).astype(F32)
        factors[k] = jnp.sin(phase * (2.0 * math.pi / PERIOD))
    values = []
    for k in range(COMPS):
        value = strip([f[k, p + 2, 0:ROWS] for p in range(PLANES)], ROWS)
        strips[k] = value
        values.append(value)
    right, left = face_pack(values, ROWS)
    for a in range(2):
        right_out[a] = right[a]
        left_out[a] = left[a]


def profile(position, extent, thickness):
    distance = jnp.minimum(position, extent - 1 - position)
    depth = jnp.maximum(thickness - distance, 0).astype(F32) / thickness.astype(F32)
    return 0.8 * depth * depth


def magnetic(ex, ey, ez, ex_up, ey_up, hx, hy, hz, r, next_x, next_y, at=(0, 1, 2)):
    cx = (next_y(ez, 2) - ez) - (ey_up - ey)
    cy = (ex_up - ex) - (next_x(ez, 2) - ez)
    cz = (next_x(ey, 1) - ey) - (next_y(ex, 0) - ex)
    return [r * (h + h - 0.5 * c) - h for h, c in ((hx, cx), (hy, cy), (hz, cz))]


def electric(hx, hy, hz, hx_down, hy_down, ex, ey, ez, q, g, drive, prev_x, prev_y):
    cx = (hz - prev_y(hz, 2)) - (hy - hy_down)
    cy = (hx - hx_down) - (hz - prev_x(hz, 2))
    cz = (hy - prev_x(hy, 1)) - (hx - prev_y(hx, 0))
    if drive is not None:
        cz = cz - drive
    return [q * (g * e + c) for e, c in ((ex, cx), (ey, cy), (ez, cz))]


def grid_sizes():
    return PLANES * lax.axis_size("gz"), ROWS * lax.axis_size("gy"), COLS * lax.axis_size("gx")


def row_grid():
    row = subs(TALL)
    at = ROWS * lax.axis_index("gy") + jnp.where(row >= 36, row - TALL, row)
    return at, (at >= 0) & (at < grid_sizes()[1])


def damping(sigma, inside):
    return jnp.where(inside, 1.0 / (1.0 + 0.25 * sigma), 0.0)


def electric_coefficients(r, half_sigma, permittivity):
    twice = 2.0 * jnp.maximum(permittivity, 1.0)
    return jnp.where(r > 0.0, 1.0 / (twice + half_sigma), 0.0), twice - half_sigma


def block_sigma(pml):
    nz, ny, nx = grid_sizes()
    at, row_in = row_grid()
    flat = profile(at, ny, pml[1]) + profile(COLS * lax.axis_index("gx") + lanes(TALL), nx, pml[2])

    def of_plane(p):
        z_at = jnp.full((TALL, COLS), PLANES * lax.axis_index("gz") + p, jnp.int32)
        sigma = profile(z_at[0:8], nz, pml[0])
        sigma = jnp.concatenate([sigma] * (TALL // 8), axis=0) + flat
        return sigma, row_in & (z_at >= 0) & (z_at < nz)

    return of_plane


def side_sigma(pml):
    nz, ny, nx = grid_sizes()
    at, row_in = row_grid()
    lane = lanes(TALL)
    column = lane & 7
    x_at = COLS * lax.axis_index("gx") + jnp.where(column < 4, COLS - 2 + column, column - 6)
    z_at = PLANES * lax.axis_index("gz") + (lane >> 3) - 2
    inside = row_in & (z_at >= 0) & (z_at < nz) & (x_at >= 0) & (x_at < nx)
    return profile(z_at, nz, pml[0]) + profile(at, ny, pml[1]) + profile(x_at, nx, pml[2]), inside


def up_row(value, _):
    return pltpu.roll(value, TALL - 1, 0)


def down_row(value, _):
    return pltpu.roll(value, 1, 0)


def side_magnetic(e, h, r):
    return magnetic(
        *e, pltpu.roll(e[0], 120, 1), pltpu.roll(e[1], 120, 1), *h, r, lambda v, _: pltpu.roll(v, 127, 1), up_row
    )


def side_electric(h, e, q, g, drive):
    return electric(
        *h, pltpu.roll(h[0], 8, 1), pltpu.roll(h[1], 8, 1), *e, q, g, drive, lambda v, _: pltpu.roll(v, 1, 1), down_row
    )


def face_blocks(faces, rows, values):
    blocks = [values[item][0:ROWS] for item in faces]
    sub = subs()
    for i in range(0, len(rows), 4):
        tile = jnp.zeros((8, COLS), F32)
        for j, (kind, k, first) in enumerate(rows[i : i + 4]):
            tile = jnp.where((sub >> 1) == j, turn(values[kind, k][ROWS:TALL], 2 * j - first, 0), tile)
        blocks.append(tile)
    whole = jnp.concatenate(blocks, axis=0)
    fill = FACE_ROWS - whole.shape[0]
    return jnp.concatenate([whole, jnp.zeros((fill, COLS), F32)], axis=0) if fill else whole


def face_in(ref, faces, rows, keep):
    got = {}
    for i, item in enumerate(faces):
        got[item] = [ref[ROWS * i : ROWS * i + ROWS] * keep, jnp.zeros((8, COLS), F32)]
    sub = subs()
    for i, (kind, k, first) in enumerate(rows):
        at = ROWS * len(faces) + 8 * (i // 4)
        tile = turn(ref[at : at + 8], first - 2 * (i % 4), 0) * keep
        mask = (sub == first) | (sub == (first + 1) % 8)
        got[kind, k][1] = jnp.where(mask, tile, got[kind, k][1])
    return {item: jnp.concatenate(parts, axis=0) for item, parts in got.items()}


def second_kernel(ya, yb, right_in, left_in, tiles, strips, xa, xb):
    index = lax.axis_index("gy")
    even = parity("gy")
    has_after = (index < lax.axis_size("gy") - 1).astype(F32)
    has_before = (index > 0).astype(F32)
    sub = subs()
    values = []
    for k in range(COMPS):
        planes = []
        for half in range(2):
            at = 8 * (2 * k + half)
            got_a, got_b = ya[at : at + 8], yb[at : at + 8]
            after = jnp.where(even, got_a, got_b) * has_after
            before = jnp.where(even, got_b, got_a) * has_before
            for j in range(4):
                tile = jnp.where(sub < 2, turn(after, -2 * j, 0), jnp.where(sub >= 6, turn(before, 6 - 2 * j, 0), 0.0))
                tiles[k, 4 * half + j] = tile
                planes.append(tile)
        value = strip(planes, 8)
        strips[k] = value
        values.append(value)
    right, left = face_pack(values, 8)
    even = parity("gx")
    for a in range(2):
        xa[a, 0:ROWS] = jnp.where(even, right_in[a], left_in[a])
        xb[a, 0:ROWS] = jnp.where(even, left_in[a], right_in[a])
        xa[a, ROWS:TALL] = jnp.where(even, right[a], left[a])
        xb[a, ROWS:TALL] = jnp.where(even, left[a], right[a])


def face_kernel(f, tiles, factors, rr, ss, za, zb):
    def field(k, p):
        return jnp.concatenate([f[k, p + 2, 0:ROWS], tiles[k, p]], axis=0)

    zero = jnp.zeros((TALL, COLS), F32)
    drive = jnp.concatenate([factors[0]] * (TALL // 8), axis=0) * field(13, 7)

    def next_x(value, _):
        return pltpu.roll(value, COLS - 1, 1)

    def prev_x(value, _):
        return pltpu.roll(value, 1, 1)

    def half_step(base, p):
        up = [field(base + c, p + 1) for c in range(2)] if p < 7 else [zero, zero]
        return magnetic(
            *[field(base + c, p) for c in range(3)], *up, *[field(base + 3 + c, p) for c in range(3)],
            rr[p + 2], next_x, up_row,
        )

    sent = []
    for p, faces, rows in ((7, UP_FACES, UP_ROWS), (0, DOWN_FACES, DOWN_ROWS)):
        values = {("f", k): field(k, p) for k in (0, 1, 6, 7, 12)}
        q, g = electric_coefficients(rr[p + 2], ss[p + 2], values["f", 12])
        for base in (0, 6):
            h = half_step(base, p)
            down = half_step(base, 6)[0:2] if p == 7 else [zero, zero]
            e = electric(
                *h, *down, *[field(base + c, p) for c in range(3)], q, g, drive if p == 7 and base == 0 else None, prev_x, down_row
            )
            for c in range(3):
                values["h", base + 3 + c] = h[c]
                values["e", base + c] = e[c]
        sent.append(face_blocks(faces, rows, values))
    even = parity("gz")
    za[...] = jnp.where(even, sent[0], sent[1])
    zb[...] = jnp.where(even, sent[1], sent[0])


def third_kernel(xa, xb, strips, strips_rim, factors, xr, xs, sides, rim_a, rim_b):
    index = lax.axis_index("gx")
    even = parity("gx")
    has_after = (index < lax.axis_size("gx") - 1).astype(F32)
    has_before = (index > 0).astype(F32)
    lane = lanes(TALL)
    pair_of = (lane & 7) >> 1
    own = (lane >= 16) & (lane < 80)
    after = [jnp.where(even, xa[a], xb[a]) * has_after for a in range(2)]
    before = [jnp.where(even, xb[a], xa[a]) * has_before for a in range(2)]
    side = []
    for k in range(COMPS):
        array, half, pair = slot(k)
        mine = jnp.concatenate([strips[k], strips_rim[k]], axis=0)
        value = jnp.where(pair_of == 0, mine, turn(mine, 4, 1))
        value = jnp.where(pair_of == 1, turn(after[array], 2 - 2 * pair - 64 * half, 1), value)
        value = jnp.where(pair_of == 2, turn(before[array], 4 - 2 * pair - 64 * half, 1), value)
        value = jnp.where(own, value, 0.0)
        sides[k] = value
        side.append(value)
    r = xr[...]
    q, g = electric_coefficients(r, xs[...], side[12])
    drive = jnp.concatenate([factors[0]] * (TALL // 8), axis=0) * side[13]
    values = {("f", k): side[k] for k in range(COMPS)}
    for base in (0, 6):
        e = side[base : base + 3]
        h = [jnp.where(own, v, 0.0) for v in side_magnetic(e, side[base + 3 : base + 6], r)]
        e = side_electric(h, e, q, g, drive if base == 0 else None)
        for c in range(3):
            values["h", base + 3 + c] = h[c]
            values["e", base + c] = e[c]
    sent = []
    for items, p in ((UP_SIDES, 7), (DOWN_SIDES, 0)):
        packed = jnp.zeros((TALL, COLS), F32)
        for i, item in enumerate(items):
            packed = jnp.where((lane >> 3) == i, turn(values[item], 8 * i - 8 * (p + 2), 1), packed)
        sent.append(packed)
    even = parity("gz")
    rim_a[...] = jnp.where(even, sent[0], sent[1])
    rim_b[...] = jnp.where(even, sent[1], sent[0])


def home(layer):
    mine = lax.axis_index("gz") >> 1
    return (((layer >> 2) ^ mine) << 2) + (layer & 3)


def run_steps(side_loss, factors, f, one, rr, qq, gg, xf, xone, planes, put_field, put_density, halo=None):
    xr = side_loss[0][...]
    xq, xg = electric_coefficients(xr, side_loss[1][...], xf[12])
    factors = [jnp.concatenate([factors[k]] * (TALL // 8), axis=0) for k in range(2)]
    lane = lanes(TALL)
    first_lane, last_lane = lane == 0, lane == COLS - 1

    def side_half(e_ref, e_base, h_base):
        new = side_magnetic([e_ref[e_base + c] for c in range(3)], [xf[h_base + c] for c in range(3)], xr)
        for c in range(3):
            xf[h_base + c] = new[c]

    def side_full(e_base, h_base, out_base, factor):
        drive = None if factor is None else xf[13] * factor
        new = side_electric(
            [xf[h_base + c] for c in range(3)], [xf[e_base + c] for c in range(3)], xq, xg, drive
        )
        for c in range(3):
            xone[out_base + c] = new[c]

    def plane_magnetic(idx, e_ref, x_ref, e_base, h_base):
        def next_x(value, c):
            halo = pltpu.roll(x_ref[e_base + c], 125 - 8 * idx, 1)
            return jnp.where(last_lane, halo, pltpu.roll(value, COLS - 1, 1))

        new = magnetic(
            *[e_ref[e_base + c, idx] for c in range(3)], e_ref[e_base, idx + 1], e_ref[e_base + 1, idx + 1],
            *[f[h_base + c, idx] for c in range(3)], rr[idx], next_x, up_row,
        )
        for c in range(3):
            f[h_base + c, idx] = new[c]

    def plane_electric(idx, e_ref, e_base, h_base, factor):
        def prev_x(value, c):
            halo = pltpu.roll(xf[h_base + c], 123 - 8 * idx, 1)
            return jnp.where(first_lane, halo, pltpu.roll(value, 1, 1))

        drive = None if factor is None else f[13, idx] * factor
        return electric(
            *[f[h_base + c, idx] for c in range(3)], f[h_base, idx - 1], f[h_base + 1, idx - 1],
            *[e_ref[e_base + c, idx] for c in range(3)], qq[idx], gg[idx], drive, prev_x, down_row,
        )

    def over(which, body):
        for idx in planes[which]:
            body(idx)

    def body(idx):
        plane_magnetic(idx, f, xf, 0, 3)
        plane_magnetic(idx, f, xf, 6, 9)

    over(0, body)
    side_half(xf, 0, 3)
    side_half(xf, 6, 9)
    if halo is not None:
        halo(xr, xq, sides=False)

    def body(idx):
        for base, out, factor in ((0, 0, factors[0]), (6, 3, None)):
            new = plane_electric(idx, f, base, base + 3, factor)
            for c in range(3):
                one[out + c, idx] = new[c]

    over(1, body)
    side_full(0, 3, 0, factors[0])
    side_full(6, 9, 3, None)
    if halo is not None:
        halo(xr, xq, sides=True)

    def body(idx):
        plane_magnetic(idx, one, xone, 0, 3)
        plane_magnetic(idx, one, xone, 3, 9)

    over(2, body)
    side_half(xone, 0, 3)
    side_half(xone, 3, 9)

    def body(idx):
        two = plane_electric(idx, one, 0, 3, factors[1])
        zero = plane_electric(idx, one, 3, 9, None)
        density = jnp.zeros((ROWS, COLS), F32)
        for c in range(3):
            last = zero[c][0:ROWS]
            put_field(c, idx, last, f[9 + c, idx, 0:ROWS])
            density = density + f[c, idx, 0:ROWS] * last + one[c, idx, 0:ROWS] * one[3 + c, idx, 0:ROWS]
            density = density + two[c][0:ROWS] * f[6 + c, idx, 0:ROWS]
        put_density(idx, density)

    over(3, body)


def inner_kernel(layer, factors, rr, ss, xr, xs, own, tiles, sides, f, one, qq, gg, sums, e_mid, h_mid, homes, xf, xone):
    del own
    for k in range(COMPS):
        for p in range(PLANES):
            f[k, p + 2, ROWS:TALL] = tiles[k, p]
        xf[k] = sides[k]

    def coefficients(i, carry):
        qq[i + 2], gg[i + 2] = electric_coefficients(rr[i + 2], ss[i + 2], f[12, i + 2])
        return carry

    lax.fori_loop(0, PLANES, coefficients, 0)
    sums[...] = jnp.zeros((LAYERS, ROWS, COLS), F32)
    for i, p in enumerate((0, 1, 6, 7)):
        homes[i] = jnp.full((8, COLS), home(layer[p]), jnp.int32).astype(F32)

    def put(c, idx, e_new, h_new):
        e_mid[c, idx - 4] = e_new
        h_mid[c, idx - 4] = h_new

    def put_density(idx, density):
        sums[home(layer[idx - 2])] = density

    planes = [range(2, 9), range(3, 9), range(3, 8), range(4, 8)]
    run_steps((xr, xs), factors, f, one, rr, qq, gg, xf, xone, planes, put, put_density)


def outer_kernel(
    factors, rr, ss, xr, xs, f_in, one_in, qq_in, gg_in, sums, homes, za, zb, sides, rim_a, rim_b,
    f, one, qq, gg, e_rest, h_rest, zeroth, first, second, third, xf, xone,
):
    del f_in, one_in, qq_in, gg_in
    index = lax.axis_index("gz")
    has_above = (index < lax.axis_size("gz") - 1).astype(F32)
    has_below = (index > 0).astype(F32)
    lane = lanes(TALL)
    low, top = 1, PLANES + 2
    for k in range(COMPS):
        xf[k] = sides[k]
    got = {}
    even = parity("gz")
    for pick, faces, rows, items, idx, keep in (
        (lambda a, b: jnp.where(even, b, a), UP_FACES, UP_ROWS, UP_SIDES, low, has_below),
        (lambda a, b: jnp.where(even, a, b), DOWN_FACES, DOWN_ROWS, DOWN_SIDES, top, has_above),
    ):
        ref = pick(za[...], zb[...])
        packed = pick(rim_a[...], rim_b[...]) * keep
        planes = face_in(ref, faces, rows, keep)
        for i, (kind, k) in enumerate(items):
            if kind != "f":
                at_last, at_first = turn(packed, 126 - 8 * i, 1), turn(packed, -6 - 8 * i, 1)
                fixed = jnp.where(lane == COLS - 1, at_last, planes[kind, k])
                planes[kind, k] = jnp.where(lane == 0, at_first, fixed) if kind == "e" else fixed
            got[kind, k, idx] = (planes[kind, k], turn(packed, 8 * idx - 8 * i, 1))
        for k in (0, 1, 6, 7, 12):
            if ("f", k) in planes:
                f[k, idx] = planes["f", k]
                xf[k] = jnp.where((lane >> 3) == idx, got["f", k, idx][1], xf[k])
    for idx in (low, top):
        qq[idx], gg[idx] = electric_coefficients(rr[idx], ss[idx], f[12, idx])

    def add_z(q, x, y, prev_x):
        return q * ((y - prev_x(y)) - (x - down_row(x, 0)))

    def halo(xr, xq, sides):
        q, q_top, r_half = qq[low], qq[top], 0.5 * rr[low]
        for base, out in ((0, 0), (6, 3)):
            x_side = 0.5 * xr * pltpu.roll(xf[base + 1], 120, 1)
            y_side = -0.5 * xr * pltpu.roll(xf[base], 120, 1)
            if sides:
                added = got["e", base + 2, low][1] + add_z(xq, x_side, y_side, lambda v: pltpu.roll(v, 1, 1))
                xone[out + 2] = jnp.where((lane >> 3) == low, added, xone[out + 2])
                added = got["e", base, top][1] + xq * pltpu.roll(xf[base + 4], 8, 1)
                xone[out] = jnp.where((lane >> 3) == top, added, xone[out])
                added = got["e", base + 1, top][1] - xq * pltpu.roll(xf[base + 3], 8, 1)
                xone[out + 1] = jnp.where((lane >> 3) == top, added, xone[out + 1])
                continue
            x, y = r_half * f[base + 1, 2], -r_half * f[base, 2]

            def prev_x(value):
                return jnp.where(lane == 0, pltpu.roll(y_side, 123 - 8 * low, 1), pltpu.roll(value, 1, 1))

            for k, term, side_term in ((base + 3, x, x_side), (base + 4, y, y_side)):
                plane, side = got["h", k, low]
                f[k, low] = plane + term
                xf[k] = jnp.where((lane >> 3) == low, side + side_term, xf[k])
            f[base + 5, low] = jnp.zeros((TALL, COLS), F32)
            one[out, low] = got["e", base, low][0] - q * y
            one[out + 1, low] = got["e", base + 1, low][0] + q * x
            one[out + 2, low] = got["e", base + 2, low][0] + add_z(q, x, y, prev_x)
            one[out, top] = got["e", base, top][0] + q_top * f[base + 4, top - 1]
            one[out + 1, top] = got["e", base + 1, top][0] - q_top * f[base + 3, top - 1]

    def put(c, idx, e_new, h_new):
        at = idx - 2 if idx < 4 else idx - 6
        e_rest[c, at] = e_new
        h_rest[c, at] = h_new

    late = []

    def put_density(idx, density):
        late.append(density)

    planes = [(9,), (2, 9), (1, 2, 8, 9), (2, 3, 8, 9)]
    run_steps((xr, xs), factors, f, one, rr, qq, gg, xf, xone, planes, put, put_density, halo)
    for i, out in enumerate((zeroth, first, second, third)):
        for j in range(4):
            total = sums[4 * i + j]
            for at, density in enumerate(late):
                here = homes[at] == float(4 * i + j)
                total = total + jnp.where(jnp.concatenate([here] * (ROWS // 8), axis=0), density, 0.0)
            out[j] = total


def store_kernel(e_mid, h_mid, e_rest, h_rest, e_out, h_out, sems):
    copies = []
    for mid, rest, out in ((e_mid, e_rest, e_out), (h_mid, h_rest, h_out)):
        for source, at, first, count in ((mid, 0, 2, 4), (rest, 0, 0, 2), (rest, 2, 6, 2)):
            copies.append((source.at[:, at : at + count], out.at[:, first : first + count]))
    copies = [pltpu.make_async_copy(a, b, sems.at[i]) for i, (a, b) in enumerate(copies)]
    for copy in copies:
        copy.start()
    for copy in copies:
        copy.wait()


def fold_kernel(sums, first, second, third, kept, sent):
    upper = lax.rem(lax.axis_index("gz"), 2) == 1
    for i in range(2):
        low, high = (sums[j] + first[j] + second[j] + third[j] for j in (i, i + 2))
        kept[i] = jnp.where(upper, high, low)
        sent[i] = jnp.where(upper, low, high)


def sum_kernel(kept, got, out):
    out[...] = kept[...] + got[...]


def call(kernel, outs, scratch=(), scalars=0, far=0, aliases=None, out_space=pltpu.VMEM, flops=1000000):
    def run(*args):
        near = len(args) - scalars - far
        specs = [pl.BlockSpec(memory_space=pltpu.SMEM)] * scalars
        specs += [pl.BlockSpec(memory_space=pltpu.VMEM)] * near + [pl.BlockSpec(memory_space=pl.ANY)] * far
        size = sum(4 * math.prod(s) for s in outs) + sum(4 * math.prod(a.shape) for a in args)
        return pl.pallas_call(
            kernel,
            out_shape=[jax.ShapeDtypeStruct(s, F32) for s in outs],
            in_specs=specs,
            out_specs=[pl.BlockSpec(memory_space=out_space)] * len(outs),
            scratch_shapes=[pltpu.VMEM(s, F32) if isinstance(s, tuple) else s for s in scratch],
            input_output_aliases=aliases or {},
            compiler_params=pltpu.CompilerParams(vmem_limit_bytes=24 * 2**20),
            cost_estimate=pl.CostEstimate(flops=flops, bytes_accessed=size, transcendentals=0),
        )(*args)

    return run


def swaps(axis, first):
    count = lax.axis_size(axis)
    pairs = [(i, (i + 1) % count) for i in range(first, count, 2)]
    return pairs + [(b, a) for a, b in pairs]


def across(axis, bits):
    return [(i, i ^ bits) for i in range(lax.axis_size(axis))]


def inner_swaps():
    count, width = lax.axis_size("gy"), lax.axis_size("gx")
    pairs = []
    for j in range(width):
        pairs += [(i * width + j, (i + 1) * width + j) for i in range(1, count - 1, 2)]
        if j % 2 == 0:
            pairs += [(i * width + j, i * width + j + 1) for i in (0, count - 1)]
    return pairs + [(b, a) for a, b in pairs]


def local(e_start, h_start, adjoint_e, adjoint_h, permittivity, current, layer_of_cell, pml_cells, start_step):
    raw = (e_start, h_start, adjoint_e, adjoint_h, permittivity, current)
    raw = [pltpu.with_memory_space_constraint(a, pltpu.HBM) for a in raw]
    block, deep, tall = (ROWS, COLS), (DEEP, TALL, COLS), (TALL, COLS)
    f, ya, yb = call(
        first_kernel, [(COMPS,) + deep, (16 * COMPS, COLS), (16 * COMPS, COLS)], [pltpu.SemaphoreType.DMA((COMPS,))], far=6
    )(*raw)
    yb = lax.ppermute(yb, ("gy", "gx"), inner_swaps())
    ya = lax.ppermute(ya, "gy", swaps("gy", 0))
    strips, right, left, *loss = call(
        strip_kernel, [(COMPS,) + block, (2,) + block, (2,) + block, (2, 8, COLS), deep, deep, tall, tall], scalars=2
    )(start_step, pml_cells, f)
    side = (2,) + tall
    tiles, strips_rim, xa, xb = call(second_kernel, [(COMPS, PLANES, 8, COLS), (COMPS, 8, COLS), side, side])(ya, yb, right, left)
    za, zb = call(face_kernel, [(FACE_ROWS, COLS)] * 2)(f, tiles, *loss[:3])
    za = lax.ppermute(za, "gz", swaps("gz", 0))
    zb = lax.ppermute(zb, "gz", swaps("gz", 1))
    xa = lax.ppermute(xa, "gx", swaps("gx", 0))
    xb = lax.ppermute(xb, "gx", swaps("gx", 1))
    sides, rim_a, rim_b = call(third_kernel, [(COMPS,) + tall, tall, tall])(
        xa, xb, strips, strips_rim, loss[0], *loss[3:]
    )
    rim_a = lax.ppermute(rim_a, "gz", swaps("gz", 0))
    rim_b = lax.ppermute(rim_b, "gz", swaps("gz", 1))
    state = [(COMPS,) + deep, (6,) + deep, deep, deep]
    mid, out = (3, PLANES // 2) + block, (3, PLANES) + block
    side = [(COMPS,) + tall, (6,) + tall]
    *held, sums, e_mid, h_mid, homes = call(inner_kernel, state + [(LAYERS,) + block, mid, mid, (4, 8, COLS)], side, scalars=1, aliases={6: 0}, flops=10**11)(
        layer_of_cell, *loss, f, tiles, sides
    )
    quarter, pair = (LAYERS // 4,) + block, (2,) + block
    *_, e_rest, h_rest, zeroth, first, second, third = call(
        outer_kernel, state + [mid, mid] + [quarter] * 4, side, aliases={5 + i: i for i in range(len(state))}
    )(*loss, *held, sums, homes, za, zb, sides, rim_a, rim_b)
    e_out, h_out = call(store_kernel, [out, out], [pltpu.SemaphoreType.DMA((6,))], out_space=pltpu.HBM)(e_mid, h_mid, e_rest, h_rest)
    first, second, third = (lax.ppermute(v, "gz", across("gz", m)) for v, m in ((first, 2), (second, 4), (third, 6)))
    kept, sent = call(fold_kernel, [pair, pair])(zeroth, first, second, third)
    (gradient,) = call(sum_kernel, [pair])(kept, lax.ppermute(sent, "gz", across("gz", 1)))
    return gradient, e_out, h_out


def solution(mesh):
    fields = P(None, "gz", "gy", "gx")
    cells = P("gz", "gy", "gx")
    return jax.shard_map(
        local,
        mesh=mesh,
        in_specs=(fields, fields, fields, fields, cells, cells, P("gz"), P(), P()),
        out_specs=(cells, fields, fields),
        check_vma=False,
    )
```

```python
import functools
import math

import jax
import jax.numpy as jnp
from jax import lax
from jax.experimental import pallas as pl
from jax.experimental.pallas import tpu as pltpu
from jax.sharding import PartitionSpec as P

F32 = jnp.float32
PLANES, ROWS, COLS = 8, 32, 128
DEEP, TALL = PLANES + 4, ROWS + 8
LAYERS = 16
PERIOD = 64
COMPS = 14
UP_FACES = [("h", k) for k in (3, 4, 9, 10)] + [("e", k) for k in (0, 1, 2, 6, 7, 8)] + [("f", 12)]
DOWN_FACES = [("f", k) for k in (0, 1, 6, 7, 12)] + [("e", k) for k in (0, 1, 6, 7)]
UP_ROWS = [("h", k, 7) for k in (3, 4, 9, 10)] + [("e", 2, 7), ("e", 8, 7), ("f", 12, 7)]
DOWN_ROWS = [("f", k, 7) for k in (0, 1, 6, 7, 12)] + [("e", 1, 7), ("e", 7, 7), ("f", 1, 6), ("f", 7, 6)]
UP_SIDES, DOWN_SIDES = UP_FACES, DOWN_FACES


def face_rows(faces, rows):
    return ROWS * len(faces) + 8 * ((len(rows) + 3) // 4)


FACE_ROWS = max(face_rows(UP_FACES, UP_ROWS), face_rows(DOWN_FACES, DOWN_ROWS))


def lanes(rows=8):
    return lax.broadcasted_iota(jnp.int32, (rows, COLS), 1)


def subs(rows=8):
    return lax.broadcasted_iota(jnp.int32, (rows, COLS), 0)


def turn(value, shift, axis):
    shift = shift % value.shape[axis]
    return value if shift == 0 else pltpu.roll(value, shift, axis)


def slot(k):
    return k // 8, (k % 8) // 4, k % 4


def slot_mask(k, rows):
    _, half, pair = slot(k)
    lane = lanes(rows)
    inside = ((lane - 16 - 64 * half) & 127) < 64
    return inside & (((lane & 7) >> 1) == pair)


def window(p, rows):
    lane = lanes(rows)
    return (lane >= 8 * (p + 2)) & (lane < 8 * (p + 2) + 4)


def parity(axis):
    return lax.rem(lax.axis_index(axis), 2) == 0


def strip(planes, rows):
    out = jnp.zeros((rows, COLS), F32)
    for p, plane in enumerate(planes):
        out = jnp.where(window(p, rows), turn(plane, 8 * (p + 2) + 2, 1), out)
    return out


def face_pack(strips, rows):
    right = [jnp.zeros((rows, COLS), F32) for _ in range(2)]
    left = [jnp.zeros((rows, COLS), F32) for _ in range(2)]
    for k, value in enumerate(strips):
        array, half, pair = slot(k)
        mask = slot_mask(k, rows)
        right[array] = jnp.where(mask, turn(value, 2 * pair + 64 * half, 1), right[array])
        left[array] = jnp.where(mask, turn(value, 2 * pair - 2 + 64 * half, 1), left[array])
    return right, left


def first_kernel(e, h, ae, ah, eps, cur, f, ya, yb, sems):
    copies = []
    for k in range(COMPS):
        source = (e, h, ae, ah)[k // 3].at[k % 3] if k < 12 else (eps, cur)[k - 12]
        copies.append(pltpu.make_async_copy(source, f.at[k, 2 : PLANES + 2, 0:ROWS], sems.at[k]))
    for copy in copies:
        copy.start()
    even = parity("gy")
    sub = subs()
    for k in range(COMPS):
        copies[k].wait()
        for half in range(2):
            up = jnp.zeros((8, COLS), F32)
            down = jnp.zeros((8, COLS), F32)
            for j in range(4):
                idx = 4 * half + j + 2
                mask = (sub >> 1) == j
                up = jnp.where(mask, turn(f[k, idx, 24:32], 2 * j - 6, 0), up)
                down = jnp.where(mask, turn(f[k, idx, 0:8], 2 * j, 0), down)
            at = 8 * (2 * k + half)
            ya[at : at + 8] = jnp.where(even, up, down)
            yb[at : at + 8] = jnp.where(even, down, up)


def strip_kernel(start, pml, f, strips, right_out, left_out, factors, rr, ss, xr, xs):
    of_plane = block_sigma(pml)
    for idx in range(1, PLANES + 3):
        sigma, inside = of_plane(idx - 2)
        rr[idx], ss[idx] = damping(sigma, inside), 0.5 * sigma
    sigma, inside = side_sigma(pml)
    xr[...], xs[...] = damping(sigma, inside), 0.5 * sigma
    for k in range(2):
        phase = jnp.full((8, COLS), lax.rem(start[0] + k + 1, PERIOD), jnp.int32).astype(F32)
        factors[k] = jnp.sin(phase * (2.0 * math.pi / PERIOD))
    values = []
    for k in range(COMPS):
        value = strip([f[k, p + 2, 0:ROWS] for p in range(PLANES)], ROWS)
        strips[k] = value
        values.append(value)
    right, left = face_pack(values, ROWS)
    for a in range(2):
        right_out[a] = right[a]
        left_out[a] = left[a]


def profile(position, extent, thickness):
    distance = jnp.minimum(position, extent - 1 - position)
    depth = jnp.maximum(thickness - distance, 0).astype(F32) / thickness.astype(F32)
    return 0.8 * depth * depth


def magnetic(ex, ey, ez, ex_up, ey_up, hx, hy, hz, r, next_x, next_y, at=(0, 1, 2)):
    cx = (next_y(ez, 2) - ez) - (ey_up - ey)
    cy = (ex_up - ex) - (next_x(ez, 2) - ez)
    cz = (next_x(ey, 1) - ey) - (next_y(ex, 0) - ex)
    return [r * (h + h - 0.5 * c) - h for h, c in ((hx, cx), (hy, cy), (hz, cz))]


def electric(hx, hy, hz, hx_down, hy_down, ex, ey, ez, q, g, drive, prev_x, prev_y):
    cx = (hz - prev_y(hz, 2)) - (hy - hy_down)
    cy = (hx - hx_down) - (hz - prev_x(hz, 2))
    cz = (hy - prev_x(hy, 1)) - (hx - prev_y(hx, 0))
    if drive is not None:
        cz = cz - drive
    return [q * (g * e + c) for e, c in ((ex, cx), (ey, cy), (ez, cz))]


def grid_sizes():
    return PLANES * lax.axis_size("gz"), ROWS * lax.axis_size("gy"), COLS * lax.axis_size("gx")


def row_grid():
    row = subs(TALL)
    at = ROWS * lax.axis_index("gy") + jnp.where(row >= 36, row - TALL, row)
    return at, (at >= 0) & (at < grid_sizes()[1])


def damping(sigma, inside):
    return jnp.where(inside, 1.0 / (1.0 + 0.25 * sigma), 0.0)


def electric_coefficients(r, half_sigma, permittivity):
    twice = 2.0 * jnp.maximum(permittivity, 1.0)
    return jnp.where(r > 0.0, 1.0 / (twice + half_sigma), 0.0), twice - half_sigma


def block_sigma(pml):
    nz, ny, nx = grid_sizes()
    at, row_in = row_grid()
    flat = profile(at, ny, pml[1]) + profile(COLS * lax.axis_index("gx") + lanes(TALL), nx, pml[2])

    def of_plane(p):
        z_at = jnp.full((TALL, COLS), PLANES * lax.axis_index("gz") + p, jnp.int32)
        sigma = profile(z_at[0:8], nz, pml[0])
        sigma = jnp.concatenate([sigma] * (TALL // 8), axis=0) + flat
        return sigma, row_in & (z_at >= 0) & (z_at < nz)

    return of_plane


def side_sigma(pml):
    nz, ny, nx = grid_sizes()
    at, row_in = row_grid()
    lane = lanes(TALL)
    column = lane & 7
    x_at = COLS * lax.axis_index("gx") + jnp.where(column < 4, COLS - 2 + column, column - 6)
    z_at = PLANES * lax.axis_index("gz") + (lane >> 3) - 2
    inside = row_in & (z_at >= 0) & (z_at < nz) & (x_at >= 0) & (x_at < nx)
    return profile(z_at, nz, pml[0]) + profile(at, ny, pml[1]) + profile(x_at, nx, pml[2]), inside


def up_row(value, _):
    return pltpu.roll(value, TALL - 1, 0)


def down_row(value, _):
    return pltpu.roll(value, 1, 0)


def side_magnetic(e, h, r):
    return magnetic(
        *e, pltpu.roll(e[0], 120, 1), pltpu.roll(e[1], 120, 1), *h, r, lambda v, _: pltpu.roll(v, 127, 1), up_row
    )


def side_electric(h, e, q, g, drive):
    return electric(
        *h, pltpu.roll(h[0], 8, 1), pltpu.roll(h[1], 8, 1), *e, q, g, drive, lambda v, _: pltpu.roll(v, 1, 1), down_row
    )


def face_blocks(faces, rows, values):
    blocks = [values[item][0:ROWS] for item in faces]
    sub = subs()
    for i in range(0, len(rows), 4):
        tile = jnp.zeros((8, COLS), F32)
        for j, (kind, k, first) in enumerate(rows[i : i + 4]):
            tile = jnp.where((sub >> 1) == j, turn(values[kind, k][ROWS:TALL], 2 * j - first, 0), tile)
        blocks.append(tile)
    whole = jnp.concatenate(blocks, axis=0)
    fill = FACE_ROWS - whole.shape[0]
    return jnp.concatenate([whole, jnp.zeros((fill, COLS), F32)], axis=0) if fill else whole


def face_in(ref, faces, rows, keep):
    got = {}
    for i, item in enumerate(faces):
        got[item] = [ref[ROWS * i : ROWS * i + ROWS] * keep, jnp.zeros((8, COLS), F32)]
    sub = subs()
    for i, (kind, k, first) in enumerate(rows):
        at = ROWS * len(faces) + 8 * (i // 4)
        tile = turn(ref[at : at + 8], first - 2 * (i % 4), 0) * keep
        mask = (sub == first) | (sub == (first + 1) % 8)
        got[kind, k][1] = jnp.where(mask, tile, got[kind, k][1])
    return {item: jnp.concatenate(parts, axis=0) for item, parts in got.items()}


def second_kernel(yb, ya, right_in, left_in, tiles, strips, xa, xb):
    index = lax.axis_index("gy")
    even = parity("gy")
    has_after = (index < lax.axis_size("gy") - 1).astype(F32)
    has_before = (index > 0).astype(F32)
    sub = subs()
    values = []
    for k in range(COMPS):
        planes = []
        for half in range(2):
            at = 8 * (2 * k + half)
            got_a, got_b = ya[at : at + 8], yb[at : at + 8]
            after = jnp.where(even, got_a, got_b) * has_after
            before = jnp.where(even, got_b, got_a) * has_before
            for j in range(4):
                tile = jnp.where(sub < 2, turn(after, -2 * j, 0), jnp.where(sub >= 6, turn(before, 6 - 2 * j, 0), 0.0))
                tiles[k, 4 * half + j] = tile
                planes.append(tile)
        value = strip(planes, 8)
        strips[k] = value
        values.append(value)
    right, left = face_pack(values, 8)
    even = parity("gx")
    for a in range(2):
        xa[a, 0:ROWS] = jnp.where(even, right_in[a], left_in[a])
        xb[a, 0:ROWS] = jnp.where(even, left_in[a], right_in[a])
        xa[a, ROWS:TALL] = jnp.where(even, right[a], left[a])
        xb[a, ROWS:TALL] = jnp.where(even, left[a], right[a])


def face_kernel(f, tiles, factors, rr, ss, za, zb):
    def field(k, p):
        return jnp.concatenate([f[k, p + 2, 0:ROWS], tiles[k, p]], axis=0)

    zero = jnp.zeros((TALL, COLS), F32)
    drive = jnp.concatenate([factors[0]] * (TALL // 8), axis=0) * field(13, 7)

    def next_x(value, _):
        return pltpu.roll(value, COLS - 1, 1)

    def prev_x(value, _):
        return pltpu.roll(value, 1, 1)

    def half_step(base, p):
        up = [field(base + c, p + 1) for c in range(2)] if p < 7 else [zero, zero]
        return magnetic(
            *[field(base + c, p) for c in range(3)], *up, *[field(base + 3 + c, p) for c in range(3)],
            rr[p + 2], next_x, up_row,
        )

    sent = []
    for p, faces, rows in ((7, UP_FACES, UP_ROWS), (0, DOWN_FACES, DOWN_ROWS)):
        values = {("f", k): field(k, p) for k in (0, 1, 6, 7, 12)}
        q, g = electric_coefficients(rr[p + 2], ss[p + 2], values["f", 12])
        for base in (0, 6):
            h = half_step(base, p)
            down = half_step(base, 6)[0:2] if p == 7 else [zero, zero]
            e = electric(
                *h, *down, *[field(base + c, p) for c in range(3)], q, g, drive if p == 7 and base == 0 else None, prev_x, down_row
            )
            for c in range(3):
                values["h", base + 3 + c] = h[c]
                values["e", base + c] = e[c]
        sent.append(face_blocks(faces, rows, values))
    even = parity("gz")
    za[...] = jnp.where(even, sent[0], sent[1])
    zb[...] = jnp.where(even, sent[1], sent[0])


def third_kernel(xa, xb, strips, strips_rim, factors, xr, xs, sides, rim_a, rim_b):
    index = lax.axis_index("gx")
    even = parity("gx")
    has_after = (index < lax.axis_size("gx") - 1).astype(F32)
    has_before = (index > 0).astype(F32)
    lane = lanes(TALL)
    pair_of = (lane & 7) >> 1
    own = (lane >= 16) & (lane < 80)
    after = [jnp.where(even, xa[a], xb[a]) * has_after for a in range(2)]
    before = [jnp.where(even, xb[a], xa[a]) * has_before for a in range(2)]
    side = []
    for k in range(COMPS):
        array, half, pair = slot(k)
        mine = jnp.concatenate([strips[k], strips_rim[k]], axis=0)
        value = jnp.where(pair_of == 0, mine, turn(mine, 4, 1))
        value = jnp.where(pair_of == 1, turn(after[array], 2 - 2 * pair - 64 * half, 1), value)
        value = jnp.where(pair_of == 2, turn(before[array], 4 - 2 * pair - 64 * half, 1), value)
        value = jnp.where(own, value, 0.0)
        sides[k] = value
        side.append(value)
    r = xr[...]
    q, g = electric_coefficients(r, xs[...], side[12])
    drive = jnp.concatenate([factors[0]] * (TALL // 8), axis=0) * side[13]
    values = {("f", k): side[k] for k in range(COMPS)}
    for base in (0, 6):
        e = side[base : base + 3]
        h = [jnp.where(own, v, 0.0) for v in side_magnetic(e, side[base + 3 : base + 6], r)]
        e = side_electric(h, e, q, g, drive if base == 0 else None)
        for c in range(3):
            values["h", base + 3 + c] = h[c]
            values["e", base + c] = e[c]
    sent = []
    for items, p in ((UP_SIDES, 7), (DOWN_SIDES, 0)):
        packed = jnp.zeros((TALL, COLS), F32)
        for i, item in enumerate(items):
            packed = jnp.where((lane >> 3) == i, turn(values[item], 8 * i - 8 * (p + 2), 1), packed)
        sent.append(packed)
    even = parity("gz")
    rim_a[...] = jnp.where(even, sent[0], sent[1])
    rim_b[...] = jnp.where(even, sent[1], sent[0])


def home(layer):
    mine = lax.axis_index("gz") >> 1
    return (((layer >> 2) ^ mine) << 2) + (layer & 3)


def run_steps(side_loss, factors, f, one, rr, qq, gg, xf, xone, planes, put_field, put_density, halo=None):
    xr = side_loss[0][...]
    xq, xg = electric_coefficients(xr, side_loss[1][...], xf[12])
    factors = [jnp.concatenate([factors[k]] * (TALL // 8), axis=0) for k in range(2)]
    lane = lanes(TALL)
    first_lane, last_lane = lane == 0, lane == COLS - 1

    def side_half(e_ref, e_base, h_base):
        new = side_magnetic([e_ref[e_base + c] for c in range(3)], [xf[h_base + c] for c in range(3)], xr)
        for c in range(3):
            xf[h_base + c] = new[c]

    def side_full(e_base, h_base, out_base, factor):
        drive = None if factor is None else xf[13] * factor
        new = side_electric(
            [xf[h_base + c] for c in range(3)], [xf[e_base + c] for c in range(3)], xq, xg, drive
        )
        for c in range(3):
            xone[out_base + c] = new[c]

    def plane_magnetic(idx, e_ref, x_ref, e_base, h_base):
        def next_x(value, c):
            halo = pltpu.roll(x_ref[e_base + c], 125 - 8 * idx, 1)
            return jnp.where(last_lane, halo, pltpu.roll(value, COLS - 1, 1))

        new = magnetic(
            *[e_ref[e_base + c, idx] for c in range(3)], e_ref[e_base, idx + 1], e_ref[e_base + 1, idx + 1],
            *[f[h_base + c, idx] for c in range(3)], rr[idx], next_x, up_row,
        )
        for c in range(3):
            f[h_base + c, idx] = new[c]

    def plane_electric(idx, e_ref, e_base, h_base, factor):
        def prev_x(value, c):
            halo = pltpu.roll(xf[h_base + c], 123 - 8 * idx, 1)
            return jnp.where(first_lane, halo, pltpu.roll(value, 1, 1))

        drive = None if factor is None else f[13, idx] * factor
        return electric(
            *[f[h_base + c, idx] for c in range(3)], f[h_base, idx - 1], f[h_base + 1, idx - 1],
            *[e_ref[e_base + c, idx] for c in range(3)], qq[idx], gg[idx], drive, prev_x, down_row,
        )

    def over(which, body):
        for idx in planes[which]:
            body(idx)

    def body(idx):
        plane_magnetic(idx, f, xf, 0, 3)
        plane_magnetic(idx, f, xf, 6, 9)

    over(0, body)
    side_half(xf, 0, 3)
    side_half(xf, 6, 9)
    if halo is not None:
        halo(xr, xq, sides=False)

    def body(idx):
        for base, out, factor in ((0, 0, factors[0]), (6, 3, None)):
            new = plane_electric(idx, f, base, base + 3, factor)
            for c in range(3):
                one[out + c, idx] = new[c]

    over(1, body)
    side_full(0, 3, 0, factors[0])
    side_full(6, 9, 3, None)
    if halo is not None:
        halo(xr, xq, sides=True)

    def body(idx):
        plane_magnetic(idx, one, xone, 0, 3)
        plane_magnetic(idx, one, xone, 3, 9)

    over(2, body)
    side_half(xone, 0, 3)
    side_half(xone, 3, 9)

    def body(idx):
        two = plane_electric(idx, one, 0, 3, factors[1])
        zero = plane_electric(idx, one, 3, 9, None)
        density = jnp.zeros((ROWS, COLS), F32)
        for c in range(3):
            last = zero[c][0:ROWS]
            put_field(c, idx, last, f[9 + c, idx, 0:ROWS])
            density = density + f[c, idx, 0:ROWS] * last + one[c, idx, 0:ROWS] * one[3 + c, idx, 0:ROWS]
            density = density + two[c][0:ROWS] * f[6 + c, idx, 0:ROWS]
        put_density(idx, density)

    over(3, body)


def inner_kernel(layer, factors, rr, ss, xr, xs, own, tiles, sides, f, one, qq, gg, sums, e_mid, h_mid, homes, xf, xone):
    del own
    for k in range(COMPS):
        for p in range(PLANES):
            f[k, p + 2, ROWS:TALL] = tiles[k, p]
        xf[k] = sides[k]

    def coefficients(i, carry):
        qq[i + 2], gg[i + 2] = electric_coefficients(rr[i + 2], ss[i + 2], f[12, i + 2])
        return carry

    lax.fori_loop(0, PLANES, coefficients, 0)
    sums[...] = jnp.zeros((LAYERS, ROWS, COLS), F32)
    for i, p in enumerate((0, 1, 6, 7)):
        homes[i] = jnp.full((8, COLS), home(layer[p]), jnp.int32).astype(F32)

    def put(c, idx, e_new, h_new):
        e_mid[c, idx - 4] = e_new
        h_mid[c, idx - 4] = h_new

    def put_density(idx, density):
        sums[home(layer[idx - 2])] = density

    planes = [range(2, 9), range(3, 9), range(3, 8), range(4, 8)]
    run_steps((xr, xs), factors, f, one, rr, qq, gg, xf, xone, planes, put, put_density)


def outer_kernel(
    factors, rr, ss, xr, xs, f_in, one_in, qq_in, gg_in, sums, homes, zb, za, sides, rim_b, rim_a,
    f, one, qq, gg, e_rest, h_rest, zeroth, first, second, third, xf, xone,
):
    del f_in, one_in, qq_in, gg_in
    index = lax.axis_index("gz")
    has_above = (index < lax.axis_size("gz") - 1).astype(F32)
    has_below = (index > 0).astype(F32)
    lane = lanes(TALL)
    low, top = 1, PLANES + 2
    for k in range(COMPS):
        xf[k] = sides[k]
    got = {}
    even = parity("gz")
    for pick, faces, rows, items, idx, keep in (
        (lambda a, b: jnp.where(even, b, a), UP_FACES, UP_ROWS, UP_SIDES, low, has_below),
        (lambda a, b: jnp.where(even, a, b), DOWN_FACES, DOWN_ROWS, DOWN_SIDES, top, has_above),
    ):
        ref = pick(za[...], zb[...])
        packed = pick(rim_a[...], rim_b[...]) * keep
        planes = face_in(ref, faces, rows, keep)
        for i, (kind, k) in enumerate(items):
            if kind != "f":
                at_last, at_first = turn(packed, 126 - 8 * i, 1), turn(packed, -6 - 8 * i, 1)
                fixed = jnp.where(lane == COLS - 1, at_last, planes[kind, k])
                planes[kind, k] = jnp.where(lane == 0, at_first, fixed) if kind == "e" else fixed
            got[kind, k, idx] = (planes[kind, k], turn(packed, 8 * idx - 8 * i, 1))
        for k in (0, 1, 6, 7, 12):
            if ("f", k) in planes:
                f[k, idx] = planes["f", k]
                xf[k] = jnp.where((lane >> 3) == idx, got["f", k, idx][1], xf[k])
    for idx in (low, top):
        qq[idx], gg[idx] = electric_coefficients(rr[idx], ss[idx], f[12, idx])

    def add_z(q, x, y, prev_x):
        return q * ((y - prev_x(y)) - (x - down_row(x, 0)))

    def halo(xr, xq, sides):
        q, q_top, r_half = qq[low], qq[top], 0.5 * rr[low]
        for base, out in ((0, 0), (6, 3)):
            x_side = 0.5 * xr * pltpu.roll(xf[base + 1], 120, 1)
            y_side = -0.5 * xr * pltpu.roll(xf[base], 120, 1)
            if sides:
                added = got["e", base + 2, low][1] + add_z(xq, x_side, y_side, lambda v: pltpu.roll(v, 1, 1))
                xone[out + 2] = jnp.where((lane >> 3) == low, added, xone[out + 2])
                added = got["e", base, top][1] + xq * pltpu.roll(xf[base + 4], 8, 1)
                xone[out] = jnp.where((lane >> 3) == top, added, xone[out])
                added = got["e", base + 1, top][1] - xq * pltpu.roll(xf[base + 3], 8, 1)
                xone[out + 1] = jnp.where((lane >> 3) == top, added, xone[out + 1])
                continue
            x, y = r_half * f[base + 1, 2], -r_half * f[base, 2]

            def prev_x(value):
                return jnp.where(lane == 0, pltpu.roll(y_side, 123 - 8 * low, 1), pltpu.roll(value, 1, 1))

            for k, term, side_term in ((base + 3, x, x_side), (base + 4, y, y_side)):
                plane, side = got["h", k, low]
                f[k, low] = plane + term
                xf[k] = jnp.where((lane >> 3) == low, side + side_term, xf[k])
            f[base + 5, low] = jnp.zeros((TALL, COLS), F32)
            one[out, low] = got["e", base, low][0] - q * y
            one[out + 1, low] = got["e", base + 1, low][0] + q * x
            one[out + 2, low] = got["e", base + 2, low][0] + add_z(q, x, y, prev_x)
            one[out, top] = got["e", base, top][0] + q_top * f[base + 4, top - 1]
            one[out + 1, top] = got["e", base + 1, top][0] - q_top * f[base + 3, top - 1]

    def put(c, idx, e_new, h_new):
        at = idx - 2 if idx < 4 else idx - 6
        e_rest[c, at] = e_new
        h_rest[c, at] = h_new

    late = []

    def put_density(idx, density):
        late.append(density)

    planes = [(9,), (2, 9), (1, 2, 8, 9), (2, 3, 8, 9)]
    run_steps((xr, xs), factors, f, one, rr, qq, gg, xf, xone, planes, put, put_density, halo)
    for i, out in enumerate((zeroth, first, second, third)):
        for j in range(4):
            total = sums[4 * i + j]
            for at, density in enumerate(late):
                here = homes[at] == float(4 * i + j)
                total = total + jnp.where(jnp.concatenate([here] * (ROWS // 8), axis=0), density, 0.0)
            out[j] = total


def store_kernel(e_mid, h_mid, e_rest, h_rest, e_out, h_out, sems):
    copies = []
    for mid, rest, out in ((e_mid, e_rest, e_out), (h_mid, h_rest, h_out)):
        for source, at, first, count in ((mid, 0, 2, 4), (rest, 0, 0, 2), (rest, 2, 6, 2)):
            copies.append((source.at[:, at : at + count], out.at[:, first : first + count]))
    copies = [pltpu.make_async_copy(a, b, sems.at[i]) for i, (a, b) in enumerate(copies)]
    for copy in copies:
        copy.start()
    for copy in copies:
        copy.wait()


def fold_kernel(sums, second, first, third, kept, sent):
    upper = lax.rem(lax.axis_index("gz"), 2) == 1
    for i in range(2):
        low, high = (sums[j] + first[j] + second[j] + third[j] for j in (i, i + 2))
        kept[i] = jnp.where(upper, high, low)
        sent[i] = jnp.where(upper, low, high)


def sum_kernel(kept, got, out):
    out[...] = kept[...] + got[...]


def call(kernel, outs, scratch=(), scalars=0, far=0, aliases=None, out_space=pltpu.VMEM, flops=1000000):
    def run(*args):
        near = len(args) - scalars - far
        specs = [pl.BlockSpec(memory_space=pltpu.SMEM)] * scalars
        specs += [pl.BlockSpec(memory_space=pltpu.VMEM)] * near + [pl.BlockSpec(memory_space=pl.ANY)] * far
        size = sum(4 * math.prod(s) for s in outs) + sum(4 * math.prod(a.shape) for a in args)
        return pl.pallas_call(
            kernel,
            out_shape=[jax.ShapeDtypeStruct(s, F32) for s in outs],
            in_specs=specs,
            out_specs=[pl.BlockSpec(memory_space=out_space)] * len(outs),
            scratch_shapes=[pltpu.VMEM(s, F32) if isinstance(s, tuple) else s for s in scratch],
            input_output_aliases=aliases or {},
            compiler_params=pltpu.CompilerParams(vmem_limit_bytes=24 * 2**20),
            cost_estimate=pl.CostEstimate(flops=flops, bytes_accessed=size, transcendentals=0),
        )(*args)

    return run


def swaps(axis, first):
    count = lax.axis_size(axis)
    pairs = [(i, (i + 1) % count) for i in range(first, count, 2)]
    return pairs + [(b, a) for a, b in pairs]


def across(axis, bits):
    return [(i, i ^ bits) for i in range(lax.axis_size(axis))]


def inner_swaps():
    count, width = lax.axis_size("gy"), lax.axis_size("gx")
    pairs = []
    for j in range(width):
        pairs += [(i * width + j, (i + 1) * width + j) for i in range(1, count - 1, 2)]
        if j % 2 == 0:
            pairs += [(i * width + j, i * width + j + 1) for i in (0, count - 1)]
    return pairs + [(b, a) for a, b in pairs]


def local(e_start, h_start, adjoint_e, adjoint_h, permittivity, current, layer_of_cell, pml_cells, start_step):
    raw = (e_start, h_start, adjoint_e, adjoint_h, permittivity, current)
    raw = [pltpu.with_memory_space_constraint(a, pltpu.HBM) for a in raw]
    block, deep, tall = (ROWS, COLS), (DEEP, TALL, COLS), (TALL, COLS)
    f, ya, yb = call(
        first_kernel, [(COMPS,) + deep, (16 * COMPS, COLS), (16 * COMPS, COLS)], [pltpu.SemaphoreType.DMA((COMPS,))], far=6
    )(*raw)
    yb = lax.ppermute(yb, ("gy", "gx"), inner_swaps())
    ya = lax.ppermute(ya, "gy", swaps("gy", 0))
    strips, right, left, *loss = call(
        strip_kernel, [(COMPS,) + block, (2,) + block, (2,) + block, (2, 8, COLS), deep, deep, tall, tall], scalars=2
    )(start_step, pml_cells, f)
    side = (2,) + tall
    tiles, strips_rim, xa, xb = call(second_kernel, [(COMPS, PLANES, 8, COLS), (COMPS, 8, COLS), side, side])(yb, ya, right, left)
    za, zb = call(face_kernel, [(FACE_ROWS, COLS)] * 2)(f, tiles, *loss[:3])
    za = lax.ppermute(za, "gz", swaps("gz", 0))
    zb = lax.ppermute(zb, "gz", swaps("gz", 1))
    xa = lax.ppermute(xa, "gx", swaps("gx", 0))
    xb = lax.ppermute(xb, "gx", swaps("gx", 1))
    sides, rim_a, rim_b = call(third_kernel, [(COMPS,) + tall, tall, tall])(
        xa, xb, strips, strips_rim, loss[0], *loss[3:]
    )
    rim_a = lax.ppermute(rim_a, "gz", swaps("gz", 0))
    rim_b = lax.ppermute(rim_b, "gz", swaps("gz", 1))
    state = [(COMPS,) + deep, (6,) + deep, deep, deep]
    mid, out = (3, PLANES // 2) + block, (3, PLANES) + block
    side = [(COMPS,) + tall, (6,) + tall]
    *held, sums, e_mid, h_mid, homes = call(inner_kernel, state + [(LAYERS,) + block, mid, mid, (4, 8, COLS)], side, scalars=1, aliases={6: 0}, flops=10**11)(
        layer_of_cell, *loss, f, tiles, sides
    )
    quarter, pair = (LAYERS // 4,) + block, (2,) + block
    *_, e_rest, h_rest, zeroth, first, second, third = call(
        outer_kernel, state + [mid, mid] + [quarter] * 4, side, aliases={5 + i: i for i in range(len(state))}
    )(*loss, *held, sums, homes, zb, za, sides, rim_b, rim_a)
    e_out, h_out = call(store_kernel, [out, out], [pltpu.SemaphoreType.DMA((6,))], out_space=pltpu.HBM)(e_mid, h_mid, e_rest, h_rest)
    first, second, third = (lax.ppermute(v, "gz", across("gz", m)) for v, m in ((first, 2), (second, 4), (third, 6)))
    kept, sent = call(fold_kernel, [pair, pair])(zeroth, second, first, third)
    (gradient,) = call(sum_kernel, [pair])(kept, lax.ppermute(sent, "gz", across("gz", 1)))
    return gradient, e_out, h_out


def solution(mesh):
    fields = P(None, "gz", "gy", "gx")
    cells = P("gz", "gy", "gx")
    return jax.shard_map(
        local,
        mesh=mesh,
        in_specs=(fields, fields, fields, fields, cells, cells, P("gz"), P(), P()),
        out_specs=(cells, fields, fields),
        check_vma=False,
    )
```

```python
import functools
import math

import jax
import jax.numpy as jnp
from jax import lax
from jax.experimental import pallas as pl
from jax.experimental.pallas import tpu as pltpu
from jax.sharding import PartitionSpec as P

F32 = jnp.float32
PLANES, ROWS, COLS = 8, 32, 128
DEEP, TALL = PLANES + 4, ROWS + 8
LAYERS = 16
PERIOD = 64
COMPS = 14
LOW, TOP = 1, PLANES + 2
UP_FACES = [("h", k) for k in (3, 4, 9, 10)] + [("e", k) for k in (0, 1, 2, 6, 7, 8)] + [("f", 12)]
DOWN_FACES = [("f", k) for k in (0, 1, 6, 7, 12)] + [("e", k) for k in (0, 1, 6, 7)]
UP_ROWS = [("h", k, 7) for k in (3, 4, 9, 10)] + [("e", 2, 7), ("e", 8, 7), ("f", 12, 7)]
DOWN_ROWS = [("f", k, 7) for k in (0, 1, 6, 7, 12)] + [("e", 1, 7), ("e", 7, 7), ("f", 1, 6), ("f", 7, 6)]
UP_SIDES, DOWN_SIDES = UP_FACES, DOWN_FACES


def face_rows(faces, rows):
    return ROWS * len(faces) + 8 * ((len(rows) + 3) // 4)


FACE_ROWS = max(face_rows(UP_FACES, UP_ROWS), face_rows(DOWN_FACES, DOWN_ROWS))


def lanes(rows=8):
    return lax.broadcasted_iota(jnp.int32, (rows, COLS), 1)


def subs(rows=8):
    return lax.broadcasted_iota(jnp.int32, (rows, COLS), 0)


def turn(value, shift, axis):
    shift = shift % value.shape[axis]
    return value if shift == 0 else pltpu.roll(value, shift, axis)


def slot(k):
    return k // 8, (k % 8) // 4, k % 4


def slot_mask(k, rows):
    _, half, pair = slot(k)
    lane = lanes(rows)
    inside = ((lane - 16 - 64 * half) & 127) < 64
    return inside & (((lane & 7) >> 1) == pair)


def window(p, rows):
    lane = lanes(rows)
    return (lane >= 8 * (p + 2)) & (lane < 8 * (p + 2) + 4)


def parity(axis):
    return lax.rem(lax.axis_index(axis), 2) == 0


def strip(planes, rows):
    out = jnp.zeros((rows, COLS), F32)
    for p, plane in enumerate(planes):
        out = jnp.where(window(p, rows), turn(plane, 8 * (p + 2) + 2, 1), out)
    return out


def face_pack(strips, rows):
    right = [jnp.zeros((rows, COLS), F32) for _ in range(2)]
    left = [jnp.zeros((rows, COLS), F32) for _ in range(2)]
    for k, value in enumerate(strips):
        array, half, pair = slot(k)
        mask = slot_mask(k, rows)
        right[array] = jnp.where(mask, turn(value, 2 * pair + 64 * half, 1), right[array])
        left[array] = jnp.where(mask, turn(value, 2 * pair - 2 + 64 * half, 1), left[array])
    return right, left


def first_kernel(e, h, ae, ah, eps, cur, f, ya, yb, sems):
    copies = []
    for k in range(COMPS):
        source = (e, h, ae, ah)[k // 3].at[k % 3] if k < 12 else (eps, cur)[k - 12]
        copies.append(pltpu.make_async_copy(source, f.at[k, 2 : PLANES + 2, 0:ROWS], sems.at[k]))
    for copy in copies:
        copy.start()
    even = parity("gy")
    sub = subs()
    for k in range(COMPS):
        copies[k].wait()
        for half in range(2):
            up = jnp.zeros((8, COLS), F32)
            down = jnp.zeros((8, COLS), F32)
            for j in range(4):
                idx = 4 * half + j + 2
                mask = (sub >> 1) == j
                up = jnp.where(mask, turn(f[k, idx, 24:32], 2 * j - 6, 0), up)
                down = jnp.where(mask, turn(f[k, idx, 0:8], 2 * j, 0), down)
            at = 8 * (2 * k + half)
            ya[at : at + 8] = jnp.where(even, up, down)
            yb[at : at + 8] = jnp.where(even, down, up)


def strip_kernel(start, pml, f, strips, right_out, left_out, factors, rr, ss, xr, xs):
    of_plane = block_sigma(pml)
    for idx in range(1, PLANES + 3):
        sigma, inside = of_plane(idx - 2)
        rr[idx], ss[idx] = damping(sigma, inside), 0.5 * sigma
    sigma, inside = side_sigma(pml)
    xr[...], xs[...] = damping(sigma, inside), 0.5 * sigma
    for k in range(2):
        phase = jnp.full((8, COLS), lax.rem(start[0] + k + 1, PERIOD), jnp.int32).astype(F32)
        factors[k] = jnp.sin(phase * (2.0 * math.pi / PERIOD))
    values = []
    for k in range(COMPS):
        value = strip([f[k, p + 2, 0:ROWS] for p in range(PLANES)], ROWS)
        strips[k] = value
        values.append(value)
    right, left = face_pack(values, ROWS)
    for a in range(2):
        right_out[a] = right[a]
        left_out[a] = left[a]


def profile(position, extent, thickness):
    distance = jnp.minimum(position, extent - 1 - position)
    depth = jnp.maximum(thickness - distance, 0).astype(F32) / thickness.astype(F32)
    return 0.8 * depth * depth


def magnetic(ex, ey, ez, ex_up, ey_up, hx, hy, hz, r, next_x, next_y, at=(0, 1, 2)):
    cx = (next_y(ez, 2) - ez) - (ey_up - ey)
    cy = (ex_up - ex) - (next_x(ez, 2) - ez)
    cz = (next_x(ey, 1) - ey) - (next_y(ex, 0) - ex)
    return [r * (h + h - 0.5 * c) - h for h, c in ((hx, cx), (hy, cy), (hz, cz))]


def electric(hx, hy, hz, hx_down, hy_down, ex, ey, ez, q, g, drive, prev_x, prev_y):
    cx = (hz - prev_y(hz, 2)) - (hy - hy_down)
    cy = (hx - hx_down) - (hz - prev_x(hz, 2))
    cz = (hy - prev_x(hy, 1)) - (hx - prev_y(hx, 0))
    if drive is not None:
        cz = cz - drive
    return [q * (g * e + c) for e, c in ((ex, cx), (ey, cy), (ez, cz))]


def grid_sizes():
    return PLANES * lax.axis_size("gz"), ROWS * lax.axis_size("gy"), COLS * lax.axis_size("gx")


def row_grid():
    row = subs(TALL)
    at = ROWS * lax.axis_index("gy") + jnp.where(row >= 36, row - TALL, row)
    return at, (at >= 0) & (at < grid_sizes()[1])


def damping(sigma, inside):
    return jnp.where(inside, 1.0 / (1.0 + 0.25 * sigma), 0.0)


def electric_coefficients(r, half_sigma, permittivity):
    twice = 2.0 * jnp.maximum(permittivity, 1.0)
    return jnp.where(r > 0.0, 1.0 / (twice + half_sigma), 0.0), twice - half_sigma


def block_sigma(pml):
    nz, ny, nx = grid_sizes()
    at, row_in = row_grid()
    flat = profile(at, ny, pml[1]) + profile(COLS * lax.axis_index("gx") + lanes(TALL), nx, pml[2])

    def of_plane(p):
        z_at = jnp.full((TALL, COLS), PLANES * lax.axis_index("gz") + p, jnp.int32)
        sigma = profile(z_at[0:8], nz, pml[0])
        sigma = jnp.concatenate([sigma] * (TALL // 8), axis=0) + flat
        return sigma, row_in & (z_at >= 0) & (z_at < nz)

    return of_plane


def side_sigma(pml):
    nz, ny, nx = grid_sizes()
    at, row_in = row_grid()
    lane = lanes(TALL)
    column = lane & 7
    x_at = COLS * lax.axis_index("gx") + jnp.where(column < 4, COLS - 2 + column, column - 6)
    z_at = PLANES * lax.axis_index("gz") + (lane >> 3) - 2
    inside = row_in & (z_at >= 0) & (z_at < nz) & (x_at >= 0) & (x_at < nx)
    return profile(z_at, nz, pml[0]) + profile(at, ny, pml[1]) + profile(x_at, nx, pml[2]), inside


def up_row(value, _):
    return pltpu.roll(value, TALL - 1, 0)


def down_row(value, _):
    return pltpu.roll(value, 1, 0)


def side_magnetic(e, h, r):
    return magnetic(
        *e, pltpu.roll(e[0], 120, 1), pltpu.roll(e[1], 120, 1), *h, r, lambda v, _: pltpu.roll(v, 127, 1), up_row
    )


def side_electric(h, e, q, g, drive):
    return electric(
        *h, pltpu.roll(h[0], 8, 1), pltpu.roll(h[1], 8, 1), *e, q, g, drive, lambda v, _: pltpu.roll(v, 1, 1), down_row
    )


def face_blocks(faces, rows, values):
    blocks = [values[item][0:ROWS] for item in faces]
    sub = subs()
    for i in range(0, len(rows), 4):
        tile = jnp.zeros((8, COLS), F32)
        for j, (kind, k, first) in enumerate(rows[i : i + 4]):
            tile = jnp.where((sub >> 1) == j, turn(values[kind, k][ROWS:TALL], 2 * j - first, 0), tile)
        blocks.append(tile)
    whole = jnp.concatenate(blocks, axis=0)
    fill = FACE_ROWS - whole.shape[0]
    return jnp.concatenate([whole, jnp.zeros((fill, COLS), F32)], axis=0) if fill else whole


def face_in(ref, faces, rows, keep):
    got = {}
    for i, item in enumerate(faces):
        got[item] = [ref[ROWS * i : ROWS * i + ROWS] * keep, jnp.zeros((8, COLS), F32)]
    sub = subs()
    for i, (kind, k, first) in enumerate(rows):
        at = ROWS * len(faces) + 8 * (i // 4)
        tile = turn(ref[at : at + 8], first - 2 * (i % 4), 0) * keep
        mask = (sub == first) | (sub == (first + 1) % 8)
        got[kind, k][1] = jnp.where(mask, tile, got[kind, k][1])
    return {item: jnp.concatenate(parts, axis=0) for item, parts in got.items()}


def second_kernel(yb, ya, right_in, left_in, tiles, strips, xa, xb):
    index = lax.axis_index("gy")
    even = parity("gy")
    has_after = (index < lax.axis_size("gy") - 1).astype(F32)
    has_before = (index > 0).astype(F32)
    sub = subs()
    values = []
    for k in range(COMPS):
        planes = []
        for half in range(2):
            at = 8 * (2 * k + half)
            got_a, got_b = ya[at : at + 8], yb[at : at + 8]
            after = jnp.where(even, got_a, got_b) * has_after
            before = jnp.where(even, got_b, got_a) * has_before
            for j in range(4):
                tile = jnp.where(sub < 2, turn(after, -2 * j, 0), jnp.where(sub >= 6, turn(before, 6 - 2 * j, 0), 0.0))
                tiles[k, 4 * half + j] = tile
                planes.append(tile)
        value = strip(planes, 8)
        strips[k] = value
        values.append(value)
    right, left = face_pack(values, 8)
    even = parity("gx")
    for a in range(2):
        xa[a, 0:ROWS] = jnp.where(even, right_in[a], left_in[a])
        xb[a, 0:ROWS] = jnp.where(even, left_in[a], right_in[a])
        xa[a, ROWS:TALL] = jnp.where(even, right[a], left[a])
        xb[a, ROWS:TALL] = jnp.where(even, left[a], right[a])


def face_kernel(f, tiles, factors, rr, ss, za, zb):
    def field(k, p):
        return jnp.concatenate([f[k, p + 2, 0:ROWS], tiles[k, p]], axis=0)

    zero = jnp.zeros((TALL, COLS), F32)
    drive = jnp.concatenate([factors[0]] * (TALL // 8), axis=0) * field(13, 7)

    def next_x(value, _):
        return pltpu.roll(value, COLS - 1, 1)

    def prev_x(value, _):
        return pltpu.roll(value, 1, 1)

    def half_step(base, p):
        up = [field(base + c, p + 1) for c in range(2)] if p < 7 else [zero, zero]
        return magnetic(
            *[field(base + c, p) for c in range(3)], *up, *[field(base + 3 + c, p) for c in range(3)],
            rr[p + 2], next_x, up_row,
        )

    sent = []
    for p, faces, rows in ((7, UP_FACES, UP_ROWS), (0, DOWN_FACES, DOWN_ROWS)):
        values = {("f", k): field(k, p) for k in (0, 1, 6, 7, 12)}
        q, g = electric_coefficients(rr[p + 2], ss[p + 2], values["f", 12])
        for base in (0, 6):
            h = half_step(base, p)
            down = half_step(base, 6)[0:2] if p == 7 else [zero, zero]
            e = electric(
                *h, *down, *[field(base + c, p) for c in range(3)], q, g, drive if p == 7 and base == 0 else None, prev_x, down_row
            )
            for c in range(3):
                values["h", base + 3 + c] = h[c]
                values["e", base + c] = e[c]
        sent.append(face_blocks(faces, rows, values))
    even = parity("gz")
    za[...] = jnp.where(even, sent[0], sent[1])
    zb[...] = jnp.where(even, sent[1], sent[0])


def third_kernel(xb, xa, strips, strips_rim, factors, xr, xs, sides, rim_a, rim_b):
    index = lax.axis_index("gx")
    even = parity("gx")
    has_after = (index < lax.axis_size("gx") - 1).astype(F32)
    has_before = (index > 0).astype(F32)
    lane = lanes(TALL)
    pair_of = (lane & 7) >> 1
    own = (lane >= 16) & (lane < 80)
    after = [jnp.where(even, xa[a], xb[a]) * has_after for a in range(2)]
    before = [jnp.where(even, xb[a], xa[a]) * has_before for a in range(2)]
    side = []
    for k in range(COMPS):
        array, half, pair = slot(k)
        mine = jnp.concatenate([strips[k], strips_rim[k]], axis=0)
        value = jnp.where(pair_of == 0, mine, turn(mine, 4, 1))
        value = jnp.where(pair_of == 1, turn(after[array], 2 - 2 * pair - 64 * half, 1), value)
        value = jnp.where(pair_of == 2, turn(before[array], 4 - 2 * pair - 64 * half, 1), value)
        value = jnp.where(own, value, 0.0)
        sides[k] = value
        side.append(value)
    r = xr[...]
    q, g = electric_coefficients(r, xs[...], side[12])
    drive = jnp.concatenate([factors[0]] * (TALL // 8), axis=0) * side[13]
    values = {("f", k): side[k] for k in range(COMPS)}
    for base in (0, 6):
        e = side[base : base + 3]
        h = [jnp.where(own, v, 0.0) for v in side_magnetic(e, side[base + 3 : base + 6], r)]
        e = side_electric(h, e, q, g, drive if base == 0 else None)
        for c in range(3):
            values["h", base + 3 + c] = h[c]
            values["e", base + c] = e[c]
    sent = []
    for items, p in ((UP_SIDES, 7), (DOWN_SIDES, 0)):
        packed = jnp.zeros((TALL, COLS), F32)
        for i, item in enumerate(items):
            packed = jnp.where((lane >> 3) == i, turn(values[item], 8 * i - 8 * (p + 2), 1), packed)
        sent.append(packed)
    even = parity("gz")
    rim_a[...] = jnp.where(even, sent[0], sent[1])
    rim_b[...] = jnp.where(even, sent[1], sent[0])


def home(layer):
    mine = lax.axis_index("gz") >> 1
    return (((layer >> 2) ^ mine) << 2) + (layer & 3)


def run_steps(side_loss, factors, f, one, rr, qq, gg, xf, xone, planes, put_field, put_density, halo=None):
    xr = side_loss[0][...]
    xq, xg = electric_coefficients(xr, side_loss[1][...], xf[12])
    factors = [jnp.concatenate([factors[k]] * (TALL // 8), axis=0) for k in range(2)]
    lane = lanes(TALL)
    first_lane, last_lane = lane == 0, lane == COLS - 1

    def side_half(e_ref, e_base, h_base):
        new = side_magnetic([e_ref[e_base + c] for c in range(3)], [xf[h_base + c] for c in range(3)], xr)
        for c in range(3):
            xf[h_base + c] = new[c]

    def side_full(e_base, h_base, out_base, factor):
        drive = None if factor is None else xf[13] * factor
        new = side_electric(
            [xf[h_base + c] for c in range(3)], [xf[e_base + c] for c in range(3)], xq, xg, drive
        )
        for c in range(3):
            xone[out_base + c] = new[c]

    def plane_magnetic(idx, e_ref, x_ref, e_base, h_base):
        def next_x(value, c):
            halo = pltpu.roll(x_ref[e_base + c], 125 - 8 * idx, 1)
            return jnp.where(last_lane, halo, pltpu.roll(value, COLS - 1, 1))

        new = magnetic(
            *[e_ref[e_base + c, idx] for c in range(3)], e_ref[e_base, idx + 1], e_ref[e_base + 1, idx + 1],
            *[f[h_base + c, idx] for c in range(3)], rr[idx], next_x, up_row,
        )
        for c in range(3):
            f[h_base + c, idx] = new[c]

    def plane_electric(idx, e_ref, e_base, h_base, factor):
        def prev_x(value, c):
            halo = pltpu.roll(xf[h_base + c], 123 - 8 * idx, 1)
            return jnp.where(first_lane, halo, pltpu.roll(value, 1, 1))

        drive = None if factor is None else f[13, idx] * factor
        return electric(
            *[f[h_base + c, idx] for c in range(3)], f[h_base, idx - 1], f[h_base + 1, idx - 1],
            *[e_ref[e_base + c, idx] for c in range(3)], qq[idx], gg[idx], drive, prev_x, down_row,
        )

    def over(which, body):
        for idx in planes[which]:
            body(idx)

    def body(idx):
        plane_magnetic(idx, f, xf, 0, 3)
        plane_magnetic(idx, f, xf, 6, 9)

    over(0, body)
    side_half(xf, 0, 3)
    side_half(xf, 6, 9)
    if halo is not None:
        halo(xr, xq, sides=False)

    def body(idx):
        for base, out, factor in ((0, 0, factors[0]), (6, 3, None)):
            new = plane_electric(idx, f, base, base + 3, factor)
            for c in range(3):
                one[out + c, idx] = new[c]

    over(1, body)
    side_full(0, 3, 0, factors[0])
    side_full(6, 9, 3, None)
    if halo is not None:
        halo(xr, xq, sides=True)

    def body(idx):
        plane_magnetic(idx, one, xone, 0, 3)
        plane_magnetic(idx, one, xone, 3, 9)

    over(2, body)
    side_half(xone, 0, 3)
    side_half(xone, 3, 9)

    def body(idx):
        two = plane_electric(idx, one, 0, 3, factors[1])
        zero = plane_electric(idx, one, 3, 9, None)
        density = jnp.zeros((ROWS, COLS), F32)
        for c in range(3):
            last = zero[c][0:ROWS]
            put_field(c, idx, last, f[9 + c, idx, 0:ROWS])
            density = density + f[c, idx, 0:ROWS] * last + one[c, idx, 0:ROWS] * one[3 + c, idx, 0:ROWS]
            density = density + two[c][0:ROWS] * f[6 + c, idx, 0:ROWS]
        put_density(idx, density)

    over(3, body)


def inner_kernel(layer, factors, rr, ss, xr, xs, own, tiles, sides, f, one, qq, gg, sums, e_mid, h_mid, homes, xf, xone):
    del own
    for k in range(COMPS):
        for p in range(PLANES):
            f[k, p + 2, ROWS:TALL] = tiles[k, p]
        xf[k] = sides[k]

    def coefficients(i, carry):
        qq[i + 2], gg[i + 2] = electric_coefficients(rr[i + 2], ss[i + 2], f[12, i + 2])
        return carry

    lax.fori_loop(0, PLANES, coefficients, 0)
    sums[...] = jnp.zeros((LAYERS, ROWS, COLS), F32)
    for i, p in enumerate((0, 1, 6, 7)):
        homes[i] = jnp.full((8, COLS), home(layer[p]), jnp.int32).astype(F32)

    def put(c, idx, e_new, h_new):
        e_mid[c, idx - 4] = e_new
        h_mid[c, idx - 4] = h_new

    def put_density(idx, density):
        sums[home(layer[idx - 2])] = density

    planes = [range(2, 9), range(3, 9), range(3, 8), range(4, 8)]
    run_steps((xr, xs), factors, f, one, rr, qq, gg, xf, xone, planes, put, put_density)


def halo_kernel(rr, ss, sides, f_in, qq_in, gg_in, zb, za, f, qq, gg, below, above):
    del f_in, qq_in, gg_in
    index = lax.axis_index("gz")
    even = parity("gz")
    lane = lanes(TALL)
    for pick, faces, rows, out, idx, keep in (
        (lambda a, b: jnp.where(even, b, a), UP_FACES, UP_ROWS, below, LOW, (index > 0).astype(F32)),
        (lambda a, b: jnp.where(even, a, b), DOWN_FACES, DOWN_ROWS, above, TOP, (index < lax.axis_size("gz") - 1).astype(F32)),
    ):
        planes = face_in(pick(za[...], zb[...]), faces, rows, keep)
        for i, (kind, k) in enumerate(faces):
            if kind == "f":
                f[k, idx] = planes[kind, k]
            else:
                out[i] = planes[kind, k]
        qq[idx], gg[idx] = electric_coefficients(rr[idx], ss[idx], f[12, idx])
    last = TOP - 1
    for base in (0, 6):

        def next_x(value, c):
            return jnp.where(lane == COLS - 1, turn(sides[base + c], 125 - 8 * last, 1), pltpu.roll(value, COLS - 1, 1))

        new = magnetic(
            *[f[base + c, last] for c in range(3)], f[base, TOP], f[base + 1, TOP],
            *[f[base + 3 + c, last] for c in range(3)], rr[last], next_x, up_row,
        )
        for c in range(3):
            f[base + 3 + c, last] = new[c]


def outer_kernel(
    factors, rr, xr, xs, f_in, one_in, qq, gg, sums, homes, below, above, sides, rim_b, rim_a,
    f, one, e_rest, h_rest, zeroth, first, second, third, xf, xone,
):
    del f_in, one_in
    index = lax.axis_index("gz")
    has_above = (index < lax.axis_size("gz") - 1).astype(F32)
    has_below = (index > 0).astype(F32)
    lane = lanes(TALL)
    low, top = LOW, TOP
    for k in range(COMPS):
        xf[k] = sides[k]
    got = {}
    even = parity("gz")
    for pick, ref, faces, idx, keep in (
        (lambda a, b: jnp.where(even, b, a), below, UP_FACES, low, has_below),
        (lambda a, b: jnp.where(even, a, b), above, DOWN_FACES, top, has_above),
    ):
        packed = pick(rim_a[...], rim_b[...]) * keep
        for i, (kind, k) in enumerate(faces):
            side = turn(packed, 8 * idx - 8 * i, 1)
            if kind == "f":
                xf[k] = jnp.where((lane >> 3) == idx, side, xf[k])
                continue
            plane = jnp.where(lane == COLS - 1, turn(packed, 126 - 8 * i, 1), ref[i])
            if kind == "e":
                plane = jnp.where(lane == 0, turn(packed, -6 - 8 * i, 1), plane)
            got[kind, k, idx] = (plane, side)

    def add_z(q, x, y, prev_x):
        return q * ((y - prev_x(y)) - (x - down_row(x, 0)))

    def halo(xr, xq, sides):
        q, q_top, r_half = qq[low], qq[top], 0.5 * rr[low]
        for base, out in ((0, 0), (6, 3)):
            x_side = 0.5 * xr * pltpu.roll(xf[base + 1], 120, 1)
            y_side = -0.5 * xr * pltpu.roll(xf[base], 120, 1)
            if sides:
                added = got["e", base + 2, low][1] + add_z(xq, x_side, y_side, lambda v: pltpu.roll(v, 1, 1))
                xone[out + 2] = jnp.where((lane >> 3) == low, added, xone[out + 2])
                added = got["e", base, top][1] + xq * pltpu.roll(xf[base + 4], 8, 1)
                xone[out] = jnp.where((lane >> 3) == top, added, xone[out])
                added = got["e", base + 1, top][1] - xq * pltpu.roll(xf[base + 3], 8, 1)
                xone[out + 1] = jnp.where((lane >> 3) == top, added, xone[out + 1])
                continue
            x, y = r_half * f[base + 1, 2], -r_half * f[base, 2]

            def prev_x(value):
                return jnp.where(lane == 0, pltpu.roll(y_side, 123 - 8 * low, 1), pltpu.roll(value, 1, 1))

            for k, term, side_term in ((base + 3, x, x_side), (base + 4, y, y_side)):
                plane, side = got["h", k, low]
                f[k, low] = plane + term
                xf[k] = jnp.where((lane >> 3) == low, side + side_term, xf[k])
            f[base + 5, low] = jnp.zeros((TALL, COLS), F32)
            one[out, low] = got["e", base, low][0] - q * y
            one[out + 1, low] = got["e", base + 1, low][0] + q * x
            one[out + 2, low] = got["e", base + 2, low][0] + add_z(q, x, y, prev_x)
            one[out, top] = got["e", base, top][0] + q_top * f[base + 4, top - 1]
            one[out + 1, top] = got["e", base + 1, top][0] - q_top * f[base + 3, top - 1]

    def put(c, idx, e_new, h_new):
        at = idx - 2 if idx < 4 else idx - 6
        e_rest[c, at] = e_new
        h_rest[c, at] = h_new

    late = []

    def put_density(idx, density):
        late.append(density)

    planes = [(), (2, 9), (1, 2, 8, 9), (2, 3, 8, 9)]
    run_steps((xr, xs), factors, f, one, rr, qq, gg, xf, xone, planes, put, put_density, halo)
    for i, out in enumerate((zeroth, first, second, third)):
        for j in range(4):
            total = sums[4 * i + j]
            for at, density in enumerate(late):
                here = homes[at] == float(4 * i + j)
                total = total + jnp.where(jnp.concatenate([here] * (ROWS // 8), axis=0), density, 0.0)
            out[j] = total


def store_kernel(e_mid, h_mid, e_rest, h_rest, e_out, h_out, sems):
    copies = []
    for mid, rest, out in ((e_mid, e_rest, e_out), (h_mid, h_rest, h_out)):
        for source, at, first, count in ((mid, 0, 2, 4), (rest, 0, 0, 2), (rest, 2, 6, 2)):
            copies.append((source.at[:, at : at + count], out.at[:, first : first + count]))
    copies = [pltpu.make_async_copy(a, b, sems.at[i]) for i, (a, b) in enumerate(copies)]
    for copy in copies:
        copy.start()
    for copy in copies:
        copy.wait()


def fold_kernel(sums, second, first, third, kept, sent):
    upper = lax.rem(lax.axis_index("gz"), 2) == 1
    for i in range(2):
        low, high = (sums[j] + first[j] + second[j] + third[j] for j in (i, i + 2))
        kept[i] = jnp.where(upper, high, low)
        sent[i] = jnp.where(upper, low, high)


def sum_kernel(kept, got, out):
    out[...] = kept[...] + got[...]


def call(kernel, outs, scratch=(), scalars=0, far=0, aliases=None, out_space=pltpu.VMEM, flops=1000000):
    def run(*args):
        near = len(args) - scalars - far
        specs = [pl.BlockSpec(memory_space=pltpu.SMEM)] * scalars
        specs += [pl.BlockSpec(memory_space=pltpu.VMEM)] * near + [pl.BlockSpec(memory_space=pl.ANY)] * far
        size = sum(4 * math.prod(s) for s in outs) + sum(4 * math.prod(a.shape) for a in args)
        return pl.pallas_call(
            kernel,
            out_shape=[jax.ShapeDtypeStruct(s, F32) for s in outs],
            in_specs=specs,
            out_specs=[pl.BlockSpec(memory_space=out_space)] * len(outs),
            scratch_shapes=[pltpu.VMEM(s, F32) if isinstance(s, tuple) else s for s in scratch],
            input_output_aliases=aliases or {},
            compiler_params=pltpu.CompilerParams(vmem_limit_bytes=24 * 2**20),
            cost_estimate=pl.CostEstimate(flops=flops, bytes_accessed=size, transcendentals=0),
        )(*args)

    return run


def swaps(axis, first):
    count = lax.axis_size(axis)
    pairs = [(i, (i + 1) % count) for i in range(first, count, 2)]
    return pairs + [(b, a) for a, b in pairs]


def across(axis, bits):
    return [(i, i ^ bits) for i in range(lax.axis_size(axis))]


def inner_swaps():
    count, width = lax.axis_size("gy"), lax.axis_size("gx")
    pairs = []
    for j in range(width):
        pairs += [(i * width + j, (i + 1) * width + j) for i in range(1, count - 1, 2)]
        if j % 2 == 0:
            pairs += [(i * width + j, i * width + j + 1) for i in (0, count - 1)]
    return pairs + [(b, a) for a, b in pairs]


def local(e_start, h_start, adjoint_e, adjoint_h, permittivity, current, layer_of_cell, pml_cells, start_step):
    raw = (e_start, h_start, adjoint_e, adjoint_h, permittivity, current)
    raw = [pltpu.with_memory_space_constraint(a, pltpu.HBM) for a in raw]
    block, deep, tall = (ROWS, COLS), (DEEP, TALL, COLS), (TALL, COLS)
    f, ya, yb = call(
        first_kernel, [(COMPS,) + deep, (16 * COMPS, COLS), (16 * COMPS, COLS)], [pltpu.SemaphoreType.DMA((COMPS,))], far=6
    )(*raw)
    yb = lax.ppermute(yb, ("gy", "gx"), inner_swaps())
    ya = lax.ppermute(ya, "gy", swaps("gy", 0))
    strips, right, left, *loss = call(
        strip_kernel, [(COMPS,) + block, (2,) + block, (2,) + block, (2, 8, COLS), deep, deep, tall, tall], scalars=2
    )(start_step, pml_cells, f)
    side = (2,) + tall
    tiles, strips_rim, xa, xb = call(second_kernel, [(COMPS, PLANES, 8, COLS), (COMPS, 8, COLS), side, side])(yb, ya, right, left)
    za, zb = call(face_kernel, [(FACE_ROWS, COLS)] * 2)(f, tiles, *loss[:3])
    za = lax.ppermute(za, "gz", swaps("gz", 0))
    zb = lax.ppermute(zb, "gz", swaps("gz", 1))
    xa = lax.ppermute(xa, "gx", swaps("gx", 0))
    xb = lax.ppermute(xb, "gx", swaps("gx", 1))
    sides, rim_a, rim_b = call(third_kernel, [(COMPS,) + tall, tall, tall])(
        xb, xa, strips, strips_rim, loss[0], *loss[3:]
    )
    rim_a = lax.ppermute(rim_a, "gz", swaps("gz", 0))
    rim_b = lax.ppermute(rim_b, "gz", swaps("gz", 1))
    state = [(COMPS,) + deep, (6,) + deep, deep, deep]
    mid, out = (3, PLANES // 2) + block, (3, PLANES) + block
    side = [(COMPS,) + tall, (6,) + tall]
    *held, sums, e_mid, h_mid, homes = call(inner_kernel, state + [(LAYERS,) + block, mid, mid, (4, 8, COLS)], side, scalars=1, aliases={6: 0}, flops=10**11)(
        layer_of_cell, *loss, f, tiles, sides
    )
    quarter, pair = (LAYERS // 4,) + block, (2,) + block
    f, one, qq, gg = held
    factors, rr, ss, xr, xs = loss
    f, qq, gg, below, above = call(
        halo_kernel,
        [(COMPS,) + deep, deep, deep, (len(UP_FACES),) + tall, (len(DOWN_FACES),) + tall],
        aliases={3: 0, 4: 1, 5: 2},
    )(rr, ss, sides, f, qq, gg, zb, za)
    *_, e_rest, h_rest, zeroth, first, second, third = call(
        outer_kernel, [(COMPS,) + deep, (6,) + deep, mid, mid] + [quarter] * 4, side, aliases={4: 0, 5: 1}
    )(factors, rr, xr, xs, f, one, qq, gg, sums, homes, below, above, sides, rim_b, rim_a)
    e_out, h_out = call(store_kernel, [out, out], [pltpu.SemaphoreType.DMA((6,))], out_space=pltpu.HBM)(e_mid, h_mid, e_rest, h_rest)
    first, second, third = (lax.ppermute(v, "gz", across("gz", m)) for v, m in ((first, 2), (second, 4), (third, 6)))
    kept, sent = call(fold_kernel, [pair, pair])(zeroth, second, first, third)
    (gradient,) = call(sum_kernel, [pair])(kept, lax.ppermute(sent, "gz", across("gz", 1)))
    return gradient, e_out, h_out


def solution(mesh):
    fields = P(None, "gz", "gy", "gx")
    cells = P("gz", "gy", "gx")
    return jax.shard_map(
        local,
        mesh=mesh,
        in_specs=(fields, fields, fields, fields, cells, cells, P("gz"), P(), P()),
        out_specs=(cells, fields, fields),
        check_vma=False,
    )
```

```python
import functools
import math

import jax
import jax.numpy as jnp
from jax import lax
from jax.experimental import pallas as pl
from jax.experimental.pallas import tpu as pltpu
from jax.sharding import PartitionSpec as P

F32 = jnp.float32
PLANES, ROWS, COLS = 8, 32, 128
DEEP, TALL = PLANES + 4, ROWS + 8
LAYERS = 16
PERIOD = 64
COMPS = 14
LOW, TOP = 1, PLANES + 2
UP_FACES = [("h", k) for k in (3, 4, 9, 10)] + [("e", k) for k in (0, 1, 2, 6, 7, 8)] + [("f", 12)]
DOWN_FACES = [("f", k) for k in (0, 1, 6, 7, 12)] + [("e", k) for k in (0, 1, 6, 7)]
UP_ROWS = [("h", k, 7) for k in (3, 4, 9, 10)] + [("e", 2, 7), ("e", 8, 7), ("f", 12, 7)]
DOWN_ROWS = [("f", k, 7) for k in (0, 1, 6, 7, 12)] + [("e", 1, 7), ("e", 7, 7), ("f", 1, 6), ("f", 7, 6)]
UP_SIDES, DOWN_SIDES = UP_FACES, DOWN_FACES


def face_rows(faces, rows):
    return ROWS * len(faces) + 8 * ((len(rows) + 3) // 4)


FACE_ROWS = max(face_rows(UP_FACES, UP_ROWS), face_rows(DOWN_FACES, DOWN_ROWS))


def lanes(rows=8):
    return lax.broadcasted_iota(jnp.int32, (rows, COLS), 1)


def subs(rows=8):
    return lax.broadcasted_iota(jnp.int32, (rows, COLS), 0)


def turn(value, shift, axis):
    shift = shift % value.shape[axis]
    return value if shift == 0 else pltpu.roll(value, shift, axis)


def slot(k):
    return k // 8, (k % 8) // 4, k % 4


def slot_mask(k, rows):
    _, half, pair = slot(k)
    lane = lanes(rows)
    inside = ((lane - 16 - 64 * half) & 127) < 64
    return inside & (((lane & 7) >> 1) == pair)


def window(p, rows):
    lane = lanes(rows)
    return (lane >= 8 * (p + 2)) & (lane < 8 * (p + 2) + 4)


def parity(axis):
    return lax.rem(lax.axis_index(axis), 2) == 0


def strip(planes, rows):
    out = jnp.zeros((rows, COLS), F32)
    for p, plane in enumerate(planes):
        out = jnp.where(window(p, rows), turn(plane, 8 * (p + 2) + 2, 1), out)
    return out


def face_pack(strips, rows):
    right = [jnp.zeros((rows, COLS), F32) for _ in range(2)]
    left = [jnp.zeros((rows, COLS), F32) for _ in range(2)]
    for k, value in enumerate(strips):
        array, half, pair = slot(k)
        mask = slot_mask(k, rows)
        right[array] = jnp.where(mask, turn(value, 2 * pair + 64 * half, 1), right[array])
        left[array] = jnp.where(mask, turn(value, 2 * pair - 2 + 64 * half, 1), left[array])
    return right, left


def first_kernel(e, h, ae, ah, eps, cur, f, ya, yb, sems):
    copies = []
    for k in range(COMPS):
        source = (e, h, ae, ah)[k // 3].at[k % 3] if k < 12 else (eps, cur)[k - 12]
        copies.append(pltpu.make_async_copy(source, f.at[k, 2 : PLANES + 2, 0:ROWS], sems.at[k]))
    for copy in copies:
        copy.start()
    even = parity("gy")
    sub = subs()
    for k in range(COMPS):
        copies[k].wait()
        for half in range(2):
            up = jnp.zeros((8, COLS), F32)
            down = jnp.zeros((8, COLS), F32)
            for j in range(4):
                idx = 4 * half + j + 2
                mask = (sub >> 1) == j
                up = jnp.where(mask, turn(f[k, idx, 24:32], 2 * j - 6, 0), up)
                down = jnp.where(mask, turn(f[k, idx, 0:8], 2 * j, 0), down)
            at = 8 * (2 * k + half)
            ya[at : at + 8] = jnp.where(even, up, down)
            yb[at : at + 8] = jnp.where(even, down, up)


def strip_kernel(start, pml, f, strips, right_out, left_out, factors, rr, ss, xr, xs):
    of_plane = block_sigma(pml)
    for idx in range(1, PLANES + 3):
        sigma, inside = of_plane(idx - 2)
        rr[idx], ss[idx] = damping(sigma, inside), 0.5 * sigma
    sigma, inside = side_sigma(pml)
    xr[...], xs[...] = damping(sigma, inside), 0.5 * sigma
    for k in range(2):
        phase = jnp.full((8, COLS), lax.rem(start[0] + k + 1, PERIOD), jnp.int32).astype(F32)
        factors[k] = jnp.sin(phase * (2.0 * math.pi / PERIOD))
    values = []
    for k in range(COMPS):
        value = strip([f[k, p + 2, 0:ROWS] for p in range(PLANES)], ROWS)
        strips[k] = value
        values.append(value)
    right, left = face_pack(values, ROWS)
    for a in range(2):
        right_out[a] = right[a]
        left_out[a] = left[a]


def profile(position, extent, thickness):
    distance = jnp.minimum(position, extent - 1 - position)
    depth = jnp.maximum(thickness - distance, 0).astype(F32) / thickness.astype(F32)
    return 0.8 * depth * depth


def magnetic(ex, ey, ez, ex_up, ey_up, hx, hy, hz, r, next_x, next_y, at=(0, 1, 2)):
    cx = (next_y(ez, 2) - ez) - (ey_up - ey)
    cy = (ex_up - ex) - (next_x(ez, 2) - ez)
    cz = (next_x(ey, 1) - ey) - (next_y(ex, 0) - ex)
    return [r * (h + h - 0.5 * c) - h for h, c in ((hx, cx), (hy, cy), (hz, cz))]


def electric(hx, hy, hz, hx_down, hy_down, ex, ey, ez, q, g, drive, prev_x, prev_y):
    cx = (hz - prev_y(hz, 2)) - (hy - hy_down)
    cy = (hx - hx_down) - (hz - prev_x(hz, 2))
    cz = (hy - prev_x(hy, 1)) - (hx - prev_y(hx, 0))
    if drive is not None:
        cz = cz - drive
    return [q * (g * e + c) for e, c in ((ex, cx), (ey, cy), (ez, cz))]


def grid_sizes():
    return PLANES * lax.axis_size("gz"), ROWS * lax.axis_size("gy"), COLS * lax.axis_size("gx")


def row_grid():
    row = subs(TALL)
    at = ROWS * lax.axis_index("gy") + jnp.where(row >= 36, row - TALL, row)
    return at, (at >= 0) & (at < grid_sizes()[1])


def damping(sigma, inside):
    return jnp.where(inside, 1.0 / (1.0 + 0.25 * sigma), 0.0)


def electric_coefficients(r, half_sigma, permittivity):
    twice = 2.0 * jnp.maximum(permittivity, 1.0)
    return jnp.where(r > 0.0, 1.0 / (twice + half_sigma), 0.0), twice - half_sigma


def block_sigma(pml):
    nz, ny, nx = grid_sizes()
    at, row_in = row_grid()
    flat = profile(at, ny, pml[1]) + profile(COLS * lax.axis_index("gx") + lanes(TALL), nx, pml[2])

    def of_plane(p):
        z_at = jnp.full((TALL, COLS), PLANES * lax.axis_index("gz") + p, jnp.int32)
        sigma = profile(z_at[0:8], nz, pml[0])
        sigma = jnp.concatenate([sigma] * (TALL // 8), axis=0) + flat
        return sigma, row_in & (z_at >= 0) & (z_at < nz)

    return of_plane


def side_sigma(pml):
    nz, ny, nx = grid_sizes()
    at, row_in = row_grid()
    lane = lanes(TALL)
    column = lane & 7
    x_at = COLS * lax.axis_index("gx") + jnp.where(column < 4, COLS - 2 + column, column - 6)
    z_at = PLANES * lax.axis_index("gz") + (lane >> 3) - 2
    inside = row_in & (z_at >= 0) & (z_at < nz) & (x_at >= 0) & (x_at < nx)
    return profile(z_at, nz, pml[0]) + profile(at, ny, pml[1]) + profile(x_at, nx, pml[2]), inside


def up_row(value, _):
    return pltpu.roll(value, TALL - 1, 0)


def down_row(value, _):
    return pltpu.roll(value, 1, 0)


def side_magnetic(e, h, r):
    return magnetic(
        *e, pltpu.roll(e[0], 120, 1), pltpu.roll(e[1], 120, 1), *h, r, lambda v, _: pltpu.roll(v, 127, 1), up_row
    )


def side_electric(h, e, q, g, drive):
    return electric(
        *h, pltpu.roll(h[0], 8, 1), pltpu.roll(h[1], 8, 1), *e, q, g, drive, lambda v, _: pltpu.roll(v, 1, 1), down_row
    )


def face_blocks(faces, rows, values):
    blocks = [values[item][0:ROWS] for item in faces]
    sub = subs()
    for i in range(0, len(rows), 4):
        tile = jnp.zeros((8, COLS), F32)
        for j, (kind, k, first) in enumerate(rows[i : i + 4]):
            tile = jnp.where((sub >> 1) == j, turn(values[kind, k][ROWS:TALL], 2 * j - first, 0), tile)
        blocks.append(tile)
    whole = jnp.concatenate(blocks, axis=0)
    fill = FACE_ROWS - whole.shape[0]
    return jnp.concatenate([whole, jnp.zeros((fill, COLS), F32)], axis=0) if fill else whole


def face_in(ref, faces, rows, keep):
    got = {}
    for i, item in enumerate(faces):
        got[item] = [ref[ROWS * i : ROWS * i + ROWS] * keep, jnp.zeros((8, COLS), F32)]
    sub = subs()
    for i, (kind, k, first) in enumerate(rows):
        at = ROWS * len(faces) + 8 * (i // 4)
        tile = turn(ref[at : at + 8], first - 2 * (i % 4), 0) * keep
        mask = (sub == first) | (sub == (first + 1) % 8)
        got[kind, k][1] = jnp.where(mask, tile, got[kind, k][1])
    return {item: jnp.concatenate(parts, axis=0) for item, parts in got.items()}


def second_kernel(yb, ya, right_in, left_in, tiles, strips, xa, xb):
    index = lax.axis_index("gy")
    even = parity("gy")
    has_after = (index < lax.axis_size("gy") - 1).astype(F32)
    has_before = (index > 0).astype(F32)
    sub = subs()
    values = []
    for k in range(COMPS):
        planes = []
        for half in range(2):
            at = 8 * (2 * k + half)
            got_a, got_b = ya[at : at + 8], yb[at : at + 8]
            after = jnp.where(even, got_a, got_b) * has_after
            before = jnp.where(even, got_b, got_a) * has_before
            for j in range(4):
                tile = jnp.where(sub < 2, turn(after, -2 * j, 0), jnp.where(sub >= 6, turn(before, 6 - 2 * j, 0), 0.0))
                tiles[k, 4 * half + j] = tile
                planes.append(tile)
        value = strip(planes, 8)
        strips[k] = value
        values.append(value)
    right, left = face_pack(values, 8)
    even = parity("gx")
    for a in range(2):
        xa[a, 0:ROWS] = jnp.where(even, right_in[a], left_in[a])
        xb[a, 0:ROWS] = jnp.where(even, left_in[a], right_in[a])
        xa[a, ROWS:TALL] = jnp.where(even, right[a], left[a])
        xb[a, ROWS:TALL] = jnp.where(even, left[a], right[a])


def face_kernel(f, tiles, factors, rr, ss, za, zb):
    def field(k, p):
        return jnp.concatenate([f[k, p + 2, 0:ROWS], tiles[k, p]], axis=0)

    zero = jnp.zeros((TALL, COLS), F32)
    drive = jnp.concatenate([factors[0]] * (TALL // 8), axis=0) * field(13, 7)

    def next_x(value, _):
        return pltpu.roll(value, COLS - 1, 1)

    def prev_x(value, _):
        return pltpu.roll(value, 1, 1)

    def half_step(base, p):
        up = [field(base + c, p + 1) for c in range(2)] if p < 7 else [zero, zero]
        return magnetic(
            *[field(base + c, p) for c in range(3)], *up, *[field(base + 3 + c, p) for c in range(3)],
            rr[p + 2], next_x, up_row,
        )

    sent = []
    for p, faces, rows in ((7, UP_FACES, UP_ROWS), (0, DOWN_FACES, DOWN_ROWS)):
        values = {("f", k): field(k, p) for k in (0, 1, 6, 7, 12)}
        q, g = electric_coefficients(rr[p + 2], ss[p + 2], values["f", 12])
        for base in (0, 6):
            h = half_step(base, p)
            down = half_step(base, 6)[0:2] if p == 7 else [zero, zero]
            e = electric(
                *h, *down, *[field(base + c, p) for c in range(3)], q, g, drive if p == 7 and base == 0 else None, prev_x, down_row
            )
            for c in range(3):
                values["h", base + 3 + c] = h[c]
                values["e", base + c] = e[c]
        sent.append(face_blocks(faces, rows, values))
    even = parity("gz")
    za[...] = jnp.where(even, sent[0], sent[1])
    zb[...] = jnp.where(even, sent[1], sent[0])


def third_kernel(xb, xa, strips, strips_rim, factors, xr, xs, sides, rim_a, rim_b):
    index = lax.axis_index("gx")
    even = parity("gx")
    has_after = (index < lax.axis_size("gx") - 1).astype(F32)
    has_before = (index > 0).astype(F32)
    lane = lanes(TALL)
    pair_of = (lane & 7) >> 1
    own = (lane >= 16) & (lane < 80)
    after = [jnp.where(even, xa[a], xb[a]) * has_after for a in range(2)]
    before = [jnp.where(even, xb[a], xa[a]) * has_before for a in range(2)]
    side = []
    for k in range(COMPS):
        array, half, pair = slot(k)
        mine = jnp.concatenate([strips[k], strips_rim[k]], axis=0)
        value = jnp.where(pair_of == 0, mine, turn(mine, 4, 1))
        value = jnp.where(pair_of == 1, turn(after[array], 2 - 2 * pair - 64 * half, 1), value)
        value = jnp.where(pair_of == 2, turn(before[array], 4 - 2 * pair - 64 * half, 1), value)
        value = jnp.where(own, value, 0.0)
        sides[k] = value
        side.append(value)
    r = xr[...]
    q, g = electric_coefficients(r, xs[...], side[12])
    drive = jnp.concatenate([factors[0]] * (TALL // 8), axis=0) * side[13]
    values = {("f", k): side[k] for k in range(COMPS)}
    for base in (0, 6):
        e = side[base : base + 3]
        h = [jnp.where(own, v, 0.0) for v in side_magnetic(e, side[base + 3 : base + 6], r)]
        e = side_electric(h, e, q, g, drive if base == 0 else None)
        for c in range(3):
            values["h", base + 3 + c] = h[c]
            values["e", base + c] = e[c]
    sent = []
    for items, p in ((UP_SIDES, 7), (DOWN_SIDES, 0)):
        packed = jnp.zeros((TALL, COLS), F32)
        for i, item in enumerate(items):
            packed = jnp.where((lane >> 3) == i, turn(values[item], 8 * i - 8 * (p + 2), 1), packed)
        sent.append(packed)
    even = parity("gz")
    rim_a[...] = jnp.where(even, sent[0], sent[1])
    rim_b[...] = jnp.where(even, sent[1], sent[0])


def home(layer):
    mine = lax.axis_index("gz") >> 1
    return (((layer >> 2) ^ mine) << 2) + (layer & 3)


def run_steps(side_loss, factors, f, one, rr, qq, gg, xf, xone, planes, put_field, put_density, halo=None):
    xr = side_loss[0][...]
    xq, xg = electric_coefficients(xr, side_loss[1][...], xf[12])
    factors = [jnp.concatenate([factors[k]] * (TALL // 8), axis=0) for k in range(2)]
    lane = lanes(TALL)
    first_lane, last_lane = lane == 0, lane == COLS - 1

    def side_half(e_ref, e_base, h_base):
        new = side_magnetic([e_ref[e_base + c] for c in range(3)], [xf[h_base + c] for c in range(3)], xr)
        for c in range(3):
            xf[h_base + c] = new[c]

    def side_full(e_base, h_base, out_base, factor):
        drive = None if factor is None else xf[13] * factor
        new = side_electric(
            [xf[h_base + c] for c in range(3)], [xf[e_base + c] for c in range(3)], xq, xg, drive
        )
        for c in range(3):
            xone[out_base + c] = new[c]

    def plane_magnetic(idx, e_ref, x_ref, e_base, h_base):
        def next_x(value, c):
            halo = pltpu.roll(x_ref[e_base + c], 125 - 8 * idx, 1)
            return jnp.where(last_lane, halo, pltpu.roll(value, COLS - 1, 1))

        new = magnetic(
            *[e_ref[e_base + c, idx] for c in range(3)], e_ref[e_base, idx + 1], e_ref[e_base + 1, idx + 1],
            *[f[h_base + c, idx] for c in range(3)], rr[idx], next_x, up_row,
        )
        for c in range(3):
            f[h_base + c, idx] = new[c]

    def plane_electric(idx, e_ref, e_base, h_base, factor):
        def prev_x(value, c):
            halo = pltpu.roll(xf[h_base + c], 123 - 8 * idx, 1)
            return jnp.where(first_lane, halo, pltpu.roll(value, 1, 1))

        drive = None if factor is None else f[13, idx] * factor
        return electric(
            *[f[h_base + c, idx] for c in range(3)], f[h_base, idx - 1], f[h_base + 1, idx - 1],
            *[e_ref[e_base + c, idx] for c in range(3)], qq[idx], gg[idx], drive, prev_x, down_row,
        )

    def over(which, body):
        for idx in planes[which]:
            body(idx)

    def body(idx):
        plane_magnetic(idx, f, xf, 0, 3)
        plane_magnetic(idx, f, xf, 6, 9)

    over(0, body)
    side_half(xf, 0, 3)
    side_half(xf, 6, 9)
    if halo is not None:
        halo(xr, xq, sides=False)

    def body(idx):
        for base, out, factor in ((0, 0, factors[0]), (6, 3, None)):
            new = plane_electric(idx, f, base, base + 3, factor)
            for c in range(3):
                one[out + c, idx] = new[c]

    over(1, body)
    side_full(0, 3, 0, factors[0])
    side_full(6, 9, 3, None)
    if halo is not None:
        halo(xr, xq, sides=True)

    def body(idx):
        plane_magnetic(idx, one, xone, 0, 3)
        plane_magnetic(idx, one, xone, 3, 9)

    over(2, body)
    side_half(xone, 0, 3)
    side_half(xone, 3, 9)

    def body(idx):
        two = plane_electric(idx, one, 0, 3, factors[1])
        zero = plane_electric(idx, one, 3, 9, None)
        density = jnp.zeros((ROWS, COLS), F32)
        for c in range(3):
            last = zero[c][0:ROWS]
            put_field(c, idx, last, f[9 + c, idx, 0:ROWS])
            density = density + f[c, idx, 0:ROWS] * last + one[c, idx, 0:ROWS] * one[3 + c, idx, 0:ROWS]
            density = density + two[c][0:ROWS] * f[6 + c, idx, 0:ROWS]
        put_density(idx, density)

    over(3, body)


def inner_kernel(layer, factors, rr, ss, xr, xs, own, tiles, sides, f, one, qq, gg, sums, e_mid, h_mid, homes, xf, xone):
    del own
    for k in range(COMPS):
        for p in range(PLANES):
            f[k, p + 2, ROWS:TALL] = tiles[k, p]
        xf[k] = sides[k]

    def coefficients(i, carry):
        qq[i + 2], gg[i + 2] = electric_coefficients(rr[i + 2], ss[i + 2], f[12, i + 2])
        return carry

    lax.fori_loop(0, PLANES, coefficients, 0)
    sums[...] = jnp.zeros((LAYERS, ROWS, COLS), F32)
    for i, p in enumerate((0, 1, 6, 7)):
        homes[i] = jnp.full((8, COLS), home(layer[p]), jnp.int32).astype(F32)

    def put(c, idx, e_new, h_new):
        e_mid[c, idx - 4] = e_new
        h_mid[c, idx - 4] = h_new

    def put_density(idx, density):
        sums[home(layer[idx - 2])] = density

    planes = [range(2, 9), range(3, 9), range(3, 8), range(4, 8)]
    run_steps((xr, xs), factors, f, one, rr, qq, gg, xf, xone, planes, put, put_density)


def halo_kernel(rr, ss, sides, f_in, qq_in, gg_in, zb, za, f, qq, gg, below, above):
    del f_in, qq_in, gg_in
    index = lax.axis_index("gz")
    even = parity("gz")
    lane = lanes(TALL)
    for pick, faces, rows, out, idx, keep in (
        (lambda a, b: jnp.where(even, b, a), UP_FACES, UP_ROWS, below, LOW, (index > 0).astype(F32)),
        (lambda a, b: jnp.where(even, a, b), DOWN_FACES, DOWN_ROWS, above, TOP, (index < lax.axis_size("gz") - 1).astype(F32)),
    ):
        planes = face_in(pick(za[...], zb[...]), faces, rows, keep)
        for i, (kind, k) in enumerate(faces):
            if kind == "f":
                f[k, idx] = planes[kind, k]
            else:
                out[i] = planes[kind, k]
        qq[idx], gg[idx] = electric_coefficients(rr[idx], ss[idx], f[12, idx])
    last = TOP - 1
    for base in (0, 6):

        def next_x(value, c):
            return jnp.where(lane == COLS - 1, turn(sides[base + c], 125 - 8 * last, 1), pltpu.roll(value, COLS - 1, 1))

        new = magnetic(
            *[f[base + c, last] for c in range(3)], f[base, TOP], f[base + 1, TOP],
            *[f[base + 3 + c, last] for c in range(3)], rr[last], next_x, up_row,
        )
        for c in range(3):
            f[base + 3 + c, last] = new[c]


def outer_kernel(
    factors, rr, xr, xs, f_in, one_in, qq, gg, sums, homes, below, above, sides, rim_b, rim_a,
    f, one, e_rest, h_rest, zeroth, first, second, third, xf, xone,
):
    del f_in, one_in
    index = lax.axis_index("gz")
    has_above = (index < lax.axis_size("gz") - 1).astype(F32)
    has_below = (index > 0).astype(F32)
    lane = lanes(TALL)
    low, top = LOW, TOP
    for k in range(COMPS):
        xf[k] = sides[k]
    got = {}
    even = parity("gz")
    for pick, ref, faces, idx, keep in (
        (lambda a, b: jnp.where(even, b, a), below, UP_FACES, low, has_below),
        (lambda a, b: jnp.where(even, a, b), above, DOWN_FACES, top, has_above),
    ):
        packed = pick(rim_a[...], rim_b[...]) * keep
        for i, (kind, k) in enumerate(faces):
            side = turn(packed, 8 * idx - 8 * i, 1)
            if kind == "f":
                xf[k] = jnp.where((lane >> 3) == idx, side, xf[k])
                continue
            plane = jnp.where(lane == COLS - 1, turn(packed, 126 - 8 * i, 1), ref[i])
            if kind == "e":
                plane = jnp.where(lane == 0, turn(packed, -6 - 8 * i, 1), plane)
            got[kind, k, idx] = (plane, side)

    def add_z(q, x, y, prev_x):
        return q * ((y - prev_x(y)) - (x - down_row(x, 0)))

    def halo(xr, xq, sides):
        q, q_top, r_half = qq[low], qq[top], 0.5 * rr[low]
        for base, out in ((0, 0), (6, 3)):
            x_side = 0.5 * xr * pltpu.roll(xf[base + 1], 120, 1)
            y_side = -0.5 * xr * pltpu.roll(xf[base], 120, 1)
            if sides:
                added = got["e", base + 2, low][1] + add_z(xq, x_side, y_side, lambda v: pltpu.roll(v, 1, 1))
                xone[out + 2] = jnp.where((lane >> 3) == low, added, xone[out + 2])
                added = got["e", base, top][1] + xq * pltpu.roll(xf[base + 4], 8, 1)
                xone[out] = jnp.where((lane >> 3) == top, added, xone[out])
                added = got["e", base + 1, top][1] - xq * pltpu.roll(xf[base + 3], 8, 1)
                xone[out + 1] = jnp.where((lane >> 3) == top, added, xone[out + 1])
                continue
            x, y = r_half * f[base + 1, 2], -r_half * f[base, 2]

            def prev_x(value):
                return jnp.where(lane == 0, pltpu.roll(y_side, 123 - 8 * low, 1), pltpu.roll(value, 1, 1))

            for k, term, side_term in ((base + 3, x, x_side), (base + 4, y, y_side)):
                plane, side = got["h", k, low]
                f[k, low] = plane + term
                xf[k] = jnp.where((lane >> 3) == low, side + side_term, xf[k])
            f[base + 5, low] = jnp.zeros((TALL, COLS), F32)
            one[out, low] = got["e", base, low][0] - q * y
            one[out + 1, low] = got["e", base + 1, low][0] + q * x
            one[out + 2, low] = got["e", base + 2, low][0] + add_z(q, x, y, prev_x)
            one[out, top] = got["e", base, top][0] + q_top * f[base + 4, top - 1]
            one[out + 1, top] = got["e", base + 1, top][0] - q_top * f[base + 3, top - 1]

    def put(c, idx, e_new, h_new):
        at = idx - 2 if idx < 4 else idx - 6
        e_rest[c, at] = e_new
        h_rest[c, at] = h_new

    late = []

    def put_density(idx, density):
        late.append(density)

    planes = [(), (2, 9), (1, 2, 8, 9), (2, 3, 8, 9)]
    run_steps((xr, xs), factors, f, one, rr, qq, gg, xf, xone, planes, put, put_density, halo)
    for i, out in enumerate((zeroth, first, second, third)):
        for j in range(4):
            total = sums[4 * i + j]
            for at, density in enumerate(late):
                here = homes[at] == float(4 * i + j)
                total = total + jnp.where(jnp.concatenate([here] * (ROWS // 8), axis=0), density, 0.0)
            out[j] = total


def store_kernel(e_mid, h_mid, e_rest, h_rest, e_out, h_out, sems):
    copies = []
    for mid, rest, out in ((e_mid, e_rest, e_out), (h_mid, h_rest, h_out)):
        for source, at, first, count in ((mid, 0, 2, 4), (rest, 0, 0, 2), (rest, 2, 6, 2)):
            copies.append((source.at[:, at : at + count], out.at[:, first : first + count]))
    copies = [pltpu.make_async_copy(a, b, sems.at[i]) for i, (a, b) in enumerate(copies)]
    for copy in copies:
        copy.start()
    for copy in copies:
        copy.wait()


def fold_kernel(sums, second, first, third, kept, sent):
    upper = lax.rem(lax.axis_index("gz"), 2) == 1
    for i in range(2):
        low, high = (sums[j] + first[j] + second[j] + third[j] for j in (i, i + 2))
        kept[i] = jnp.where(upper, high, low)
        sent[i] = jnp.where(upper, low, high)


def sum_kernel(kept, got, out):
    out[...] = kept[...] + got[...]


def call(kernel, outs, scratch=(), scalars=0, far=0, aliases=None, out_space=pltpu.VMEM, flops=1000000):
    def run(*args):
        near = len(args) - scalars - far
        specs = [pl.BlockSpec(memory_space=pltpu.SMEM)] * scalars
        specs += [pl.BlockSpec(memory_space=pltpu.VMEM)] * near + [pl.BlockSpec(memory_space=pl.ANY)] * far
        size = sum(4 * math.prod(s) for s in outs) + sum(4 * math.prod(a.shape) for a in args)
        return pl.pallas_call(
            kernel,
            out_shape=[jax.ShapeDtypeStruct(s, F32) for s in outs],
            in_specs=specs,
            out_specs=[pl.BlockSpec(memory_space=out_space)] * len(outs),
            scratch_shapes=[pltpu.VMEM(s, F32) if isinstance(s, tuple) else s for s in scratch],
            input_output_aliases=aliases or {},
            compiler_params=pltpu.CompilerParams(vmem_limit_bytes=24 * 2**20),
            cost_estimate=pl.CostEstimate(flops=flops, bytes_accessed=size, transcendentals=0),
        )(*args)

    return run


def swaps(axis, first):
    count = lax.axis_size(axis)
    pairs = [(i, (i + 1) % count) for i in range(first, count, 2)]
    return pairs + [(b, a) for a, b in pairs]


def across(axis, bits):
    return [(i, i ^ bits) for i in range(lax.axis_size(axis))]


def inner_swaps():
    count, width = lax.axis_size("gy"), lax.axis_size("gx")
    pairs = []
    for j in range(width):
        pairs += [(i * width + j, (i + 1) * width + j) for i in range(1, count - 1, 2)]
        if j % 2 == 0:
            pairs += [(i * width + j, i * width + j + 1) for i in (0, count - 1)]
    return pairs + [(b, a) for a, b in pairs]


def side_swaps():
    count, width = lax.axis_size("gy"), lax.axis_size("gx")
    pairs = []
    for i in range(count):
        pairs += [(i * width + j, i * width + j + 1) for j in range(1, width - 1, 2)]
        if i % 2 == 0:
            pairs += [(i * width + j, (i + 1) * width + j) for j in (0, width - 1)]
    return pairs + [(b, a) for a, b in pairs]


def depth_swaps():
    count, width = lax.axis_size("gz"), lax.axis_size("gy")
    pairs = []
    for j in range(width):
        pairs += [(i * width + j, (i + 1) * width + j) for i in range(1, count - 1, 2)]
        if j % 2 == 0:
            pairs += [(i * width + j, i * width + j + 1) for i in (0, count - 1)]
    return pairs + [(b, a) for a, b in pairs]


def local(e_start, h_start, adjoint_e, adjoint_h, permittivity, current, layer_of_cell, pml_cells, start_step):
    raw = (e_start, h_start, adjoint_e, adjoint_h, permittivity, current)
    raw = [pltpu.with_memory_space_constraint(a, pltpu.HBM) for a in raw]
    block, deep, tall = (ROWS, COLS), (DEEP, TALL, COLS), (TALL, COLS)
    f, ya, yb = call(
        first_kernel, [(COMPS,) + deep, (16 * COMPS, COLS), (16 * COMPS, COLS)], [pltpu.SemaphoreType.DMA((COMPS,))], far=6
    )(*raw)
    yb = lax.ppermute(yb, ("gy", "gx"), inner_swaps())
    ya = lax.ppermute(ya, "gy", swaps("gy", 0))
    strips, right, left, *loss = call(
        strip_kernel, [(COMPS,) + block, (2,) + block, (2,) + block, (2, 8, COLS), deep, deep, tall, tall], scalars=2
    )(start_step, pml_cells, f)
    side = (2,) + tall
    tiles, strips_rim, xa, xb = call(second_kernel, [(COMPS, PLANES, 8, COLS), (COMPS, 8, COLS), side, side])(yb, ya, right, left)
    za, zb = call(face_kernel, [(FACE_ROWS, COLS)] * 2)(f, tiles, *loss[:3])
    za = lax.ppermute(za, "gz", swaps("gz", 0))
    zb = lax.ppermute(zb, ("gz", "gy"), depth_swaps())
    xa = lax.ppermute(xa, "gx", swaps("gx", 0))
    xb = lax.ppermute(xb, ("gy", "gx"), side_swaps())
    sides, rim_a, rim_b = call(third_kernel, [(COMPS,) + tall, tall, tall])(
        xb, xa, strips, strips_rim, loss[0], *loss[3:]
    )
    rim_a = lax.ppermute(rim_a, "gz", swaps("gz", 0))
    rim_b = lax.ppermute(rim_b, ("gz", "gy"), depth_swaps())
    state = [(COMPS,) + deep, (6,) + deep, deep, deep]
    mid, out = (3, PLANES // 2) + block, (3, PLANES) + block
    side = [(COMPS,) + tall, (6,) + tall]
    *held, sums, e_mid, h_mid, homes = call(inner_kernel, state + [(LAYERS,) + block, mid, mid, (4, 8, COLS)], side, scalars=1, aliases={6: 0}, flops=10**11)(
        layer_of_cell, *loss, f, tiles, sides
    )
    quarter, pair = (LAYERS // 4,) + block, (2,) + block
    f, one, qq, gg = held
    factors, rr, ss, xr, xs = loss
    f, qq, gg, below, above = call(
        halo_kernel,
        [(COMPS,) + deep, deep, deep, (len(UP_FACES),) + tall, (len(DOWN_FACES),) + tall],
        aliases={3: 0, 4: 1, 5: 2},
    )(rr, ss, sides, f, qq, gg, zb, za)
    *_, e_rest, h_rest, zeroth, first, second, third = call(
        outer_kernel, [(COMPS,) + deep, (6,) + deep, mid, mid] + [quarter] * 4, side, aliases={4: 0, 5: 1}
    )(factors, rr, xr, xs, f, one, qq, gg, sums, homes, below, above, sides, rim_b, rim_a)
    e_out, h_out = call(store_kernel, [out, out], [pltpu.SemaphoreType.DMA((6,))], out_space=pltpu.HBM)(e_mid, h_mid, e_rest, h_rest)
    first, second, third = (lax.ppermute(v, "gz", across("gz", m)) for v, m in ((first, 2), (second, 4), (third, 6)))
    kept, sent = call(fold_kernel, [pair, pair])(zeroth, second, first, third)
    (gradient,) = call(sum_kernel, [pair])(kept, lax.ppermute(sent, "gz", across("gz", 1)))
    return gradient, e_out, h_out


def solution(mesh):
    fields = P(None, "gz", "gy", "gx")
    cells = P("gz", "gy", "gx")
    return jax.shard_map(
        local,
        mesh=mesh,
        in_specs=(fields, fields, fields, fields, cells, cells, P("gz"), P(), P()),
        out_specs=(cells, fields, fields),
        check_vma=False,
    )
```

```python
import functools
import math

import jax
import jax.numpy as jnp
from jax import lax
from jax.experimental import pallas as pl
from jax.experimental.pallas import tpu as pltpu
from jax.sharding import PartitionSpec as P

F32 = jnp.float32
PLANES, ROWS, COLS = 8, 32, 128
DEEP, TALL = PLANES + 4, ROWS + 8
LAYERS = 16
PERIOD = 64
COMPS = 14
LOW, TOP = 1, PLANES + 2
UP_FACES = [("h", k) for k in (3, 4, 9, 10)] + [("e", k) for k in (0, 1, 2, 6, 7, 8)] + [("f", 12)]
DOWN_FACES = [("f", k) for k in (0, 1, 6, 7, 12)] + [("e", k) for k in (0, 1, 6, 7)]
UP_ROWS = [("h", k, 7) for k in (3, 4, 9, 10)] + [("e", 2, 7), ("e", 8, 7), ("f", 12, 7)]
DOWN_ROWS = [("f", k, 7) for k in (0, 1, 6, 7, 12)] + [("e", 1, 7), ("e", 7, 7), ("f", 1, 6), ("f", 7, 6)]
UP_SIDES, DOWN_SIDES = UP_FACES, DOWN_FACES


def face_rows(faces, rows):
    return ROWS * len(faces) + 8 * ((len(rows) + 3) // 4)


FACE_ROWS = max(face_rows(UP_FACES, UP_ROWS), face_rows(DOWN_FACES, DOWN_ROWS))


def lanes(rows=8):
    return lax.broadcasted_iota(jnp.int32, (rows, COLS), 1)


def subs(rows=8):
    return lax.broadcasted_iota(jnp.int32, (rows, COLS), 0)


def turn(value, shift, axis):
    shift = shift % value.shape[axis]
    return value if shift == 0 else pltpu.roll(value, shift, axis)


def slot(k):
    return k // 8, (k % 8) // 4, k % 4


def slot_mask(k, rows):
    _, half, pair = slot(k)
    lane = lanes(rows)
    inside = ((lane - 16 - 64 * half) & 127) < 64
    return inside & (((lane & 7) >> 1) == pair)


def window(p, rows):
    lane = lanes(rows)
    return (lane >= 8 * (p + 2)) & (lane < 8 * (p + 2) + 4)


def parity(axis):
    return lax.rem(lax.axis_index(axis), 2) == 0


def strip(planes, rows):
    out = jnp.zeros((rows, COLS), F32)
    for p, plane in enumerate(planes):
        out = jnp.where(window(p, rows), turn(plane, 8 * (p + 2) + 2, 1), out)
    return out


def face_pack(strips, rows):
    right = [jnp.zeros((rows, COLS), F32) for _ in range(2)]
    left = [jnp.zeros((rows, COLS), F32) for _ in range(2)]
    for k, value in enumerate(strips):
        array, half, pair = slot(k)
        mask = slot_mask(k, rows)
        right[array] = jnp.where(mask, turn(value, 2 * pair + 64 * half, 1), right[array])
        left[array] = jnp.where(mask, turn(value, 2 * pair - 2 + 64 * half, 1), left[array])
    return right, left


def first_kernel(e, h, ae, ah, eps, cur, f, ya, yb, sems):
    copies = []
    for k in range(COMPS):
        source = (e, h, ae, ah)[k // 3].at[k % 3] if k < 12 else (eps, cur)[k - 12]
        copies.append(pltpu.make_async_copy(source, f.at[k, 2 : PLANES + 2, 0:ROWS], sems.at[k]))
    for copy in copies:
        copy.start()
    even = parity("gy")
    sub = subs()
    for k in range(COMPS):
        copies[k].wait()
        for half in range(2):
            up = jnp.zeros((8, COLS), F32)
            down = jnp.zeros((8, COLS), F32)
            for j in range(4):
                idx = 4 * half + j + 2
                mask = (sub >> 1) == j
                up = jnp.where(mask, turn(f[k, idx, 24:32], 2 * j - 6, 0), up)
                down = jnp.where(mask, turn(f[k, idx, 0:8], 2 * j, 0), down)
            at = 8 * (2 * k + half)
            ya[at : at + 8] = jnp.where(even, up, down)
            yb[at : at + 8] = jnp.where(even, down, up)


def strip_kernel(start, pml, f, strips, right_out, left_out, factors, rr, ss, xr, xs):
    of_plane = block_sigma(pml)
    for idx in range(1, PLANES + 3):
        sigma, inside = of_plane(idx - 2)
        rr[idx], ss[idx] = damping(sigma, inside), 0.5 * sigma
    sigma, inside = side_sigma(pml)
    xr[...], xs[...] = damping(sigma, inside), 0.5 * sigma
    for k in range(2):
        phase = jnp.full((8, COLS), lax.rem(start[0] + k + 1, PERIOD), jnp.int32).astype(F32)
        factors[k] = jnp.sin(phase * (2.0 * math.pi / PERIOD))
    values = []
    for k in range(COMPS):
        value = strip([f[k, p + 2, 0:ROWS] for p in range(PLANES)], ROWS)
        strips[k] = value
        values.append(value)
    right, left = face_pack(values, ROWS)
    for a in range(2):
        right_out[a] = right[a]
        left_out[a] = left[a]


def profile(position, extent, thickness):
    distance = jnp.minimum(position, extent - 1 - position)
    depth = jnp.maximum(thickness - distance, 0).astype(F32) / thickness.astype(F32)
    return 0.8 * depth * depth


def magnetic(ex, ey, ez, ex_up, ey_up, hx, hy, hz, r, next_x, next_y, at=(0, 1, 2)):
    cx = (next_y(ez, 2) - ez) - (ey_up - ey)
    cy = (ex_up - ex) - (next_x(ez, 2) - ez)
    cz = (next_x(ey, 1) - ey) - (next_y(ex, 0) - ex)
    return [r * (h + h - 0.5 * c) - h for h, c in ((hx, cx), (hy, cy), (hz, cz))]


def electric(hx, hy, hz, hx_down, hy_down, ex, ey, ez, q, g, drive, prev_x, prev_y):
    cx = (hz - prev_y(hz, 2)) - (hy - hy_down)
    cy = (hx - hx_down) - (hz - prev_x(hz, 2))
    cz = (hy - prev_x(hy, 1)) - (hx - prev_y(hx, 0))
    if drive is not None:
        cz = cz - drive
    return [q * (g * e + c) for e, c in ((ex, cx), (ey, cy), (ez, cz))]


def grid_sizes():
    return PLANES * lax.axis_size("gz"), ROWS * lax.axis_size("gy"), COLS * lax.axis_size("gx")


def row_grid():
    row = subs(TALL)
    at = ROWS * lax.axis_index("gy") + jnp.where(row >= 36, row - TALL, row)
    return at, (at >= 0) & (at < grid_sizes()[1])


def damping(sigma, inside):
    return jnp.where(inside, 1.0 / (1.0 + 0.25 * sigma), 0.0)


def electric_coefficients(r, half_sigma, permittivity):
    twice = 2.0 * jnp.maximum(permittivity, 1.0)
    return jnp.where(r > 0.0, 1.0 / (twice + half_sigma), 0.0), twice - half_sigma


def block_sigma(pml):
    nz, ny, nx = grid_sizes()
    at, row_in = row_grid()
    flat = profile(at, ny, pml[1]) + profile(COLS * lax.axis_index("gx") + lanes(TALL), nx, pml[2])

    def of_plane(p):
        z_at = jnp.full((TALL, COLS), PLANES * lax.axis_index("gz") + p, jnp.int32)
        sigma = profile(z_at[0:8], nz, pml[0])
        sigma = jnp.concatenate([sigma] * (TALL // 8), axis=0) + flat
        return sigma, row_in & (z_at >= 0) & (z_at < nz)

    return of_plane


def side_sigma(pml):
    nz, ny, nx = grid_sizes()
    at, row_in = row_grid()
    lane = lanes(TALL)
    column = lane & 7
    x_at = COLS * lax.axis_index("gx") + jnp.where(column < 4, COLS - 2 + column, column - 6)
    z_at = PLANES * lax.axis_index("gz") + (lane >> 3) - 2
    inside = row_in & (z_at >= 0) & (z_at < nz) & (x_at >= 0) & (x_at < nx)
    return profile(z_at, nz, pml[0]) + profile(at, ny, pml[1]) + profile(x_at, nx, pml[2]), inside


def up_row(value, _):
    return pltpu.roll(value, TALL - 1, 0)


def down_row(value, _):
    return pltpu.roll(value, 1, 0)


def side_magnetic(e, h, r):
    return magnetic(
        *e, pltpu.roll(e[0], 120, 1), pltpu.roll(e[1], 120, 1), *h, r, lambda v, _: pltpu.roll(v, 127, 1), up_row
    )


def side_electric(h, e, q, g, drive):
    return electric(
        *h, pltpu.roll(h[0], 8, 1), pltpu.roll(h[1], 8, 1), *e, q, g, drive, lambda v, _: pltpu.roll(v, 1, 1), down_row
    )


def face_blocks(faces, rows, values):
    blocks = [values[item][0:ROWS] for item in faces]
    sub = subs()
    for i in range(0, len(rows), 4):
        tile = jnp.zeros((8, COLS), F32)
        for j, (kind, k, first) in enumerate(rows[i : i + 4]):
            tile = jnp.where((sub >> 1) == j, turn(values[kind, k][ROWS:TALL], 2 * j - first, 0), tile)
        blocks.append(tile)
    whole = jnp.concatenate(blocks, axis=0)
    fill = FACE_ROWS - whole.shape[0]
    return jnp.concatenate([whole, jnp.zeros((fill, COLS), F32)], axis=0) if fill else whole


def face_in(ref, faces, rows, keep):
    got = {}
    for i, item in enumerate(faces):
        got[item] = [ref[ROWS * i : ROWS * i + ROWS] * keep, jnp.zeros((8, COLS), F32)]
    sub = subs()
    for i, (kind, k, first) in enumerate(rows):
        at = ROWS * len(faces) + 8 * (i // 4)
        tile = turn(ref[at : at + 8], first - 2 * (i % 4), 0) * keep
        mask = (sub == first) | (sub == (first + 1) % 8)
        got[kind, k][1] = jnp.where(mask, tile, got[kind, k][1])
    return {item: jnp.concatenate(parts, axis=0) for item, parts in got.items()}


def second_kernel(yb, ya, right_in, left_in, tiles, strips, xa, xb):
    index = lax.axis_index("gy")
    even = parity("gy")
    has_after = (index < lax.axis_size("gy") - 1).astype(F32)
    has_before = (index > 0).astype(F32)
    sub = subs()
    values = []
    for k in range(COMPS):
        planes = []
        for half in range(2):
            at = 8 * (2 * k + half)
            got_a, got_b = ya[at : at + 8], yb[at : at + 8]
            after = jnp.where(even, got_a, got_b) * has_after
            before = jnp.where(even, got_b, got_a) * has_before
            for j in range(4):
                tile = jnp.where(sub < 2, turn(after, -2 * j, 0), jnp.where(sub >= 6, turn(before, 6 - 2 * j, 0), 0.0))
                tiles[k, 4 * half + j] = tile
                planes.append(tile)
        value = strip(planes, 8)
        strips[k] = value
        values.append(value)
    right, left = face_pack(values, 8)
    even = parity("gx")
    for a in range(2):
        xa[a, 0:ROWS] = jnp.where(even, right_in[a], left_in[a])
        xb[a, 0:ROWS] = jnp.where(even, left_in[a], right_in[a])
        xa[a, ROWS:TALL] = jnp.where(even, right[a], left[a])
        xb[a, ROWS:TALL] = jnp.where(even, left[a], right[a])


def face_kernel(f, tiles, factors, rr, ss, za, zb):
    def field(k, p):
        return jnp.concatenate([f[k, p + 2, 0:ROWS], tiles[k, p]], axis=0)

    zero = jnp.zeros((TALL, COLS), F32)
    drive = jnp.concatenate([factors[0]] * (TALL // 8), axis=0) * field(13, 7)

    def next_x(value, _):
        return pltpu.roll(value, COLS - 1, 1)

    def prev_x(value, _):
        return pltpu.roll(value, 1, 1)

    def half_step(base, p):
        up = [field(base + c, p + 1) for c in range(2)] if p < 7 else [zero, zero]
        return magnetic(
            *[field(base + c, p) for c in range(3)], *up, *[field(base + 3 + c, p) for c in range(3)],
            rr[p + 2], next_x, up_row,
        )

    sent = []
    for p, faces, rows in ((7, UP_FACES, UP_ROWS), (0, DOWN_FACES, DOWN_ROWS)):
        values = {("f", k): field(k, p) for k in (0, 1, 6, 7, 12)}
        q, g = electric_coefficients(rr[p + 2], ss[p + 2], values["f", 12])
        for base in (0, 6):
            h = half_step(base, p)
            down = half_step(base, 6)[0:2] if p == 7 else [zero, zero]
            e = electric(
                *h, *down, *[field(base + c, p) for c in range(3)], q, g, drive if p == 7 and base == 0 else None, prev_x, down_row
            )
            for c in range(3):
                values["h", base + 3 + c] = h[c]
                values["e", base + c] = e[c]
        sent.append(face_blocks(faces, rows, values))
    even = parity("gz")
    za[...] = jnp.where(even, sent[0], sent[1])
    zb[...] = jnp.where(even, sent[1], sent[0])


def third_kernel(xa, xb, strips, strips_rim, factors, xr, xs, sides, rim_a, rim_b):
    index = lax.axis_index("gx")
    even = parity("gx")
    has_after = (index < lax.axis_size("gx") - 1).astype(F32)
    has_before = (index > 0).astype(F32)
    lane = lanes(TALL)
    pair_of = (lane & 7) >> 1
    own = (lane >= 16) & (lane < 80)
    after = [jnp.where(even, xa[a], xb[a]) * has_after for a in range(2)]
    before = [jnp.where(even, xb[a], xa[a]) * has_before for a in range(2)]
    side = []
    for k in range(COMPS):
        array, half, pair = slot(k)
        mine = jnp.concatenate([strips[k], strips_rim[k]], axis=0)
        value = jnp.where(pair_of == 0, mine, turn(mine, 4, 1))
        value = jnp.where(pair_of == 1, turn(after[array], 2 - 2 * pair - 64 * half, 1), value)
        value = jnp.where(pair_of == 2, turn(before[array], 4 - 2 * pair - 64 * half, 1), value)
        value = jnp.where(own, value, 0.0)
        sides[k] = value
        side.append(value)
    r = xr[...]
    q, g = electric_coefficients(r, xs[...], side[12])
    drive = jnp.concatenate([factors[0]] * (TALL // 8), axis=0) * side[13]
    values = {("f", k): side[k] for k in range(COMPS)}
    for base in (0, 6):
        e = side[base : base + 3]
        h = [jnp.where(own, v, 0.0) for v in side_magnetic(e, side[base + 3 : base + 6], r)]
        e = side_electric(h, e, q, g, drive if base == 0 else None)
        for c in range(3):
            values["h", base + 3 + c] = h[c]
            values["e", base + c] = e[c]
    sent = []
    for items, p in ((UP_SIDES, 7), (DOWN_SIDES, 0)):
        packed = jnp.zeros((TALL, COLS), F32)
        for i, item in enumerate(items):
            packed = jnp.where((lane >> 3) == i, turn(values[item], 8 * i - 8 * (p + 2), 1), packed)
        sent.append(packed)
    even = parity("gz")
    rim_a[...] = jnp.where(even, sent[0], sent[1])
    rim_b[...] = jnp.where(even, sent[1], sent[0])


def home(layer):
    mine = lax.axis_index("gz") >> 1
    return (((layer >> 2) ^ mine) << 2) + (layer & 3)


def run_steps(side_loss, factors, f, one, rr, qq, gg, xf, xone, planes, put_field, put_density, halo=None):
    xr = side_loss[0][...]
    xq, xg = electric_coefficients(xr, side_loss[1][...], xf[12])
    factors = [jnp.concatenate([factors[k]] * (TALL // 8), axis=0) for k in range(2)]
    lane = lanes(TALL)
    first_lane, last_lane = lane == 0, lane == COLS - 1

    def side_half(e_ref, e_base, h_base):
        new = side_magnetic([e_ref[e_base + c] for c in range(3)], [xf[h_base + c] for c in range(3)], xr)
        for c in range(3):
            xf[h_base + c] = new[c]

    def side_full(e_base, h_base, out_base, factor):
        drive = None if factor is None else xf[13] * factor
        new = side_electric(
            [xf[h_base + c] for c in range(3)], [xf[e_base + c] for c in range(3)], xq, xg, drive
        )
        for c in range(3):
            xone[out_base + c] = new[c]

    def plane_magnetic(idx, e_ref, x_ref, e_base, h_base):
        def next_x(value, c):
            halo = pltpu.roll(x_ref[e_base + c], 125 - 8 * idx, 1)
            return jnp.where(last_lane, halo, pltpu.roll(value, COLS - 1, 1))

        new = magnetic(
            *[e_ref[e_base + c, idx] for c in range(3)], e_ref[e_base, idx + 1], e_ref[e_base + 1, idx + 1],
            *[f[h_base + c, idx] for c in range(3)], rr[idx], next_x, up_row,
        )
        for c in range(3):
            f[h_base + c, idx] = new[c]

    def plane_electric(idx, e_ref, e_base, h_base, factor):
        def prev_x(value, c):
            halo = pltpu.roll(xf[h_base + c], 123 - 8 * idx, 1)
            return jnp.where(first_lane, halo, pltpu.roll(value, 1, 1))

        drive = None if factor is None else f[13, idx] * factor
        return electric(
            *[f[h_base + c, idx] for c in range(3)], f[h_base, idx - 1], f[h_base + 1, idx - 1],
            *[e_ref[e_base + c, idx] for c in range(3)], qq[idx], gg[idx], drive, prev_x, down_row,
        )

    def over(which, body):
        for idx in planes[which]:
            body(idx)

    def body(idx):
        plane_magnetic(idx, f, xf, 0, 3)
        plane_magnetic(idx, f, xf, 6, 9)

    over(0, body)
    side_half(xf, 0, 3)
    side_half(xf, 6, 9)
    if halo is not None:
        halo(xr, xq, sides=False)

    def body(idx):
        for base, out, factor in ((0, 0, factors[0]), (6, 3, None)):
            new = plane_electric(idx, f, base, base + 3, factor)
            for c in range(3):
                one[out + c, idx] = new[c]

    over(1, body)
    side_full(0, 3, 0, factors[0])
    side_full(6, 9, 3, None)
    if halo is not None:
        halo(xr, xq, sides=True)

    def body(idx):
        plane_magnetic(idx, one, xone, 0, 3)
        plane_magnetic(idx, one, xone, 3, 9)

    over(2, body)
    side_half(xone, 0, 3)
    side_half(xone, 3, 9)

    def body(idx):
        two = plane_electric(idx, one, 0, 3, factors[1])
        zero = plane_electric(idx, one, 3, 9, None)
        density = jnp.zeros((ROWS, COLS), F32)
        for c in range(3):
            last = zero[c][0:ROWS]
            put_field(c, idx, last, f[9 + c, idx, 0:ROWS])
            density = density + f[c, idx, 0:ROWS] * last + one[c, idx, 0:ROWS] * one[3 + c, idx, 0:ROWS]
            density = density + two[c][0:ROWS] * f[6 + c, idx, 0:ROWS]
        put_density(idx, density)

    over(3, body)


def inner_kernel(layer, factors, rr, ss, xr, xs, own, tiles, sides, f, one, qq, gg, sums, e_mid, h_mid, homes, xf, xone):
    del own
    for k in range(COMPS):
        for p in range(PLANES):
            f[k, p + 2, ROWS:TALL] = tiles[k, p]
        xf[k] = sides[k]

    def coefficients(i, carry):
        qq[i + 2], gg[i + 2] = electric_coefficients(rr[i + 2], ss[i + 2], f[12, i + 2])
        return carry

    lax.fori_loop(0, PLANES, coefficients, 0)
    sums[...] = jnp.zeros((LAYERS, ROWS, COLS), F32)
    for i, p in enumerate((0, 1, 6, 7)):
        homes[i] = jnp.full((8, COLS), home(layer[p]), jnp.int32).astype(F32)

    def put(c, idx, e_new, h_new):
        e_mid[c, idx - 4] = e_new
        h_mid[c, idx - 4] = h_new

    def put_density(idx, density):
        sums[home(layer[idx - 2])] = density

    planes = [range(2, 9), range(3, 9), range(3, 8), range(4, 8)]
    run_steps((xr, xs), factors, f, one, rr, qq, gg, xf, xone, planes, put, put_density)


def halo_kernel(rr, ss, sides, f_in, qq_in, gg_in, zb, za, f, qq, gg, below, above):
    del f_in, qq_in, gg_in
    index = lax.axis_index("gz")
    even = parity("gz")
    lane = lanes(TALL)
    for pick, faces, rows, out, idx, keep in (
        (lambda a, b: jnp.where(even, b, a), UP_FACES, UP_ROWS, below, LOW, (index > 0).astype(F32)),
        (lambda a, b: jnp.where(even, a, b), DOWN_FACES, DOWN_ROWS, above, TOP, (index < lax.axis_size("gz") - 1).astype(F32)),
    ):
        planes = face_in(pick(za[...], zb[...]), faces, rows, keep)
        for i, (kind, k) in enumerate(faces):
            if kind == "f":
                f[k, idx] = planes[kind, k]
            else:
                out[i] = planes[kind, k]
        qq[idx], gg[idx] = electric_coefficients(rr[idx], ss[idx], f[12, idx])
    last = TOP - 1
    for base in (0, 6):

        def next_x(value, c):
            return jnp.where(lane == COLS - 1, turn(sides[base + c], 125 - 8 * last, 1), pltpu.roll(value, COLS - 1, 1))

        new = magnetic(
            *[f[base + c, last] for c in range(3)], f[base, TOP], f[base + 1, TOP],
            *[f[base + 3 + c, last] for c in range(3)], rr[last], next_x, up_row,
        )
        for c in range(3):
            f[base + 3 + c, last] = new[c]


def outer_kernel(
    factors, rr, xr, xs, f_in, one_in, qq, gg, sums, homes, below, above, sides, rim_b, rim_a,
    f, one, e_rest, h_rest, zeroth, first, second, third, xf, xone,
):
    del f_in, one_in
    index = lax.axis_index("gz")
    has_above = (index < lax.axis_size("gz") - 1).astype(F32)
    has_below = (index > 0).astype(F32)
    lane = lanes(TALL)
    low, top = LOW, TOP
    for k in range(COMPS):
        xf[k] = sides[k]
    got = {}
    even = parity("gz")
    for pick, ref, faces, idx, keep in (
        (lambda a, b: jnp.where(even, b, a), below, UP_FACES, low, has_below),
        (lambda a, b: jnp.where(even, a, b), above, DOWN_FACES, top, has_above),
    ):
        packed = pick(rim_a[...], rim_b[...]) * keep
        for i, (kind, k) in enumerate(faces):
            side = turn(packed, 8 * idx - 8 * i, 1)
            if kind == "f":
                xf[k] = jnp.where((lane >> 3) == idx, side, xf[k])
                continue
            plane = jnp.where(lane == COLS - 1, turn(packed, 126 - 8 * i, 1), ref[i])
            if kind == "e":
                plane = jnp.where(lane == 0, turn(packed, -6 - 8 * i, 1), plane)
            got[kind, k, idx] = (plane, side)

    def add_z(q, x, y, prev_x):
        return q * ((y - prev_x(y)) - (x - down_row(x, 0)))

    def halo(xr, xq, sides):
        q, q_top, r_half = qq[low], qq[top], 0.5 * rr[low]
        for base, out in ((0, 0), (6, 3)):
            x_side = 0.5 * xr * pltpu.roll(xf[base + 1], 120, 1)
            y_side = -0.5 * xr * pltpu.roll(xf[base], 120, 1)
            if sides:
                added = got["e", base + 2, low][1] + add_z(xq, x_side, y_side, lambda v: pltpu.roll(v, 1, 1))
                xone[out + 2] = jnp.where((lane >> 3) == low, added, xone[out + 2])
                added = got["e", base, top][1] + xq * pltpu.roll(xf[base + 4], 8, 1)
                xone[out] = jnp.where((lane >> 3) == top, added, xone[out])
                added = got["e", base + 1, top][1] - xq * pltpu.roll(xf[base + 3], 8, 1)
                xone[out + 1] = jnp.where((lane >> 3) == top, added, xone[out + 1])
                continue
            x, y = r_half * f[base + 1, 2], -r_half * f[base, 2]

            def prev_x(value):
                return jnp.where(lane == 0, pltpu.roll(y_side, 123 - 8 * low, 1), pltpu.roll(value, 1, 1))

            for k, term, side_term in ((base + 3, x, x_side), (base + 4, y, y_side)):
                plane, side = got["h", k, low]
                f[k, low] = plane + term
                xf[k] = jnp.where((lane >> 3) == low, side + side_term, xf[k])
            f[base + 5, low] = jnp.zeros((TALL, COLS), F32)
            one[out, low] = got["e", base, low][0] - q * y
            one[out + 1, low] = got["e", base + 1, low][0] + q * x
            one[out + 2, low] = got["e", base + 2, low][0] + add_z(q, x, y, prev_x)
            one[out, top] = got["e", base, top][0] + q_top * f[base + 4, top - 1]
            one[out + 1, top] = got["e", base + 1, top][0] - q_top * f[base + 3, top - 1]

    def put(c, idx, e_new, h_new):
        at = idx - 2 if idx < 4 else idx - 6
        e_rest[c, at] = e_new
        h_rest[c, at] = h_new

    late = []

    def put_density(idx, density):
        late.append(density)

    planes = [(), (2, 9), (1, 2, 8, 9), (2, 3, 8, 9)]
    run_steps((xr, xs), factors, f, one, rr, qq, gg, xf, xone, planes, put, put_density, halo)
    for i, out in enumerate((zeroth, first, second, third)):
        for j in range(4):
            total = sums[4 * i + j]
            for at, density in enumerate(late):
                here = homes[at] == float(4 * i + j)
                total = total + jnp.where(jnp.concatenate([here] * (ROWS // 8), axis=0), density, 0.0)
            out[j] = total


def store_kernel(e_mid, h_mid, e_rest, h_rest, e_out, h_out, sems):
    copies = []
    for mid, rest, out in ((e_mid, e_rest, e_out), (h_mid, h_rest, h_out)):
        for source, at, first, count in ((mid, 0, 2, 4), (rest, 0, 0, 2), (rest, 2, 6, 2)):
            copies.append((source.at[:, at : at + count], out.at[:, first : first + count]))
    copies = [pltpu.make_async_copy(a, b, sems.at[i]) for i, (a, b) in enumerate(copies)]
    for copy in copies:
        copy.start()
    for copy in copies:
        copy.wait()


def fold_kernel(sums, second, first, third, kept, sent):
    upper = lax.rem(lax.axis_index("gz"), 2) == 1
    for i in range(2):
        low, high = (sums[j] + first[j] + second[j] + third[j] for j in (i, i + 2))
        kept[i] = jnp.where(upper, high, low)
        sent[i] = jnp.where(upper, low, high)


def sum_kernel(kept, got, out):
    out[...] = kept[...] + got[...]


def call(kernel, outs, scratch=(), scalars=0, far=0, aliases=None, out_space=pltpu.VMEM, flops=1000000):
    def run(*args):
        near = len(args) - scalars - far
        specs = [pl.BlockSpec(memory_space=pltpu.SMEM)] * scalars
        specs += [pl.BlockSpec(memory_space=pltpu.VMEM)] * near + [pl.BlockSpec(memory_space=pl.ANY)] * far
        size = sum(4 * math.prod(s) for s in outs) + sum(4 * math.prod(a.shape) for a in args)
        return pl.pallas_call(
            kernel,
            out_shape=[jax.ShapeDtypeStruct(s, F32) for s in outs],
            in_specs=specs,
            out_specs=[pl.BlockSpec(memory_space=out_space)] * len(outs),
            scratch_shapes=[pltpu.VMEM(s, F32) if isinstance(s, tuple) else s for s in scratch],
            input_output_aliases=aliases or {},
            compiler_params=pltpu.CompilerParams(vmem_limit_bytes=24 * 2**20),
            cost_estimate=pl.CostEstimate(flops=flops, bytes_accessed=size, transcendentals=0),
        )(*args)

    return run


def swaps(axis, first):
    count = lax.axis_size(axis)
    pairs = [(i, (i + 1) % count) for i in range(first, count, 2)]
    return pairs + [(b, a) for a, b in pairs]


def across(axis, bits):
    return [(i, i ^ bits) for i in range(lax.axis_size(axis))]


def inner_swaps():
    count, width = lax.axis_size("gy"), lax.axis_size("gx")
    pairs = []
    for j in range(width):
        pairs += [(i * width + j, (i + 1) * width + j) for i in range(1, count - 1, 2)]
        if j % 2 == 0:
            pairs += [(i * width + j, i * width + j + 1) for i in (0, count - 1)]
    return pairs + [(b, a) for a, b in pairs]


def side_swaps():
    count, width = lax.axis_size("gy"), lax.axis_size("gx")
    pairs = []
    for i in range(count):
        pairs += [(i * width + j, i * width + j + 1) for j in range(1, width - 1, 2)]
        if i % 2 == 0:
            pairs += [(i * width + j, (i + 1) * width + j) for j in (0, width - 1)]
    return pairs + [(b, a) for a, b in pairs]


def depth_swaps():
    count, width = lax.axis_size("gz"), lax.axis_size("gy")
    pairs = []
    for j in range(width):
        pairs += [(i * width + j, (i + 1) * width + j) for i in range(1, count - 1, 2)]
        if j % 2 == 0:
            pairs += [(i * width + j, i * width + j + 1) for i in (0, count - 1)]
    return pairs + [(b, a) for a, b in pairs]


def local(e_start, h_start, adjoint_e, adjoint_h, permittivity, current, layer_of_cell, pml_cells, start_step):
    raw = (e_start, h_start, adjoint_e, adjoint_h, permittivity, current)
    raw = [pltpu.with_memory_space_constraint(a, pltpu.HBM) for a in raw]
    block, deep, tall = (ROWS, COLS), (DEEP, TALL, COLS), (TALL, COLS)
    f, ya, yb = call(
        first_kernel, [(COMPS,) + deep, (16 * COMPS, COLS), (16 * COMPS, COLS)], [pltpu.SemaphoreType.DMA((COMPS,))], far=6
    )(*raw)
    yb = lax.ppermute(yb, ("gy", "gx"), inner_swaps())
    ya = lax.ppermute(ya, "gy", swaps("gy", 0))
    strips, right, left, *loss = call(
        strip_kernel, [(COMPS,) + block, (2,) + block, (2,) + block, (2, 8, COLS), deep, deep, tall, tall], scalars=2
    )(start_step, pml_cells, f)
    side = (2,) + tall
    tiles, strips_rim, xa, xb = call(second_kernel, [(COMPS, PLANES, 8, COLS), (COMPS, 8, COLS), side, side])(yb, ya, right, left)
    za, zb = call(face_kernel, [(FACE_ROWS, COLS)] * 2)(f, tiles, *loss[:3])
    za = lax.ppermute(za, "gz", swaps("gz", 0))
    zb = lax.ppermute(zb, ("gz", "gy"), depth_swaps())
    xa = lax.ppermute(xa, "gx", swaps("gx", 0))
    xb = lax.ppermute(xb, ("gy", "gx"), side_swaps())
    sides, rim_a, rim_b = call(third_kernel, [(COMPS,) + tall, tall, tall])(
        xa, xb, strips, strips_rim, loss[0], *loss[3:]
    )
    rim_a = lax.ppermute(rim_a, "gz", swaps("gz", 0))
    rim_b = lax.ppermute(rim_b, ("gz", "gy"), depth_swaps())
    state = [(COMPS,) + deep, (6,) + deep, deep, deep]
    mid, out = (3, PLANES // 2) + block, (3, PLANES) + block
    side = [(COMPS,) + tall, (6,) + tall]
    *held, sums, e_mid, h_mid, homes = call(inner_kernel, state + [(LAYERS,) + block, mid, mid, (4, 8, COLS)], side, scalars=1, aliases={6: 0}, flops=10**11)(
        layer_of_cell, *loss, f, tiles, sides
    )
    quarter, pair = (LAYERS // 4,) + block, (2,) + block
    f, one, qq, gg = held
    factors, rr, ss, xr, xs = loss
    f, qq, gg, below, above = call(
        halo_kernel,
        [(COMPS,) + deep, deep, deep, (len(UP_FACES),) + tall, (len(DOWN_FACES),) + tall],
        aliases={3: 0, 4: 1, 5: 2},
    )(rr, ss, sides, f, qq, gg, zb, za)
    *_, e_rest, h_rest, zeroth, first, second, third = call(
        outer_kernel, [(COMPS,) + deep, (6,) + deep, mid, mid] + [quarter] * 4, side, aliases={4: 0, 5: 1}
    )(factors, rr, xr, xs, f, one, qq, gg, sums, homes, below, above, sides, rim_b, rim_a)
    e_out, h_out = call(store_kernel, [out, out], [pltpu.SemaphoreType.DMA((6,))], out_space=pltpu.HBM)(e_mid, h_mid, e_rest, h_rest)
    first, second, third = (lax.ppermute(v, "gz", across("gz", m)) for v, m in ((first, 2), (second, 4), (third, 6)))
    kept, sent = call(fold_kernel, [pair, pair])(zeroth, second, first, third)
    (gradient,) = call(sum_kernel, [pair])(kept, lax.ppermute(sent, "gz", across("gz", 1)))
    return gradient, e_out, h_out


def solution(mesh):
    fields = P(None, "gz", "gy", "gx")
    cells = P("gz", "gy", "gx")
    return jax.shard_map(
        local,
        mesh=mesh,
        in_specs=(fields, fields, fields, fields, cells, cells, P("gz"), P(), P()),
        out_specs=(cells, fields, fields),
        check_vma=False,
    )
```
